32 devices in a mesh: seq: 4 (over x, core), batch: 8 (over z, y).
Axes of the slice: x: 2, y: 2, z: 4, core: 2. Of those that a mesh axis runs over, the one named last changes fastest.
Arguments:
- tokens: bfloat16 [8, 2496, 512], P('batch', 'seq'), may hold values from -6 to 6
- doc_ids: int32 [8, 2496], P('batch'), may hold values from 0 to 6, as said below
- out_grad: bfloat16 [8, 832, 512], P('batch', 'seq'), may hold values from -6 to 6
- qkv_weight: float32 [3, 512, 512], P(None, ('seq', 'batch')), may hold values from -0.25 to 0.25
- qkv_first: float32 [3, 512, 512], P(None, ('seq', 'batch')), may hold values from -0.00030517578 to 0.00030517578
- qkv_second: float32 [3, 512, 512], P(None, ('seq', 'batch')), may hold values from 1.2699122e-10 to 2.0318596e-09
- proj_weight: float32 [512, 512], P(('seq', 'batch')), may hold values from -0.5 to 0.5
- proj_first: float32 [512, 512], P(('seq', 'batch')), may hold values from -0.00030517578 to 0.00030517578
- proj_second: float32 [512, 512], P(('seq', 'batch')), may hold values from 1.2699122e-10 to 2.0318596e-09
- up_weight: float32 [512, 2048], P(('seq', 'batch')), may hold values from -0.25 to 0.25
- up_first: float32 [512, 2048], P(('seq', 'batch')), may hold values from -0.00030517578 to 0.00030517578
- up_second: float32 [512, 2048], P(('seq', 'batch')), may hold values from 1.2699122e-10 to 2.0318596e-09
- down_weight: float32 [2048, 512], P(('seq', 'batch')), may hold values from -0.125 to 0.125
- down_first: float32 [2048, 512], P(('seq', 'batch')), may hold values from -0.00030517578 to 0.00030517578
- down_second: float32 [2048, 512], P(('seq', 'batch')), may hold values from 1.2699122e-10 to 2.0318596e-09
- pool_weight: float32 [1536, 512], P(('seq', 'batch')), may hold values from -0.15625 to 0.15625
- pool_first: float32 [1536, 512], P(('seq', 'batch')), may hold values from -0.00030517578 to 0.00030517578
- pool_second: float32 [1536, 512], P(('seq', 'batch')), may hold values from 1.2699122e-10 to 2.0318596e-09
- small_weight: float32 [5120], P(('seq', 'batch')), may hold values from -0.8 to 1.8
- small_first: float32 [5120], P(('seq', 'batch')), may hold values from -0.0012207031 to 0.0012207031
- small_second: float32 [5120], P(('seq', 'batch')), may hold values from 2.0318596e-09 to 3.2509753e-08
Outputs:
- short_out: bfloat16 [8, 832, 512], P('batch', 'seq')
- input_grad: float32 [8, 2496, 512], P('batch', 'seq')
- grad_norm: float32 [], replicated
- qkv_first_out: float32 [3, 512, 512], P(None, ('seq', 'batch'))
- qkv_second_out: float32 [3, 512, 512], P(None, ('seq', 'batch'))
- qkv_weight_out: float32 [3, 512, 512], P(None, ('seq', 'batch'))
- proj_first_out: float32 [512, 512], P(('seq', 'batch'))
- proj_second_out: float32 [512, 512], P(('seq', 'batch'))
- proj_weight_out: float32 [512, 512], P(('seq', 'batch'))
- up_first_out: float32 [512, 2048], P(('seq', 'batch'))
- up_second_out: float32 [512, 2048], P(('seq', 'batch'))
- up_weight_out: float32 [512, 2048], P(('seq', 'batch'))
- down_first_out: float32 [2048, 512], P(('seq', 'batch'))
- down_second_out: float32 [2048, 512], P(('seq', 'batch'))
- down_weight_out: float32 [2048, 512], P(('seq', 'batch'))
- pool_first_out: float32 [1536, 512], P(('seq', 'batch'))
- pool_second_out: float32 [1536, 512], P(('seq', 'batch'))
- pool_weight_out: float32 [1536, 512], P(('seq', 'batch'))
- small_first_out: float32 [5120], P(('seq', 'batch'))
- small_second_out: float32 [5120], P(('seq', 'batch'))
- small_weight_out: float32 [5120], P(('seq', 'batch'))
The draws below stay inside these ranges and needn't reach their ends.
Inputs may be any that keep to these rules, and one draw needn't show every extreme that they name: `doc_ids`: in each sequence the ids start at 0, never fall, and rise by one at each document start; every sequence holds exactly seven documents, one of which begins within the first 624 positions and ends within the last 624 positions.
All inputs are finite; a program needn't handle non-finite values.
Results may differ from the reference program's by a relative error of at most 0.012.
Values may be sent and summed in bfloat16 or wider, within the bound.
A program may use at most 448 MiB of HBM per device.

```python
import math
import jax
import jax.numpy as jnp
from jax import lax

D = 512
HEAD_DIM = 64
FF = 2048
TOK_DEV = 624
STEP = 10
LEN = 2496
SEQS = 8
NPARAMS = 3937280


def draw_doc_ids(key, part):
    key = jax.random.fold_in(key, 11)
    keys_split = jax.random.split(key, 6)
    opening = jax.random.randint(keys_split[0], (SEQS, 1), 3, TOK_DEV)
    closing = jax.random.randint(keys_split[1], (SEQS, 1), LEN - TOK_DEV, LEN - 3)
    early_one = jax.random.randint(keys_split[2], (SEQS, 1), 1, opening - 1)
    early_two = jax.random.randint(keys_split[3], (SEQS, 1), early_one + 1, opening)
    late_one = jax.random.randint(keys_split[4], (SEQS, 1), closing + 2, LEN - 1)
    late_two = jax.random.randint(keys_split[5], (SEQS, 1), late_one + 1, LEN)
    places = jnp.arange(LEN, dtype=jnp.int32)[None, :]
    starts = (places == 0) | (places == early_one) | (places == early_two) | (places == opening) | (places == closing + 1) | (places == late_one) | (places == late_two)
    return (jnp.cumsum(starts.astype(jnp.int32), axis=1) - 1).astype(jnp.int32)


def draw_small_weight(key, part):
    key = jax.random.fold_in(key, 23)
    pieces = jax.random.split(key, 2)
    ramp_up = jnp.arange(D, dtype=jnp.float32) / (D - 1)
    rising = 0.6 + 0.8 * ramp_up
    jitter = jax.random.uniform(pieces[0], (2, D), jnp.float32, 0.8, 1.2)
    biases = 0.2 * jnp.clip(jax.random.normal(pieces[1], (4 * D + FF,), jnp.float32), -4.0, 4.0)
    gain_rows = rising[None, :] * jitter
    return jnp.concatenate([gain_rows[0], biases[:D], gain_rows[1], biases[D:2 * D], biases[2 * D:]])


def shard_levels(own_key, extent, shards, smallest, high):
    gain, own = 1.0, jax.random.fold_in(own_key, 6)
    for position, shards_of in shards:
        heights = jnp.exp(jax.random.uniform(jax.random.fold_in(own, position), (shards_of,), jnp.float32, smallest / len(shards), high / len(shards)))
        gain = gain * jnp.repeat(heights, extent[position] // shards_of).reshape([-1 if axis == position else 1 for axis in range(len(extent))])
    return gain


def noise(own_key, dims, scale, most, cuts=(), held_as=jnp.bfloat16):
    values = jax.random.normal(own_key, dims, jnp.float32) * scale
    if len(cuts) > 0:
        values = shard_levels(own_key, dims, cuts, -0.22, 0.18) * values
    return jnp.clip(values, min=-most, max=most).astype(held_as)


def setup_inputs(seed: int = 0) -> dict:
    key_of = jax.random.split(jax.random.key(seed), 22)
    tokens = noise(key_of[0], (SEQS, LEN, D), 1.0, 6.0, ((0, 8), (1, 4)))
    doc_ids = draw_doc_ids(jax.random.fold_in(key_of[21], 71), 0)
    out_grad = noise(key_of[2], (SEQS, LEN // 3, D), 1.0, 6.0, ((0, 8), (1, 4)))
    qkv_weight = noise(key_of[3], (3, D, D), D ** -0.5, 0.25, ((1, 32),), jnp.float32)
    qkv_first = noise(key_of[4], (3, D, D), (0.11 * NPARAMS ** -0.5), 0.00030517578, ((1, 32),), jnp.float32)
    qkv_second = jnp.clip(jnp.exp(math.log(2.0318595694845953e-09) - 2.7725887 * jax.random.uniform(key_of[5], (3, D, D), jnp.float32) ** shard_levels(key_of[5], (3, D, D), ((1, 32),), -0.2, 0.2)), 1.269912230927872e-10, 2.0318595694845953e-09)
    proj_weight = noise(key_of[6], (D, D), (D // 4) ** -0.5, 0.5, ((0, 32),), jnp.float32)
    proj_first = noise(key_of[7], (D, D), (0.11 * NPARAMS ** -0.5), 0.00030517578, ((0, 32),), jnp.float32)
    proj_second = jnp.clip(jnp.exp(math.log(2.0318595694845953e-09) - 2.7725887 * jax.random.uniform(key_of[8], (D, D), jnp.float32) ** shard_levels(key_of[8], (D, D), ((0, 32),), -0.2, 0.2)), 1.269912230927872e-10, 2.0318595694845953e-09)
    up_weight = noise(key_of[9], (D, FF), D ** -0.5, 0.25, ((0, 32),), jnp.float32)
    up_first = noise(key_of[10], (D, FF), (0.11 * NPARAMS ** -0.5), 0.00030517578, ((0, 32),), jnp.float32)
    up_second = jnp.clip(jnp.exp(math.log(2.0318595694845953e-09) - 2.7725887 * jax.random.uniform(key_of[11], (D, FF), jnp.float32) ** shard_levels(key_of[11], (D, FF), ((0, 32),), -0.2, 0.2)), 1.269912230927872e-10, 2.0318595694845953e-09)
    down_weight = noise(key_of[12], (FF, D), FF ** -0.5, 0.125, ((0, 32),), jnp.float32)
    down_first = noise(key_of[13], (FF, D), (0.11 * NPARAMS ** -0.5), 0.00030517578, ((0, 32),), jnp.float32)
    down_second = jnp.clip(jnp.exp(math.log(2.0318595694845953e-09) - 2.7725887 * jax.random.uniform(key_of[14], (FF, D), jnp.float32) ** shard_levels(key_of[14], (FF, D), ((0, 32),), -0.2, 0.2)), 1.269912230927872e-10, 2.0318595694845953e-09)
    pool_weight = noise(key_of[15], (3 * D, D), (3 * D) ** -0.5, 0.15625, ((0, 32),), jnp.float32)
    pool_first = noise(key_of[16], (3 * D, D), (0.11 * NPARAMS ** -0.5), 0.00030517578, ((0, 32),), jnp.float32)
    pool_second = jnp.clip(jnp.exp(math.log(2.0318595694845953e-09) - 2.7725887 * jax.random.uniform(key_of[17], (3 * D, D), jnp.float32) ** shard_levels(key_of[17], (3 * D, D), ((0, 32),), -0.2, 0.2)), 1.269912230927872e-10, 2.0318595694845953e-09)
    small_weight = draw_small_weight(jax.random.fold_in(key_of[21], 71), 0)
    small_first = noise(key_of[19], (6 * D + FF,), (0.44 * NPARAMS ** -0.5), 0.0012207031, ((0, 32),), jnp.float32)
    small_second = jnp.clip(jnp.exp(math.log(3.2509753111753525e-08) - 2.7725887 * jax.random.uniform(key_of[20], (6 * D + FF,), jnp.float32) ** shard_levels(key_of[20], (6 * D + FF,), ((0, 32),), -0.2, 0.2)), 2.0318595694845953e-09, 3.2509753111753525e-08)
    return {"tokens": tokens, "doc_ids": doc_ids, "out_grad": out_grad, "qkv_weight": qkv_weight, "qkv_first": qkv_first, "qkv_second": qkv_second, "proj_weight": proj_weight, "proj_first": proj_first, "proj_second": proj_second, "up_weight": up_weight, "up_first": up_first, "up_second": up_second, "down_weight": down_weight, "down_first": down_first, "down_second": down_second, "pool_weight": pool_weight, "pool_first": pool_first, "pool_second": pool_second, "small_weight": small_weight, "small_first": small_first, "small_second": small_second}


@jax.custom_vjp
def low(v):
    return lax.optimization_barrier(v.astype(jnp.bfloat16)).astype(jnp.float32)

@jax.custom_vjp
def low_back(v):
    return v

def low_keep(v):
    return (low(v), None)

def low_pass(kept, grad):
    return (grad,)

def back_keep(v):
    return (v, None)

def back_low(kept, grad):
    return (low(grad),)
low.defvjp(low_keep, low_pass)
low_back.defvjp(back_keep, back_low)
beta_one = 0.9
beta_two = 0.999
adam_eps = 1e-08
norm_eps = 1e-05
clip_norm = 1.0
rate_matrix = 0.05
rate_vector = 0.5
decay_weight = 0.1
masked_score = -1e+30
highest = lax.Precision.HIGHEST

def layer_norm(values, scale_gain, shift_vec):
    center = values - lax.optimization_barrier(jnp.mean(values, axis=-1, keepdims=True))
    spread = lax.optimization_barrier(jnp.mean(center * center, axis=-1, keepdims=True))
    return center * lax.rsqrt(spread + norm_eps) * scale_gain + shift_vec

def rotate(values, positions):
    half_dim = HEAD_DIM // 2
    head_view = values.reshape(values.shape[0], values.shape[1] // HEAD_DIM, HEAD_DIM)
    frequency = jnp.exp(-math.log(10000.0) * jnp.arange(half_dim, dtype=jnp.float32) / half_dim)
    angles = positions.astype(jnp.float32)[:, None] * frequency[None, :]
    cosine = jnp.cos(angles)[:, None, :]
    sine_part = jnp.sin(angles)[:, None, :]
    first_half = head_view[..., :half_dim]
    second_half = head_view[..., half_dim:]
    turned = jnp.concatenate([first_half * cosine - second_half * sine_part, second_half * cosine + first_half * sine_part], axis=-1)
    return turned.reshape(values.shape)

def matmul(left_side, right_side):
    return jnp.dot(left_side, right_side, preferred_element_type=jnp.float32, precision=highest)

def sequence_forward(inputs, doc_row, qkv_master, proj_master, up_master, down_master, pool_master, small_master):
    length = inputs.shape[0]
    model_width = inputs.shape[1]
    qkv_used = low(qkv_master)
    proj_used = low(proj_master)
    up_used = low(up_master)
    down_used = low(down_master)
    pool_used = low(pool_master)
    small_used = low(small_master)
    gain_first = small_used[0:D]
    shift_first = small_used[D:2 * D]
    gain_second = small_used[2 * D:3 * D]
    shift_second = small_used[3 * D:4 * D]
    bias_down = small_used[4 * D:5 * D]
    bias_pool = small_used[5 * D:6 * D]
    bias_up = small_used[6 * D:]
    normed = low(layer_norm(inputs, gain_first, shift_first))
    projected = jnp.einsum('td,cde->cte', normed, qkv_used, precision=highest)
    positions = jnp.arange(length, dtype=jnp.int32)
    queries = low(rotate(low_back(projected[0]), positions))
    keys_rot = low(rotate(low_back(projected[1]), positions))
    values_low = low(low_back(projected[2]))
    head_count = model_width // HEAD_DIM
    blocks = length // TOK_DEV
    key_heads = keys_rot.reshape(length, head_count, HEAD_DIM)
    value_heads = values_low.reshape(length, head_count, HEAD_DIM)

    def attend_block(block_items):
        query_block, query_pos, query_doc = block_items
        raw_scores = jnp.einsum('qhd,khd->hqk', query_block, key_heads, precision=highest) * HEAD_DIM ** (-0.5)
        scores = low_back(raw_scores)
        allowed = (positions[None, :] <= query_pos[:, None]) & (doc_row[None, :] == query_doc[:, None])
        scores = jnp.where(allowed[None], scores, masked_score)
        soft_probs = low(jax.nn.softmax(scores, axis=-1))
        return jnp.einsum('hqk,khd->qhd', soft_probs, value_heads, precision=highest)
    attended = lax.map(jax.checkpoint(attend_block), (queries.reshape(blocks, TOK_DEV, head_count, HEAD_DIM), positions.reshape(blocks, TOK_DEV), doc_row.reshape(blocks, TOK_DEV)))
    attended = low(low_back(attended.reshape(length, model_width)))
    h_one = inputs + low_back(matmul(attended, proj_used))
    normed_two = low(layer_norm(h_one, gain_second, shift_second))
    hidden_pre = low_back(matmul(normed_two, up_used) + bias_up)
    activated = low(jax.nn.gelu(hidden_pre))
    h_two = h_one + low_back(matmul(activated, down_used) + bias_down)
    rounded = low(h_two)
    shifted = jnp.concatenate([jnp.zeros((2, model_width), rounded.dtype), rounded[:length - 2]], axis=0)
    grouped = shifted.reshape(length // 3, 3 * model_width)
    return matmul(grouped, pool_used) + bias_pool

def adam_update(gradient, first_moment, second_moment, weight, clip_scale, step_rate, decay_rate):
    clipped = gradient * clip_scale
    first_new = beta_one * first_moment + (1.0 - beta_one) * clipped
    second_new = beta_two * second_moment + (1.0 - beta_two) * clipped * clipped
    first_hat = first_new / (1.0 - beta_one ** STEP)
    second_hat = second_new / (1.0 - beta_two ** STEP)
    weight_new = weight - step_rate * (first_hat / (jnp.sqrt(second_hat) + adam_eps) + decay_rate * weight)
    return (first_new, second_new, weight_new)

def reference(tokens, doc_ids, out_grad, qkv_weight, qkv_first, qkv_second, proj_weight, proj_first, proj_second, up_weight, up_first, up_second, down_weight, down_first, down_second, pool_weight, pool_first, pool_second, small_weight, small_first, small_second):
    masters = (qkv_weight, proj_weight, up_weight, down_weight, pool_weight, small_weight)
    firsts = (qkv_first, proj_first, up_first, down_first, pool_first, small_first)
    seconds = (qkv_second, proj_second, up_second, down_second, pool_second, small_second)

    def per_sequence(running, block_items):
        seq_tokens, doc_row, seq_grad = block_items

        def forward(inputs, *params):
            return sequence_forward(inputs, doc_row, *params)
        result, pull_back = jax.vjp(forward, seq_tokens.astype(jnp.float32), *masters)
        gradients = pull_back(seq_grad.astype(jnp.float32))
        updated = tuple((total_part + grad_part for total_part, grad_part in zip(running, gradients[1:])))
        return (updated, (result.astype(jnp.bfloat16), gradients[0]))
    zero_grads = tuple((jnp.zeros_like(master_part) for master_part in masters))
    totals, outputs = lax.scan(per_sequence, zero_grads, (tokens, doc_ids, out_grad))
    short_out, input_grad = outputs
    grad_norm = jnp.sqrt(sum((jnp.sum(grad_part * grad_part) for grad_part in totals)))
    clip_scale = clip_norm / jnp.maximum(grad_norm, clip_norm)
    new_states = []
    for index_kind in range(6):
        step_rate = rate_vector if index_kind == 5 else rate_matrix
        decay_rate = 0.0 if index_kind == 5 else decay_weight
        new_states.append(adam_update(totals[index_kind], firsts[index_kind], seconds[index_kind], masters[index_kind], clip_scale, step_rate, decay_rate))
    return (short_out, input_grad, grad_norm, new_states[0][0], new_states[0][1], new_states[0][2], new_states[1][0], new_states[1][1], new_states[1][2], new_states[2][0], new_states[2][1], new_states[2][2], new_states[3][0], new_states[3][1], new_states[3][2], new_states[4][0], new_states[4][1], new_states[4][2], new_states[5][0], new_states[5][1], new_states[5][2])
```

```python
import math

import jax
import jax.numpy as jnp
from jax import lax
from jax.experimental import pallas as pl
from jax.experimental.pallas import tpu as pltpu
from jax.sharding import PartitionSpec as P

D = 512
HEAD_DIM = 64
STEP = 10


beta_one = 0.9
beta_two = 0.999
adam_eps = 1e-08
norm_eps = 1e-05
clip_norm = 1.0
rate_matrix = 0.05
rate_vector = 0.5
decay_weight = 0.1
masked_score = -1e30


def from_behind(block, axis, distance):
    devices = range(lax.axis_size(axis))
    route = [(i - distance, i) for i in devices if i - distance in devices]
    return lax.ppermute(block, axis, route)


def layer_norm(values, scale_gain, shift_vec):
    center = values - jnp.mean(values, axis=-1, keepdims=True)
    spread = jnp.mean(center * center, axis=-1, keepdims=True)
    return center * lax.rsqrt(spread + norm_eps) * scale_gain + shift_vec


def rotate(values, positions):
    half_dim = HEAD_DIM // 2
    head_view = values.reshape(values.shape[0], values.shape[1] // HEAD_DIM, HEAD_DIM)
    frequency = jnp.exp(-math.log(10000.0) * jnp.arange(half_dim, dtype=jnp.float32) / half_dim)
    angles = positions.astype(jnp.float32)[:, None] * frequency[None, :]
    cosine = jnp.cos(angles)[:, None, :]
    sine_part = jnp.sin(angles)[:, None, :]
    first_half = head_view[..., :half_dim]
    second_half = head_view[..., half_dim:]
    turned = jnp.concatenate(
        [
            first_half * cosine - second_half * sine_part,
            second_half * cosine + first_half * sine_part,
        ],
        axis=-1,
    )
    return turned.reshape(values.shape)


def outer_sum(left_side, right_side):
    return lax.dot_general(
        left_side, right_side, (((0,), (0,)), ((), ())), preferred_element_type=jnp.float32
    )


def times_transpose(left_side, right_side):
    return lax.dot_general(
        left_side, right_side, (((1,), (1,)), ((), ())), preferred_element_type=jnp.float32
    )


def split_heads(values):
    return values.reshape(values.shape[0], values.shape[1] // HEAD_DIM, HEAD_DIM)


def block_scores(query_heads, key_heads, query_pos, key_pos, query_doc, key_doc):
    raw_scores = jnp.einsum(
        "qhd,khd->hqk", query_heads, key_heads, preferred_element_type=jnp.float32
    ) * HEAD_DIM ** (-0.5)
    allowed = (key_pos[None, :] <= query_pos[:, None]) & (key_doc[None, :] == query_doc[:, None])
    return jnp.where(allowed[None], raw_scores, masked_score)


def adam_update(gradient, first_moment, second_moment, weight, clip_scale, step_rate, decay_rate):
    clipped = gradient * clip_scale
    first_new = beta_one * first_moment + (1.0 - beta_one) * clipped
    second_new = beta_two * second_moment + (1.0 - beta_two) * clipped * clipped
    first_hat = first_new / (1.0 - beta_one**STEP)
    second_hat = second_new / (1.0 - beta_two**STEP)
    weight_new = weight - step_rate * (
        first_hat / (jnp.sqrt(second_hat) + adam_eps) + decay_rate * weight
    )
    return (first_new, second_new, weight_new)


def local(
    tokens,
    doc_ids,
    out_grad,
    qkv_weight,
    qkv_first,
    qkv_second,
    proj_weight,
    proj_first,
    proj_second,
    up_weight,
    up_first,
    up_second,
    down_weight,
    down_first,
    down_second,
    pool_weight,
    pool_first,
    pool_second,
    small_weight,
    small_first,
    small_second,
):
    block_rows = tokens.shape[1]
    model_width = tokens.shape[2]
    seq_count = lax.axis_size("seq")
    my_block = lax.axis_index("seq")
    whole_qkv, whole_proj, whole_up, whole_down, whole_pool, whole_small = (
        lax.all_gather(qkv_weight.astype(jnp.bfloat16), ("seq", "batch"), axis=1, tiled=True),
        lax.all_gather(proj_weight.astype(jnp.bfloat16), ("seq", "batch"), axis=0, tiled=True),
        lax.all_gather(up_weight.astype(jnp.bfloat16), ("seq", "batch"), axis=0, tiled=True),
        lax.all_gather(down_weight.astype(jnp.bfloat16), ("seq", "batch"), axis=0, tiled=True),
        lax.all_gather(pool_weight.astype(jnp.bfloat16), ("seq", "batch"), axis=0, tiled=True),
        lax.all_gather(small_weight.astype(jnp.bfloat16), ("seq", "batch"), axis=0, tiled=True),
    )
    small_used = whole_small.astype(jnp.float32)
    gain_first = small_used[0:D]
    shift_first = small_used[D : 2 * D]
    gain_second = small_used[2 * D : 3 * D]
    shift_second = small_used[3 * D : 4 * D]
    bias_down = small_used[4 * D : 5 * D]
    bias_pool = small_used[5 * D : 6 * D]
    bias_up = small_used[6 * D :]
    inputs = tokens[0].astype(jnp.float32)
    doc_row = doc_ids[0]
    first_row = my_block * block_rows
    positions = first_row + jnp.arange(block_rows, dtype=jnp.int32)
    doc_mine = lax.dynamic_slice_in_dim(doc_row, first_row, block_rows)
    normed, first_pull = jax.vjp(layer_norm, inputs, gain_first, shift_first)
    normed_low = normed.astype(jnp.bfloat16)
    projected = jnp.einsum("td,cde->cte", normed_low, whole_qkv, preferred_element_type=jnp.float32)
    queries_rot, query_pull = jax.vjp(lambda values: rotate(values, positions), projected[0])
    keys_rot, key_pull = jax.vjp(lambda values: rotate(values, positions), projected[1])
    query_low = queries_rot.astype(jnp.bfloat16)
    key_low = keys_rot.astype(jnp.bfloat16)
    value_low = projected[2].astype(jnp.bfloat16)
    keys_all, values_all = (
        lax.all_gather(key_low, "seq", axis=0, tiled=True),
        lax.all_gather(value_low, "seq", axis=0, tiled=True),
    )
    query_heads = split_heads(query_low)
    head_count = query_heads.shape[1]
    zeros_head_rows = jnp.zeros((head_count, block_rows), jnp.float32)
    zeros_heads = jnp.zeros((block_rows, head_count, HEAD_DIM), jnp.float32)

    def scores_of(number):
        start_row = number * block_rows
        key_heads = split_heads(keys_all[start_row : start_row + block_rows])
        value_heads = split_heads(values_all[start_row : start_row + block_rows])
        key_pos = start_row + jnp.arange(block_rows, dtype=jnp.int32)
        key_doc = doc_row[start_row : start_row + block_rows]
        scores = block_scores(query_heads, key_heads, positions, key_pos, doc_mine, key_doc)
        return (scores, key_heads, value_heads)

    running_max = jnp.full((head_count, block_rows), masked_score, jnp.float32)
    running_sum = zeros_head_rows
    for number in range(seq_count):

        def block_stats(number=number):
            scores = scores_of(number)[0]
            block_max = jnp.max(scores, axis=-1)
            return (block_max, jnp.sum(jnp.exp(scores - block_max[..., None]), axis=-1))

        block_max, block_sum = block_stats()
        new_max = jnp.maximum(running_max, block_max)
        running_sum = running_sum * jnp.exp(running_max - new_max) + block_sum * jnp.exp(
            block_max - new_max
        )
        running_max = new_max
    log_total = running_max + jnp.log(running_sum)
    attended = zeros_heads
    for number in range(seq_count):

        def block_output(number=number):
            scores, key_heads, value_heads = scores_of(number)
            soft_probs = jnp.exp(scores - log_total[..., None]).astype(jnp.bfloat16)
            return jnp.einsum(
                "hqk,khd->qhd", soft_probs, value_heads, preferred_element_type=jnp.float32
            )

        attended = attended + block_output()
    attended_low = attended.reshape(block_rows, model_width).astype(jnp.bfloat16)
    h_one = inputs + jnp.dot(attended_low, whole_proj, preferred_element_type=jnp.float32)
    normed_two, second_pull = jax.vjp(layer_norm, h_one, gain_second, shift_second)
    normed_two_low = normed_two.astype(jnp.bfloat16)
    hidden_pre = jnp.dot(normed_two_low, whole_up, preferred_element_type=jnp.float32) + bias_up
    activated, gelu_pull = jax.vjp(jax.nn.gelu, hidden_pre)
    act_low = activated.astype(jnp.bfloat16)
    h_two = h_one + jnp.dot(act_low, whole_down, preferred_element_type=jnp.float32) + bias_down
    h_two_low = h_two.astype(jnp.bfloat16)
    prev_rows = from_behind(h_two_low[block_rows - 2 :], "seq", 1)
    shifted = jnp.concatenate([prev_rows, h_two_low[: block_rows - 2]], axis=0)
    grouped = shifted.reshape(block_rows // 3, 3 * model_width)
    short_rows = (
        jnp.dot(grouped, whole_pool, preferred_element_type=jnp.float32) + bias_pool
    ).astype(jnp.bfloat16)
    out_rows = out_grad[0]
    grad_pool = outer_sum(grouped, out_rows)
    grad_bias_pool = jnp.sum(out_rows.astype(jnp.float32), axis=0)
    spread_rows = times_transpose(out_rows, whole_pool).reshape(block_rows, model_width)
    returned = from_behind(spread_rows[:2], "seq", -1)
    grad_h_two = jnp.concatenate([spread_rows[2:], returned], axis=0)
    grad_branch = grad_h_two.astype(jnp.bfloat16)
    grad_down = outer_sum(act_low, grad_branch)
    grad_bias_down = jnp.sum(grad_branch.astype(jnp.float32), axis=0)
    grad_act = times_transpose(grad_branch, whole_down)
    grad_hidden = gelu_pull(grad_act)[0].astype(jnp.bfloat16)
    grad_up = outer_sum(normed_two_low, grad_hidden)
    grad_bias_up = jnp.sum(grad_hidden.astype(jnp.float32), axis=0)
    grad_normed_two = times_transpose(grad_hidden, whole_up)
    back_h_one, grad_gain_second, grad_shift_second = second_pull(grad_normed_two)
    grad_h_one = grad_h_two + back_h_one
    grad_attn = grad_h_one.astype(jnp.bfloat16)
    grad_proj = outer_sum(attended_low, grad_attn)
    grad_attended = times_transpose(grad_attn, whole_proj).astype(jnp.bfloat16)
    grad_heads = split_heads(grad_attended)
    row_delta = zeros_head_rows
    value_terms = []
    for number in range(seq_count):

        def block_first(number=number):
            scores, key_heads, value_heads = scores_of(number)
            soft_probs = jnp.exp(scores - log_total[..., None])
            grad_probs = jnp.einsum(
                "qhd,khd->hqk", grad_heads, value_heads, preferred_element_type=jnp.float32
            )
            part_delta = jnp.sum(soft_probs * grad_probs, axis=-1)
            value_grad = jnp.einsum(
                "hqk,qhd->khd",
                soft_probs.astype(jnp.bfloat16),
                grad_heads,
                preferred_element_type=jnp.float32,
            )
            return (part_delta, value_grad.reshape(block_rows, model_width))

        part_delta, value_grad = block_first()
        row_delta = row_delta + part_delta
        value_terms.append(value_grad)
    grad_query = zeros_heads
    key_terms = []
    for number in range(seq_count):

        def block_second(number=number):
            scores, key_heads, value_heads = scores_of(number)
            soft_probs = jnp.exp(scores - log_total[..., None])
            grad_probs = jnp.einsum(
                "qhd,khd->hqk", grad_heads, value_heads, preferred_element_type=jnp.float32
            )
            grad_scores = (soft_probs * (grad_probs - row_delta[..., None])).astype(jnp.bfloat16)
            query_part = jnp.einsum(
                "hqk,khd->qhd", grad_scores, key_heads, preferred_element_type=jnp.float32
            )
            key_part = jnp.einsum(
                "hqk,qhd->khd", grad_scores, query_heads, preferred_element_type=jnp.float32
            )
            return (query_part, key_part.reshape(block_rows, model_width))

        query_part, key_part = block_second()
        grad_query = grad_query + query_part
        key_terms.append(key_part)
    head_scale = HEAD_DIM ** (-0.5)
    grad_keys, grad_values = (
        lax.psum_scatter(
            (jnp.concatenate(key_terms, axis=0) * head_scale).astype(jnp.bfloat16),
            "seq",
            scatter_dimension=0,
            tiled=True,
        ).astype(jnp.float32),
        lax.psum_scatter(
            jnp.concatenate(value_terms, axis=0).astype(jnp.bfloat16),
            "seq",
            scatter_dimension=0,
            tiled=True,
        ).astype(jnp.float32),
    )
    grad_q_pre = query_pull(grad_query.reshape(block_rows, model_width) * head_scale)[0].astype(
        jnp.bfloat16
    )
    grad_k_pre = key_pull(grad_keys)[0].astype(jnp.bfloat16)
    grad_v_pre = grad_values.astype(jnp.bfloat16)
    stacked = jnp.stack([grad_q_pre, grad_k_pre, grad_v_pre])
    grad_qkv = jnp.einsum("td,cte->cde", normed_low, stacked, preferred_element_type=jnp.float32)
    grad_normed = jnp.einsum("cte,cde->td", stacked, whole_qkv, preferred_element_type=jnp.float32)
    back_inputs, grad_gain_first, grad_shift_first = first_pull(grad_normed)
    input_grad = (grad_h_one + back_inputs)[None]
    grad_small = jnp.concatenate(
        [
            grad_gain_first,
            grad_shift_first,
            grad_gain_second,
            grad_shift_second,
            grad_bias_down,
            grad_bias_pool,
            grad_bias_up,
        ]
    )
    all_grads = (grad_qkv, grad_proj, grad_up, grad_down, grad_pool, grad_small)
    shards = (
        lax.psum_scatter(all_grads[0], ("seq", "batch"), scatter_dimension=1, tiled=True),
        lax.psum_scatter(all_grads[1], ("seq", "batch"), scatter_dimension=0, tiled=True),
        lax.psum_scatter(all_grads[2], ("seq", "batch"), scatter_dimension=0, tiled=True),
        lax.psum_scatter(all_grads[3], ("seq", "batch"), scatter_dimension=0, tiled=True),
        lax.psum_scatter(all_grads[4], ("seq", "batch"), scatter_dimension=0, tiled=True),
        lax.psum_scatter(all_grads[5], ("seq", "batch"), scatter_dimension=0, tiled=True),
    )
    local_squares = sum((jnp.sum(portion * portion) for portion in shards))
    grad_norm = jnp.sqrt(lax.psum(local_squares, ("seq", "batch")))
    clip_scale = clip_norm / jnp.maximum(grad_norm, clip_norm)
    masters = (qkv_weight, proj_weight, up_weight, down_weight, pool_weight, small_weight)
    firsts = (qkv_first, proj_first, up_first, down_first, pool_first, small_first)
    seconds = (qkv_second, proj_second, up_second, down_second, pool_second, small_second)
    new_states = []
    for index_kind in range(6):
        step_rate = rate_vector if index_kind == 5 else rate_matrix
        decay_rate = 0.0 if index_kind == 5 else decay_weight
        new_states.append(
            adam_update(
                shards[index_kind],
                firsts[index_kind],
                seconds[index_kind],
                masters[index_kind],
                clip_scale,
                step_rate,
                decay_rate,
            )
        )
    return (
        short_rows[None],
        input_grad,
        grad_norm,
        new_states[0][0],
        new_states[0][1],
        new_states[0][2],
        new_states[1][0],
        new_states[1][1],
        new_states[1][2],
        new_states[2][0],
        new_states[2][1],
        new_states[2][2],
        new_states[3][0],
        new_states[3][1],
        new_states[3][2],
        new_states[4][0],
        new_states[4][1],
        new_states[4][2],
        new_states[5][0],
        new_states[5][1],
        new_states[5][2],
    )


MESH = pl.DeviceIdType.MESH
BF = jnp.bfloat16
F32 = jnp.float32
WIDE = 128
LOG2E = math.log2(math.e)
NN = (((1,), (0,)), ((), ()))
NT = (((1,), (1,)), ((), ()))
TN = (((0,), (0,)), ((), ()))
VMEM_LIMIT = 60 * 2**20
ARRAYS = 5
GELU_C = math.sqrt(2.0 / math.pi)


def dot(a, b, dims=NN):
    return lax.dot_general(a, b, dims, preferred_element_type=F32)


def grid_of(mesh):
    seq, batch = mesh.shape["seq"], mesh.shape["batch"]
    ny = 2 if batch % 2 == 0 else 1
    return seq // 2, batch // ny, ny


def fits(mesh):
    seq, batch = mesh.shape["seq"], mesh.shape["batch"]
    return seq == 4 and batch % 2 == 0 and D % (seq * batch * 16) == 0


class Where:
    def __init__(self, nx, nz, ny):
        self.nx, self.nz, self.ny = nx, nz, ny
        seq, batch = lax.axis_index("seq"), lax.axis_index("batch")
        self.seq = seq
        self.batch = batch
        self.x, self.c = lax.div(seq, 2), lax.rem(seq, 2)
        self.z, self.y = lax.div(batch, ny), lax.rem(batch, ny)
        self.xo, self.co, self.yo = 1 - self.x, 1 - self.c, 1 - self.y

    def dev(self, x=None, c=None, z=None, y=None):
        x = self.x if x is None else x
        c = self.c if c is None else c
        z = self.z if z is None else z
        y = self.y if y is None else y
        return (x * 2 + c, z * self.ny + y)

    def z_at(self, step):
        return lax.rem(self.z + step, self.nz)

    def seq_at(self, step):
        return lax.rem(self.seq + step, 2 * self.nx)

    def partner(self, stage):
        return {
            "x": self.dev(x=self.xo),
            "c": self.dev(c=self.co),
            "y": self.dev(y=self.yo),
        }[stage]

    def axis_peers(self):
        peers = [self.partner(s) for s in "xcy"]
        return peers + [self.dev(z=self.z_at(k)) for k in range(1, self.nz)]

    def seq_peers(self):
        return [(self.seq_at(k), self.batch) for k in range(1, 2 * self.nx)]


def greet(peers):
    barrier = pltpu.get_barrier_semaphore()
    for peer in peers:
        pl.semaphore_signal(barrier, inc=1, device_id=peer, device_id_type=MESH)
    return barrier


def remote(src, dst, send, recv, peer):
    return pltpu.make_async_remote_copy(
        src, dst, send, recv, device_id=peer, device_id_type=MESH
    )


class Gather:
    ORDERS = ("zxyc", "zyxc", "zyxc", "zxyc", "zyxc")

    def __init__(self, w, fulls, small, small_in, send, recv):
        self.w, self.fulls, self.send, self.recv = w, fulls, send, recv
        self.small, self.small_in = small, small_in
        self.copies = {}

    def view(self, a, stage):
        order = self.ORDERS[a]
        done = order[: order.index(stage)]
        w = self.w
        pick = [
            slice(None) if name in done else own
            for name, own in (("x", w.x), ("c", w.c), ("z", w.z), ("y", w.y))
        ]
        return self.fulls[a].at[pick[0], pick[1], pick[2], pick[3]]

    def start(self, a, index):
        w = self.w
        stage = self.ORDERS[a][index]
        block = self.view(a, stage)
        made = []
        if stage == "z":
            for k in range(1, w.nz):
                made.append(
                    remote(block, block, self.send.at[a, k - 1], self.recv.at[a, k - 1],
                           w.dev(z=w.z_at(k)))
                )
        else:
            slot = w.nz - 1 + "xyc".index(stage)
            made.append(
                remote(block, block, self.send.at[a, slot], self.recv.at[a, slot],
                       w.partner(stage))
            )
        for copy in made:
            copy.start()
        self.copies[a, index] = made

    def wait(self, a, index):
        for copy in self.copies[a, index]:
            copy.wait_recv()

    def finish(self):
        for made in self.copies.values():
            for copy in made:
                copy.wait_send()


def norm_stats(values):
    center = values - jnp.mean(values, axis=-1, keepdims=True)
    spread = jnp.mean(center * center, axis=-1, keepdims=True)
    scale = lax.rsqrt(spread + norm_eps)
    return center * scale, scale


def norm_back(grad, unit, scale, gain):
    inner = grad * gain
    mean_one = jnp.mean(inner, axis=-1, keepdims=True)
    mean_two = jnp.mean(inner * unit, axis=-1, keepdims=True)
    back = scale * (inner - mean_one - unit * mean_two)
    return back, jnp.sum(grad * unit, axis=0, keepdims=True), jnp.sum(grad, axis=0, keepdims=True)


def swap_halves(values):
    lane = lax.broadcasted_iota(jnp.int32, values.shape, 1)
    return jnp.where(
        lax.rem(lane, HEAD_DIM) < HEAD_DIM // 2,
        pltpu.roll(values, WIDE - HEAD_DIM // 2, 1),
        pltpu.roll(values, HEAD_DIM // 2, 1),
    )


def start_kernel(nx, nz, ny, tokens, qkv_w, proj_w, up_w, down_w, pool_w, small_in, turn,
                 g_qkv, g_proj, g_up, g_down, g_pool, small, qkv_all,
                 chunk, small_got, send, recv, send_small, recv_small, send_x, recv_x):
    w = Where(nx, nz, ny)
    rows = tokens.shape[0]
    peers = w.axis_peers() + [w.dev(x=w.xo, c=w.co)]
    barrier = greet(peers)
    shards = (qkv_w, proj_w, up_w, down_w, pool_w)
    fulls = (g_qkv, g_proj, g_up, g_down, g_pool)
    for shard, full in zip(shards, fulls):
        full[w.x, w.c, w.z, w.y] = shard[...].astype(BF)
    total = 4 * rows
    qkv_all[:, pl.ds(total, qkv_all.shape[1] - total)] = jnp.zeros(
        (3, qkv_all.shape[1] - total, WIDE), BF
    )
    small_got[0] = small_in[...]
    pl.semaphore_wait(barrier, len(peers))
    gather = Gather(w, fulls, small, small_in, send, recv)

    small_copies = []

    def small_start(index, part):
        stage = "zyxc"[index]
        if stage == "z":
            made = [
                remote(small_got.at[0], small_got.at[k], send_small.at[k - 1],
                       recv_small.at[k - 1], w.dev(z=w.z_at(k)))
                for k in range(1, w.nz)
            ]
        else:
            base = w.nz + 2 * (index - 1)
            small_got[base] = part
            made = [
                remote(small_got.at[base], small_got.at[base + 1],
                       send_small.at[w.nz + index - 2], recv_small.at[w.nz + index - 2],
                       w.partner(stage))
            ]
        for copy in made:
            copy.start()
        small_copies.append(made)

    def small_wait(index):
        for copy in small_copies[index]:
            copy.wait_recv()
        if index == 0:
            got = small_got[0].astype(F32)
            for k in range(1, w.nz):
                got = got + small_got[k].astype(F32)
        else:
            base = w.nz + 2 * (index - 1)
            got = small_got[base].astype(F32) + small_got[base + 1].astype(F32)
        return got.astype(BF)

    part = None
    small_start(0, None)
    gather.start(0, 0)
    gather.start(1, 0)
    gather.start(2, 0)
    for index in range(4):
        gather.wait(0, index)
        if index < 3:
            gather.start(0, index + 1)
        part = small_wait(index)
        if index < 3:
            small_start(index + 1, part)
        if index == 0:
            gather.start(3, 0)
            gather.start(4, 0)
        elif index == 1:
            gather.wait(1, 0)
            gather.start(1, 1)
            gather.wait(2, 0)
            gather.start(2, 1)
    small[...] = part.astype(F32)

    unit, _ = norm_stats(tokens[...].astype(F32))
    normed = (unit * small[0:1] + small[1:2]).astype(BF)

    def project(x_of):
        first = pl.multiple_of(x_of * 2 * WIDE, 2 * WIDE)
        for n in range(3):
            weight = g_qkv[:, :, :, :, n, :, pl.ds(first, 2 * WIDE)].reshape(D, 2 * WIDE)
            both = dot(normed, weight)
            for c_of in range(2):
                piece = both[:, c_of * WIDE : (c_of + 1) * WIDE]
                if n < 2:
                    piece = piece * turn[0] + swap_halves(piece) * turn[1]
                    if n == 0:
                        piece = piece * (LOG2E * HEAD_DIM ** -0.5)
                chunk[x_of * 2 + c_of, n] = piece.astype(BF)

    mine = pl.ds(pl.multiple_of(w.seq * rows, 16), rows)
    handed = []

    def hand(seq_to, slot):
        copy = remote(chunk.at[seq_to], qkv_all.at[:, mine], send_x.at[slot], recv_x.at[slot],
                      (seq_to, w.batch))
        copy.start()
        handed.append(copy)

    project(w.xo)
    hand(w.xo * 2 + w.c, 0)
    hand(w.xo * 2 + w.co, 1)
    project(w.x)
    hand(w.x * 2 + w.co, 2)
    qkv_all[:, mine] = chunk[w.seq]

    state = {1: 1, 2: 1, 3: 0, 4: 0}
    for _ in range(4):
        for a in range(1, ARRAYS):
            if state[a] < 4:
                gather.wait(a, state[a])
                state[a] += 1
                if state[a] < 4:
                    gather.start(a, state[a])
    for copy in handed:
        copy.wait()
    for made in small_copies:
        for copy in made:
            copy.wait_send()
    gather.finish()


def build_ext(doc_ref, qkv, ext):
    lane1 = lax.broadcasted_iota(jnp.int32, (1, WIDE), 1)
    feat1 = lax.rem(lane1, HEAD_DIM)
    docs = doc_ref[...]
    lo = jnp.zeros((1, WIDE), jnp.int32)
    hi = jnp.zeros((1, WIDE), jnp.int32)
    for d in range(7):
        below = jnp.sum(jnp.where(docs < d, 1, 0), axis=1, keepdims=True)
        upto = jnp.sum(jnp.where(docs <= d, 1, 0), axis=1, keepdims=True)
        lo = jnp.where(feat1 == d, below, lo)
        hi = jnp.where(feat1 == d, upto, hi)
    padded = qkv.shape[1]
    step = 512

    def body(n, _):
        r0 = pl.multiple_of(n * step, step)
        rows = lax.broadcasted_iota(jnp.int32, (step, WIDE), 0) + r0
        lane = lax.broadcasted_iota(jnp.int32, (step, WIDE), 1)
        feat = lax.rem(lane, HEAD_DIM)
        same = (rows >= lo) & (rows < hi)
        q_feat = jnp.where(same, 1.0, 0.0)
        k_feat = jnp.where(same, 0.0, masked_score)
        ones = jnp.where((feat >= 8) & (feat < 11), 1.0, 0.0)
        k_feat = jnp.where(feat < 7, k_feat, ones)
        parts = [qkv[m, pl.ds(r0, step)].astype(F32) for m in range(3)]
        for h in range(2):
            mine = (lane >= h * HEAD_DIM) & (lane < (h + 1) * HEAD_DIM)
            for m, feats in enumerate((q_feat, k_feat, 1.0)):
                ext[m, h, pl.ds(r0, step)] = jnp.where(mine, parts[m], feats).astype(BF)
        return 0

    lax.fori_loop(0, padded // step, body, 0)


def with_feats(base, lane, h, vector):
    one = vector.astype(BF).astype(F32)
    two = (vector - one).astype(BF).astype(F32)
    first = (1 - h) * HEAD_DIM + 8
    for n, term in enumerate((one, two, vector - one - two)):
        base = jnp.where(lane == first + n, term, base)
    return base


def attend_rows(ext, o_ref, o_low, i, size):
    padded = ext.shape[2]
    r0 = i * size
    n = min(padded, -(-(r0 + size) // 256) * 256)
    m0 = (r0 // 128) * 128
    lane = lax.broadcasted_iota(jnp.int32, (size, WIDE), 1)
    outs = []
    for h in range(2):
        q = ext[0, h, pl.ds(r0, size)]
        s = dot(q, ext[1, h, :n], NT)
        rows = lax.broadcasted_iota(jnp.int32, (size, n - m0), 0) + r0
        cols = lax.broadcasted_iota(jnp.int32, (size, n - m0), 1) + m0
        tail = jnp.where(cols <= rows, s[:, m0:], masked_score)
        s = jnp.concatenate([s[:, :m0], tail], axis=1) if m0 else tail
        top = jnp.max(s, axis=1, keepdims=True)
        p = jnp.exp2(s - top).astype(BF)
        sums = dot(p, ext[2, h, :n])
        outs.append(sums / pltpu.roll(sums, HEAD_DIM, 1))
        log_total = top + jnp.log2(sums)
        ext[0, h, pl.ds(r0, size)] = with_feats(q.astype(F32), lane, h, -log_total).astype(BF)
    both = jnp.where(lane < HEAD_DIM, outs[0], outs[1])
    o_ref[pl.ds(r0, size)] = both
    o_low[pl.ds(r0, size)] = both.astype(BF)


def forward_kernel(doc_ref, qkv_all, ext, o_ref, o_low):
    total = o_ref.shape[0]
    build_ext(doc_ref, qkv_all, ext)
    size = total // 8
    for i in range(8):
        attend_rows(ext, o_ref, o_low, i, size)
    for h in range(2):
        ext[0, h, pl.ds(total, ext.shape[2] - total)] = jnp.zeros(
            (ext.shape[2] - total, WIDE), BF
        )


def backward_prep(o_ref, do_ref, do_ext):
    total = o_ref.shape[0]
    step = total // 12

    def body(n, _):
        r0 = pl.multiple_of(n * step, 16)
        lane = lax.broadcasted_iota(jnp.int32, (step, WIDE), 1)
        grad = do_ref[pl.ds(r0, step)].astype(F32)
        terms = grad * o_ref[pl.ds(r0, step)]
        for h in range(2):
            mine = (lane >= h * HEAD_DIM) & (lane < (h + 1) * HEAD_DIM)
            delta = jnp.sum(jnp.where(mine, terms, 0.0), axis=1, keepdims=True)
            base = jnp.where(mine, grad, 0.0)
            do_ext[h, pl.ds(r0, step)] = with_feats(base, lane, h, -delta).astype(BF)
        return 0

    lax.fori_loop(0, 12, body, 0)
    for h in range(2):
        do_ext[h, pl.ds(total, do_ext.shape[1] - total)] = jnp.zeros(
            (do_ext.shape[1] - total, WIDE), BF
        )


def backward_pair(ext, do_ext, dq, dk, dv, h, i, j, size, on_diagonal):
    ri = pl.multiple_of(i * size, size)
    rj = pl.multiple_of(j * size, size)
    q = ext[0, h, pl.ds(ri, size)]
    k = ext[1, h, pl.ds(rj, size)]
    v = ext[2, h, pl.ds(rj, size)]
    grad = do_ext[h, pl.ds(ri, size)]
    p = jnp.exp2(dot(k, q, NT))
    if on_diagonal:
        keys = lax.broadcasted_iota(jnp.int32, (size, size), 0)
        queries = lax.broadcasted_iota(jnp.int32, (size, size), 1)
        p = jnp.where(keys <= queries, p, 0.0)
    ds = (p * dot(v, grad, NT)).astype(BF)
    p_low = p.astype(BF)
    if on_diagonal:
        dv[h, pl.ds(rj, size)] = dot(p_low, grad)
        dk[h, pl.ds(rj, size)] = dot(ds, q)
    else:
        dv[h, pl.ds(rj, size)] += dot(p_low, grad)
        dk[h, pl.ds(rj, size)] += dot(ds, q)
    dq[h, pl.ds(ri, size)] += dot(ds, k, TN)


def backward_kernel(ext, o_ref, do_ref, out, do_ext, dq, dk, dv):
    total = o_ref.shape[0]
    size = 512
    blocks = ext.shape[2] // size
    backward_prep(o_ref, do_ref, do_ext)
    dq[...] = jnp.zeros(dq.shape, F32)

    def per_head(h, _):
        def per_key(j, _):
            backward_pair(ext, do_ext, dq, dk, dv, h, j, j, size, True)

            def per_query(i, _):
                backward_pair(ext, do_ext, dq, dk, dv, h, i, j, size, False)
                return 0

            lax.fori_loop(j + 1, blocks, per_query, 0)
            return 0

        lax.fori_loop(0, blocks, per_key, 0)
        return 0

    lax.fori_loop(0, 2, per_head, 0)
    step = total // 4
    scales = (HEAD_DIM ** -0.5, 1.0 / LOG2E, 1.0)
    for n in range(4):
        rows = pl.ds(n * step, step)
        lane = lax.broadcasted_iota(jnp.int32, (step, WIDE), 1)
        for m, part in enumerate((dq, dk, dv)):
            both = jnp.where(lane < HEAD_DIM, part[0, rows], part[1, rows])
            out[n, m] = (both * scales[m]).astype(BF)


def middle_kernel(nx, nz, ny, o_low, tokens, out_grad, g_proj, g_up, g_down, g_pool, small,
                  do_all, short_out, att, normed_two, act, d_hidden, d_branch, d_attn, grouped,
                  dh_one, small_grad,
                  dh_two, h_two, h_one, sum_one, sum_two, do_send, next_grad, prev_rows, edge,
                  send, recv, send_do, recv_do, send_edge, recv_edge):
    w = Where(nx, nz, ny)
    rows = tokens.shape[0]
    pools = rows // 3
    count = 2 * w.nx
    peers = w.seq_peers()
    barrier = greet(peers)
    first, last = w.seq == 0, w.seq == count - 1
    g_low = out_grad[...]
    pool = g_pool[...].reshape(3 * D, D)
    edge[0] = g_low[0:16]
    pl.semaphore_wait(barrier, len(peers))
    grad_edge = remote(edge.at[0], next_grad, send_edge.at[0], recv_edge.at[0],
                       (w.seq_at(count - 1), w.batch))
    grad_edge.start()
    copies = []
    for k in range(1, count):
        to = w.seq_at(k)
        copy = remote(o_low.at[pl.ds(pl.multiple_of(to * rows, 16), rows)], att.at[w.seq],
                      send.at[k - 1], recv.at[k - 1], (to, w.batch))
        copy.start()
        copies.append(copy)
    att[w.seq] = o_low[pl.ds(pl.multiple_of(w.seq * rows, 16), rows)]

    spread = dot(g_low, pool, NT)
    tiles = D // WIDE

    def lay(ref, start, value):
        for n in range(tiles):
            ref[n, pl.ds(start, value.shape[0])] = value[:, n * WIDE : (n + 1) * WIDE]

    def whole(ref):
        return jnp.concatenate([ref[n, pl.ds(8, rows)] for n in range(tiles)], axis=1)

    for k in range(3):
        for n in range(tiles):
            at = k * D + n * WIDE
            dh_two[n, pl.ds(6 + k, pools, stride=3)] = spread[:, at : at + WIDE]
    grad_edge.wait()
    beyond = dot(next_grad[...], pool, NT)
    beyond = jnp.where(last, 0.0, beyond)
    lay(dh_two, 8 + rows - 2, beyond[0:1, 0:D])
    lay(dh_two, 8 + rows - 1, beyond[0:1, D : 2 * D])
    d_branch[...] = whole(dh_two).astype(BF)
    small_grad[...] = jnp.zeros(small_grad.shape, F32)
    small_grad[4:5] = jnp.sum(d_branch[...].astype(F32), axis=0, keepdims=True)
    small_grad[5:6] = jnp.sum(g_low.astype(F32), axis=0, keepdims=True)

    for copy in copies:
        copy.wait()
    attended = jnp.concatenate([att[n] for n in range(count)], axis=1)
    h_one[...] = tokens[...].astype(F32) + dot(attended, g_proj[...].reshape(D, D))
    unit, _ = norm_stats(h_one[...])
    normed_two[...] = (unit * small[2:3] + small[3:4]).astype(BF)
    sum_one[...] = jnp.zeros(sum_one.shape, F32)
    sum_two[...] = jnp.zeros(sum_two.shape, F32)
    part = act.shape[1] // count

    def feed(n, _):
        cols = pl.ds(pl.multiple_of(n * part, part), part)
        up = g_up[:, :, :, :, :, cols].reshape(D, part)
        down = g_down[lax.div(n, 2), lax.rem(n, 2)].reshape(part, D)
        hidden = dot(normed_two[...], up) + small[pl.ds(6 + n, 1)]
        square = hidden * hidden
        bend = jnp.tanh(GELU_C * hidden * (1.0 + 0.044715 * square))
        half = 0.5 * (1.0 + bend)
        act_low = (hidden * half).astype(BF)
        act[:, cols] = act_low
        slope = half + 0.5 * hidden * (1.0 - bend * bend) * (
            GELU_C * (1.0 + 3 * 0.044715 * square)
        )
        sum_one[...] += dot(act_low, down)
        d_low = (dot(d_branch[...], down, NT) * slope).astype(BF)
        d_hidden[:, cols] = d_low
        small_grad[pl.ds(6 + n, 1)] = jnp.sum(d_low.astype(F32), axis=0, keepdims=True)
        sum_two[...] += dot(d_low, up, NT)
        return 0

    lax.fori_loop(0, count, feed, 0)
    h_low = (h_one[...] + sum_one[...] + small[4:5]).astype(BF)
    lay(h_two, 8, h_low.astype(F32))
    edge[1] = h_low[rows - 16 :]
    row_edge = remote(edge.at[1], prev_rows, send_edge.at[1], recv_edge.at[1],
                      (w.seq_at(1), w.batch))
    row_edge.start()
    unit, scale = norm_stats(h_one[...])
    back, small_grad[2:3], small_grad[3:4] = norm_back(sum_two[...], unit, scale, small[2:3])
    grad_one = whole(dh_two) + back
    dh_one[...] = grad_one
    d_attn[...] = grad_one.astype(BF)
    spread_back = dot(d_attn[...], g_proj[...].reshape(D, D), NT).astype(BF)
    for n in range(count):
        do_send[n] = spread_back[:, n * WIDE : (n + 1) * WIDE]
    mine = pl.ds(pl.multiple_of(w.seq * rows, 16), rows)
    given = []
    for k in range(1, count):
        to = w.seq_at(k)
        copy = remote(do_send.at[to], do_all.at[mine], send_do.at[k - 1], recv_do.at[k - 1],
                      (to, w.batch))
        copy.start()
        given.append(copy)
    do_all[mine] = do_send[w.seq]

    row_edge.wait()
    before = jnp.where(first, 0.0, prev_rows[...].astype(F32))
    lay(h_two, 0, before[8:16])
    for k in range(3):
        for n in range(tiles):
            at = k * D + n * WIDE
            grouped[:, at : at + WIDE] = h_two[n, pl.ds(6 + k, pools, stride=3)].astype(BF)
    short_out[...] = (dot(grouped[...], pool) + small[5:6]).astype(BF)
    for copy in given:
        copy.wait()


class Scatter:
    ORDERS = ("xy", "yx", "yx", "xy", "yx")

    def __init__(self, w, acc, c_out, c_in, two_out, two_in, three_out, three_in, z_out, z_in,
                 send, recv):
        self.w, self.acc = w, acc
        self.c_out, self.c_in = c_out, c_in
        self.two_out, self.two_in = two_out, two_in
        self.three_out, self.three_in = three_out, three_in
        self.z_out, self.z_in = z_out, z_in
        self.send, self.recv = send, recv
        self.copies = {}

    def go(self, a, index, src, dst, slot, peer):
        copy = remote(src, dst, self.send.at[a, slot], self.recv.at[a, slot], peer)
        copy.start()
        self.copies.setdefault((a, index), []).append(copy)

    def arrived(self, a, index):
        for copy in self.copies[a, index]:
            copy.wait_recv()

    def begin(self, a, make):
        w = self.w
        shape = self.acc[a].shape[1:]
        for x_of in range(w.nx):
            self.c_out[a][x_of] = make(x_of * 2 + w.co).reshape(shape).astype(BF)
        self.go(a, 0, self.c_out[a], self.c_in[a], 0, w.partner("c"))
        for x_of in range(w.nx):
            self.acc[a][x_of] = make(x_of * 2 + w.c).reshape(shape)

    def step_two(self, a):
        w = self.w
        acc, got, out = self.acc[a], self.c_in[a], self.two_out[a]
        self.arrived(a, 0)
        by_x = self.ORDERS[a][0] == "x"

        def body(n, _):
            if by_x:
                out[n] = (acc[w.xo, n] + got[w.xo, n].astype(F32)).astype(BF)
            else:
                for x_of in range(w.nx):
                    out[x_of, n] = (acc[x_of, n, w.yo] + got[x_of, n, w.yo].astype(F32)).astype(BF)
            return 0

        lax.fori_loop(0, w.nz, body, 0)
        self.go(a, 1, out, self.two_in[a], 1, w.partner(self.ORDERS[a][0]))

    def step_three(self, a):
        w = self.w
        acc, got, more, out = self.acc[a], self.c_in[a], self.two_in[a], self.three_out[a]
        self.arrived(a, 1)
        by_x = self.ORDERS[a][0] == "x"

        def body(n, _):
            if by_x:
                out[n] = (acc[w.x, n, w.yo] + got[w.x, n, w.yo].astype(F32)
                          + more[n, w.yo].astype(F32)).astype(BF)
                acc[w.x, n, w.y] = (acc[w.x, n, w.y] + got[w.x, n, w.y].astype(F32)
                                    + more[n, w.y].astype(F32))
            else:
                out[n] = (acc[w.xo, n, w.y] + got[w.xo, n, w.y].astype(F32)
                          + more[w.xo, n].astype(F32)).astype(BF)
                acc[w.x, n, w.y] = (acc[w.x, n, w.y] + got[w.x, n, w.y].astype(F32)
                                    + more[w.x, n].astype(F32))
            return 0

        lax.fori_loop(0, w.nz, body, 0)
        self.go(a, 2, out, self.three_in[a], 2, w.partner(self.ORDERS[a][1]))

    def step_four(self, a):
        w = self.w
        acc, more = self.acc[a], self.three_in[a]
        self.arrived(a, 2)
        for k in range(1, w.nz):
            to = w.z_at(k)
            self.z_out[a][k - 1] = (acc[w.x, to, w.y] + more[to].astype(F32)).astype(BF)
            self.go(a, 3, self.z_out[a].at[k - 1], self.z_in[a].at[k - 1], 2 + k, w.dev(z=to))
        acc[w.x, w.z, w.y] = acc[w.x, w.z, w.y] + more[w.z].astype(F32)

    def last(self, a):
        w = self.w
        self.arrived(a, 3)
        total = self.acc[a][w.x, w.z, w.y]
        for k in range(1, w.nz):
            total = total + self.z_in[a][k - 1].astype(F32)
        return total

    def finish(self):
        for made in self.copies.values():
            for copy in made:
                copy.wait_send()


def end_kernel(nx, nz, ny, *refs):
    (d_qkv, tokens, turn, g_qkv, small, att, normed_two, act, d_hidden, d_branch, d_attn,
     grouped, out_grad, dh_one, small_grad) = refs[:15]
    states = refs[15:30]
    (input_grad, small_total, norm_out) = refs[30:33]
    new_states = refs[33:48]
    scratch = list(refs[48:])
    take = lambda n: tuple(scratch.pop(0) for _ in range(n))
    back_in, stacked, normed = take(3)
    groups = [take(ARRAYS) for _ in range(9)]
    small_got, norm_got = take(2)
    send, recv, send_x, recv_x, send_small, recv_small, send_norm, recv_norm = take(8)

    w = Where(nx, nz, ny)
    rows = tokens.shape[0]
    count = 2 * w.nx
    others = [(w.seq, lax.rem(w.batch + k, w.nz * w.ny)) for k in range(1, w.nz * w.ny)]
    peers = w.seq_peers() + others
    barrier = greet(peers)
    pl.semaphore_wait(barrier, len(peers))

    handed = []
    for k in range(1, count):
        to = w.seq_at(k)
        copy = remote(d_qkv.at[to], back_in.at[w.seq], send_x.at[k - 1], recv_x.at[k - 1],
                      (to, w.batch))
        copy.start()
        handed.append(copy)
    back_in[w.seq] = d_qkv[w.seq]

    scatter = Scatter(w, *groups, send, recv)

    def columns(ref):
        width = ref.shape[1] // count
        return lambda block: ref[:, pl.ds(pl.multiple_of(block * width, WIDE), width)]

    lhs_down, lhs_pool = columns(act), columns(grouped)
    lhs_up, lhs_qkv = columns(normed_two), columns(normed)
    scatter.begin(3, lambda block: dot(lhs_down(block), d_branch[...], TN))
    scatter.begin(2, lambda block: dot(lhs_up(block), d_hidden[...], TN))
    scatter.step_two(3)
    scatter.begin(4, lambda block: dot(lhs_pool(block), out_grad[...], TN))
    scatter.step_two(2)
    scatter.begin(1, lambda block: dot(att[block], d_attn[...], TN))
    scatter.step_two(4)
    scatter.step_two(1)

    for copy in handed:
        copy.wait()
    unit, scale = norm_stats(tokens[...].astype(F32))
    normed[...] = (unit * small[0:1] + small[1:2]).astype(BF)
    for n in range(3):
        for b in range(count):
            piece = back_in[b, n]
            if n < 2:
                piece = piece.astype(F32)
                piece = (piece * turn[0] - swap_halves(piece) * turn[1]).astype(BF)
            stacked[n, :, b * WIDE : (b + 1) * WIDE] = piece

    def grad_qkv(block):
        left = lhs_qkv(block)
        parts = [dot(left, stacked[n], TN).reshape(w.nz, w.ny, 1, -1, D) for n in range(3)]
        return jnp.concatenate(parts, axis=2)

    scatter.begin(0, grad_qkv)
    scatter.step_two(0)
    grad_normed = sum(dot(stacked[n], g_qkv[:, :, :, :, n].reshape(D, D), NT) for n in range(3))
    back, small_grad[0:1], small_grad[1:2] = norm_back(grad_normed, unit, scale, small[0:1])
    input_grad[...] = dh_one[...] + back

    small_copies = []
    small_got[0] = small_grad[...]
    for index, stage in enumerate("cyx"):
        copy = remote(small_got.at[2 * index], small_got.at[2 * index + 1],
                      send_small.at[index], recv_small.at[index], w.partner(stage))
        copy.start()
        small_copies.append(copy)
        if index == 0:
            for a in (3, 2, 4, 1):
                scatter.step_three(a)
        elif index == 1:
            scatter.step_three(0)
            scatter.step_four(3)
            scatter.step_four(2)
        copy.wait_recv()
        small_got[2 * index + 2] = small_got[2 * index] + small_got[2 * index + 1]
    z_first = 7
    for k in range(1, w.nz):
        copy = remote(small_got.at[6], small_got.at[z_first + w.z], send_small.at[2 + k],
                      recv_small.at[2 + k], w.dev(z=w.z_at(k)))
        copy.start()
        small_copies.append(copy)
    small_got[z_first + w.z] = small_got[6]
    for a in (4, 1, 0):
        scatter.step_four(a)
    for copy in small_copies[3:]:
        copy.wait_recv()
    whole = small_got[z_first]
    for k in range(1, w.nz):
        whole = whole + small_got[z_first + k]
    small_total[...] = whole

    totals = {}
    squares = jnp.zeros((8, D), F32)
    for a in range(ARRAYS):
        total = scatter.last(a)
        totals[a] = total
        width = total.shape[-1]
        flat = (total * total).reshape(-1, 8, width)
        flat = jnp.sum(flat, axis=0)
        for n in range(width // D):
            squares = squares + flat[:, n * D : (n + 1) * D]
        scatter.acc[a][w.x, w.z, w.y] = total
    squares = sum(squares[:, n * WIDE : (n + 1) * WIDE] for n in range(D // WIDE))
    norm_copies = []
    norm_got[w.seq] = squares
    for k in range(1, count):
        copy = remote(norm_got.at[w.seq], norm_got.at[w.seq], send_norm.at[k - 1],
                      recv_norm.at[k - 1], (w.seq_at(k), w.batch))
        copy.start()
        norm_copies.append(copy)
    for copy in norm_copies:
        copy.wait_recv()
    part = norm_got[0]
    for n in range(1, count):
        part = part + norm_got[n]
    here = count + w.batch
    norm_got[here] = part
    for k, peer in enumerate(others):
        copy = remote(norm_got.at[here], norm_got.at[here], send_norm.at[count - 1 + k],
                      recv_norm.at[count - 1 + k], peer)
        copy.start()
        norm_copies.append(copy)
    for copy in norm_copies[count - 1 :]:
        copy.wait_recv()
    part = norm_got[count]
    for n in range(1, w.nz * w.ny):
        part = part + norm_got[count + n]
    square = jnp.sum(jnp.sum(part, axis=1, keepdims=True), axis=0, keepdims=True)
    extra = jnp.sum(jnp.sum(whole * whole, axis=1, keepdims=True), axis=0, keepdims=True)
    grad_norm = jnp.sqrt(square + extra)
    norm_out[...] = jnp.broadcast_to(grad_norm, norm_out.shape)
    clip = clip_norm / jnp.maximum(grad_norm, clip_norm)
    for a in range(ARRAYS):
        weight, one, two = states[3 * a : 3 * a + 3]
        total = scatter.acc[a][w.x, w.z, w.y]
        limit = clip.reshape((1,) * total.ndim)
        results = adam_update(total, one[...], two[...], weight[...], limit, rate_matrix,
                              decay_weight)
        for ref, value in zip(new_states[3 * a : 3 * a + 3], results):
            ref[...] = value
    for copy in small_copies + norm_copies:
        copy.wait_send()
    scatter.finish()


def fast_local(mesh):
    nx, nz, ny = grid_of(mesh)
    count = 2 * nx
    whole_mem = pl.BlockSpec(memory_space=pltpu.VMEM)
    dma = lambda *shape: pltpu.SemaphoreType.DMA(shape)

    def call(kernel, outs, scratch, args, collective=None):
        params = dict(vmem_limit_bytes=VMEM_LIMIT)
        if collective is not None:
            params.update(collective_id=collective, has_side_effects=True)
        return pl.pallas_call(
            kernel,
            out_shape=[jax.ShapeDtypeStruct(s, t) for s, t in outs],
            in_specs=[whole_mem] * len(args),
            out_specs=[whole_mem] * len(outs),
            scratch_shapes=scratch,
            compiler_params=pltpu.CompilerParams(**params),
        )(*args)

    def body(tokens, doc_ids, out_grad,
             qkv_weight, qkv_first, qkv_second,
             proj_weight, proj_first, proj_second,
             up_weight, up_first, up_second,
             down_weight, down_first, down_second,
             pool_weight, pool_first, pool_second,
             small_weight, small_first, small_second):
        rows = tokens.shape[1]
        total = rows * count
        padded = -(-total // 512) * 512
        pools = out_grad.shape[1]
        ff = up_weight.shape[1]
        tok = tokens[0]
        grad = out_grad[0]
        seq, batch = lax.axis_index("seq"), lax.axis_index("batch")
        shard = seq * (nz * ny) + batch
        own = small_weight.shape[0]
        small_len = own * count * nz * ny
        place = lax.dynamic_update_slice(
            jnp.zeros((16 * D,), BF), small_weight.astype(BF), (shard * own,)
        ).reshape(16, D)
        half = HEAD_DIM // 2
        lanes = jnp.arange(WIDE)
        frequency = jnp.exp(-math.log(10000.0) * jnp.arange(half, dtype=F32) / half)
        positions = seq * rows + jnp.arange(rows, dtype=jnp.int32)
        angles = positions.astype(F32)[:, None] * frequency[None, :]
        cosine, sine = jnp.cos(angles), jnp.sin(angles)
        turn = jnp.stack([
            jnp.concatenate([cosine] * 4, axis=1),
            jnp.concatenate([-sine, sine] * 2, axis=1),
        ])
        weights = (qkv_weight, proj_weight, up_weight, down_weight, pool_weight)
        firsts = (qkv_first, proj_first, up_first, down_first, pool_first)
        seconds = (qkv_second, proj_second, up_second, down_second, pool_second)
        lead = (nx, 2, nz, ny)
        outs = [(lead + v.shape, BF) for v in weights]
        outs += [((16, D), F32), ((3, padded, WIDE), BF)]
        *fulls, small, qkv_all = call(
            lambda *r: start_kernel(nx, nz, ny, *r), outs,
            [pltpu.VMEM((count, 3, rows, WIDE), BF), pltpu.VMEM((nz + 6, 16, D), BF),
             dma(ARRAYS, nz + 2), dma(ARRAYS, nz + 2), dma(nz + 2), dma(nz + 2), dma(3), dma(3)],
            (tok, *weights, place, turn), 0)
        g_qkv, g_proj, g_up, g_down, g_pool = fulls
        ext, o_ref, o_low = call(
            forward_kernel,
            [((3, 2, padded, WIDE), BF), ((total, WIDE), F32), ((total, WIDE), BF)], [],
            (doc_ids, qkv_all))
        outs = [((total, WIDE), BF), ((pools, D), BF), ((count, rows, WIDE), BF),
                ((rows, D), BF), ((rows, ff), BF), ((rows, ff), BF), ((rows, D), BF),
                ((rows, D), BF), ((pools, 3 * D), BF), ((rows, D), F32), ((16, D), F32)]
        (do_all, short_out, att, normed_two, act, d_hidden, d_branch, d_attn, grouped, dh_one,
         small_grad) = call(
            lambda *r: middle_kernel(nx, nz, ny, *r), outs,
            [pltpu.VMEM((D // WIDE, rows + 16, WIDE), F32),
             pltpu.VMEM((D // WIDE, rows + 16, WIDE), F32),
             pltpu.VMEM((rows, D), F32), pltpu.VMEM((rows, D), F32), pltpu.VMEM((rows, D), F32),
             pltpu.VMEM((count, rows, WIDE), BF), pltpu.VMEM((16, D), BF),
             pltpu.VMEM((16, D), BF), pltpu.VMEM((2, 16, D), BF),
             dma(3), dma(3), dma(3), dma(3), dma(2), dma(2)],
            (o_low, tok, grad, g_proj, g_up, g_down, g_pool, small), 1)
        (d_qkv,) = call(
            backward_kernel, [((count, 3, rows, WIDE), BF)],
            [pltpu.VMEM((2, padded, WIDE), BF)] + [pltpu.VMEM((2, padded, WIDE), F32)] * 3,
            (ext, o_ref, do_all))

        shapes = [v.shape for v in weights]
        outs = [((rows, D), F32), ((16, D), F32), ((8, WIDE), F32)]
        outs += [(s, F32) for s in shapes for _ in range(3)]
        scratch = [pltpu.VMEM((count, 3, rows, WIDE), BF), pltpu.VMEM((3, rows, D), BF),
                   pltpu.VMEM((rows, D), BF)]
        scratch += [pltpu.VMEM((nx, nz, ny) + s, F32) for s in shapes]
        scratch += [pltpu.VMEM((nx, nz, ny) + s, BF) for _ in range(2) for s in shapes]
        two = [(nz, ny) if o[0] == "x" else (nx, nz) for o in Scatter.ORDERS]
        scratch += [pltpu.VMEM(t + s, BF) for _ in range(2) for t, s in zip(two, shapes)]
        scratch += [pltpu.VMEM((nz,) + s, BF) for _ in range(2) for s in shapes]
        scratch += [pltpu.VMEM((nz - 1,) + s, BF) for _ in range(2) for s in shapes]
        scratch += [pltpu.VMEM((7 + nz, 16, D), F32),
                    pltpu.VMEM((count + nz * ny, 8, WIDE), F32)]
        norm_slots = count - 1 + nz * ny - 1
        for slots in ((ARRAYS, nz + 2), (3,), (nz + 2,), (norm_slots,)):
            scratch += [dma(*slots), dma(*slots)]
        states = [v for trio in zip(weights, firsts, seconds) for v in trio]
        done = call(
            lambda *r: end_kernel(nx, nz, ny, *r), outs, scratch,
            (d_qkv, tok, turn, g_qkv, small, att, normed_two, act, d_hidden, d_branch, d_attn,
             grouped, grad, dh_one, small_grad, *states), 2)
        input_grad, small_total, norm_out = done[:3]
        new_states = done[3:]
        grad_norm = norm_out[0, 0]
        clip = clip_norm / jnp.maximum(grad_norm, clip_norm)
        small_part = lax.dynamic_slice(small_total.reshape(-1), (shard * own,), (own,))
        small_new = adam_update(small_part, small_first, small_second, small_weight, clip,
                                rate_vector, 0.0)
        return (short_out[None], input_grad[None], grad_norm, *new_states, *small_new)

    return body


def solution(mesh):
    in_specs = (
        P("batch", "seq", None),
        P("batch", None),
        P("batch", "seq", None),
        P(None, ("seq", "batch"), None),
        P(None, ("seq", "batch"), None),
        P(None, ("seq", "batch"), None),
        P(("seq", "batch"), None),
        P(("seq", "batch"), None),
        P(("seq", "batch"), None),
        P(("seq", "batch"), None),
        P(("seq", "batch"), None),
        P(("seq", "batch"), None),
        P(("seq", "batch"), None),
        P(("seq", "batch"), None),
        P(("seq", "batch"), None),
        P(("seq", "batch"), None),
        P(("seq", "batch"), None),
        P(("seq", "batch"), None),
        P(("seq", "batch")),
        P(("seq", "batch")),
        P(("seq", "batch")),
    )
    out_specs = (
        P("batch", "seq", None),
        P("batch", "seq", None),
        P(),
        P(None, ("seq", "batch"), None),
        P(None, ("seq", "batch"), None),
        P(None, ("seq", "batch"), None),
        P(("seq", "batch"), None),
        P(("seq", "batch"), None),
        P(("seq", "batch"), None),
        P(("seq", "batch"), None),
        P(("seq", "batch"), None),
        P(("seq", "batch"), None),
        P(("seq", "batch"), None),
        P(("seq", "batch"), None),
        P(("seq", "batch"), None),
        P(("seq", "batch"), None),
        P(("seq", "batch"), None),
        P(("seq", "batch"), None),
        P(("seq", "batch")),
        P(("seq", "batch")),
        P(("seq", "batch")),
    )
    body = fast_local(mesh) if fits(mesh) else local
    return jax.shard_map(body, mesh=mesh, in_specs=in_specs, out_specs=out_specs, check_vma=False)
```

```python
import math

import jax
import jax.numpy as jnp
import numpy as np
from jax import lax
from jax.experimental import pallas as pl
from jax.experimental.pallas import tpu as pltpu
from jax.sharding import PartitionSpec as P

D = 512
HEAD_DIM = 64
STEP = 10


beta_one = 0.9
beta_two = 0.999
adam_eps = 1e-08
norm_eps = 1e-05
clip_norm = 1.0
rate_matrix = 0.05
rate_vector = 0.5
decay_weight = 0.1
masked_score = -1e30


def from_behind(block, axis, distance):
    devices = range(lax.axis_size(axis))
    route = [(i - distance, i) for i in devices if i - distance in devices]
    return lax.ppermute(block, axis, route)


def layer_norm(values, scale_gain, shift_vec):
    center = values - jnp.mean(values, axis=-1, keepdims=True)
    spread = jnp.mean(center * center, axis=-1, keepdims=True)
    return center * lax.rsqrt(spread + norm_eps) * scale_gain + shift_vec


def rotate(values, positions):
    half_dim = HEAD_DIM // 2
    head_view = values.reshape(values.shape[0], values.shape[1] // HEAD_DIM, HEAD_DIM)
    frequency = jnp.exp(-math.log(10000.0) * jnp.arange(half_dim, dtype=jnp.float32) / half_dim)
    angles = positions.astype(jnp.float32)[:, None] * frequency[None, :]
    cosine = jnp.cos(angles)[:, None, :]
    sine_part = jnp.sin(angles)[:, None, :]
    first_half = head_view[..., :half_dim]
    second_half = head_view[..., half_dim:]
    turned = jnp.concatenate(
        [
            first_half * cosine - second_half * sine_part,
            second_half * cosine + first_half * sine_part,
        ],
        axis=-1,
    )
    return turned.reshape(values.shape)


def outer_sum(left_side, right_side):
    return lax.dot_general(
        left_side, right_side, (((0,), (0,)), ((), ())), preferred_element_type=jnp.float32
    )


def times_transpose(left_side, right_side):
    return lax.dot_general(
        left_side, right_side, (((1,), (1,)), ((), ())), preferred_element_type=jnp.float32
    )


def split_heads(values):
    return values.reshape(values.shape[0], values.shape[1] // HEAD_DIM, HEAD_DIM)


def block_scores(query_heads, key_heads, query_pos, key_pos, query_doc, key_doc):
    raw_scores = jnp.einsum(
        "qhd,khd->hqk", query_heads, key_heads, preferred_element_type=jnp.float32
    ) * HEAD_DIM ** (-0.5)
    allowed = (key_pos[None, :] <= query_pos[:, None]) & (key_doc[None, :] == query_doc[:, None])
    return jnp.where(allowed[None], raw_scores, masked_score)


def adam_update(gradient, first_moment, second_moment, weight, clip_scale, step_rate, decay_rate):
    clipped = gradient * clip_scale
    first_new = beta_one * first_moment + (1.0 - beta_one) * clipped
    second_new = beta_two * second_moment + (1.0 - beta_two) * clipped * clipped
    first_hat = first_new / (1.0 - beta_one**STEP)
    second_hat = second_new / (1.0 - beta_two**STEP)
    weight_new = weight - step_rate * (
        first_hat / (jnp.sqrt(second_hat) + adam_eps) + decay_rate * weight
    )
    return (first_new, second_new, weight_new)


def local(
    tokens,
    doc_ids,
    out_grad,
    qkv_weight,
    qkv_first,
    qkv_second,
    proj_weight,
    proj_first,
    proj_second,
    up_weight,
    up_first,
    up_second,
    down_weight,
    down_first,
    down_second,
    pool_weight,
    pool_first,
    pool_second,
    small_weight,
    small_first,
    small_second,
):
    block_rows = tokens.shape[1]
    model_width = tokens.shape[2]
    seq_count = lax.axis_size("seq")
    my_block = lax.axis_index("seq")
    whole_qkv, whole_proj, whole_up, whole_down, whole_pool, whole_small = (
        lax.all_gather(qkv_weight.astype(jnp.bfloat16), ("seq", "batch"), axis=1, tiled=True),
        lax.all_gather(proj_weight.astype(jnp.bfloat16), ("seq", "batch"), axis=0, tiled=True),
        lax.all_gather(up_weight.astype(jnp.bfloat16), ("seq", "batch"), axis=0, tiled=True),
        lax.all_gather(down_weight.astype(jnp.bfloat16), ("seq", "batch"), axis=0, tiled=True),
        lax.all_gather(pool_weight.astype(jnp.bfloat16), ("seq", "batch"), axis=0, tiled=True),
        lax.all_gather(small_weight.astype(jnp.bfloat16), ("seq", "batch"), axis=0, tiled=True),
    )
    small_used = whole_small.astype(jnp.float32)
    gain_first = small_used[0:D]
    shift_first = small_used[D : 2 * D]
    gain_second = small_used[2 * D : 3 * D]
    shift_second = small_used[3 * D : 4 * D]
    bias_down = small_used[4 * D : 5 * D]
    bias_pool = small_used[5 * D : 6 * D]
    bias_up = small_used[6 * D :]
    inputs = tokens[0].astype(jnp.float32)
    doc_row = doc_ids[0]
    first_row = my_block * block_rows
    positions = first_row + jnp.arange(block_rows, dtype=jnp.int32)
    doc_mine = lax.dynamic_slice_in_dim(doc_row, first_row, block_rows)
    normed, first_pull = jax.vjp(layer_norm, inputs, gain_first, shift_first)
    normed_low = normed.astype(jnp.bfloat16)
    projected = jnp.einsum("td,cde->cte", normed_low, whole_qkv, preferred_element_type=jnp.float32)
    queries_rot, query_pull = jax.vjp(lambda values: rotate(values, positions), projected[0])
    keys_rot, key_pull = jax.vjp(lambda values: rotate(values, positions), projected[1])
    query_low = queries_rot.astype(jnp.bfloat16)
    key_low = keys_rot.astype(jnp.bfloat16)
    value_low = projected[2].astype(jnp.bfloat16)
    keys_all, values_all = (
        lax.all_gather(key_low, "seq", axis=0, tiled=True),
        lax.all_gather(value_low, "seq", axis=0, tiled=True),
    )
    query_heads = split_heads(query_low)
    head_count = query_heads.shape[1]
    zeros_head_rows = jnp.zeros((head_count, block_rows), jnp.float32)
    zeros_heads = jnp.zeros((block_rows, head_count, HEAD_DIM), jnp.float32)

    def scores_of(number):
        start_row = number * block_rows
        key_heads = split_heads(keys_all[start_row : start_row + block_rows])
        value_heads = split_heads(values_all[start_row : start_row + block_rows])
        key_pos = start_row + jnp.arange(block_rows, dtype=jnp.int32)
        key_doc = doc_row[start_row : start_row + block_rows]
        scores = block_scores(query_heads, key_heads, positions, key_pos, doc_mine, key_doc)
        return (scores, key_heads, value_heads)

    running_max = jnp.full((head_count, block_rows), masked_score, jnp.float32)
    running_sum = zeros_head_rows
    for number in range(seq_count):

        def block_stats(number=number):
            scores = scores_of(number)[0]
            block_max = jnp.max(scores, axis=-1)
            return (block_max, jnp.sum(jnp.exp(scores - block_max[..., None]), axis=-1))

        block_max, block_sum = block_stats()
        new_max = jnp.maximum(running_max, block_max)
        running_sum = running_sum * jnp.exp(running_max - new_max) + block_sum * jnp.exp(
            block_max - new_max
        )
        running_max = new_max
    log_total = running_max + jnp.log(running_sum)
    attended = zeros_heads
    for number in range(seq_count):

        def block_output(number=number):
            scores, key_heads, value_heads = scores_of(number)
            soft_probs = jnp.exp(scores - log_total[..., None]).astype(jnp.bfloat16)
            return jnp.einsum(
                "hqk,khd->qhd", soft_probs, value_heads, preferred_element_type=jnp.float32
            )

        attended = attended + block_output()
    attended_low = attended.reshape(block_rows, model_width).astype(jnp.bfloat16)
    h_one = inputs + jnp.dot(attended_low, whole_proj, preferred_element_type=jnp.float32)
    normed_two, second_pull = jax.vjp(layer_norm, h_one, gain_second, shift_second)
    normed_two_low = normed_two.astype(jnp.bfloat16)
    hidden_pre = jnp.dot(normed_two_low, whole_up, preferred_element_type=jnp.float32) + bias_up
    activated, gelu_pull = jax.vjp(jax.nn.gelu, hidden_pre)
    act_low = activated.astype(jnp.bfloat16)
    h_two = h_one + jnp.dot(act_low, whole_down, preferred_element_type=jnp.float32) + bias_down
    h_two_low = h_two.astype(jnp.bfloat16)
    prev_rows = from_behind(h_two_low[block_rows - 2 :], "seq", 1)
    shifted = jnp.concatenate([prev_rows, h_two_low[: block_rows - 2]], axis=0)
    grouped = shifted.reshape(block_rows // 3, 3 * model_width)
    short_rows = (
        jnp.dot(grouped, whole_pool, preferred_element_type=jnp.float32) + bias_pool
    ).astype(jnp.bfloat16)
    out_rows = out_grad[0]
    grad_pool = outer_sum(grouped, out_rows)
    grad_bias_pool = jnp.sum(out_rows.astype(jnp.float32), axis=0)
    spread_rows = times_transpose(out_rows, whole_pool).reshape(block_rows, model_width)
    returned = from_behind(spread_rows[:2], "seq", -1)
    grad_h_two = jnp.concatenate([spread_rows[2:], returned], axis=0)
    grad_branch = grad_h_two.astype(jnp.bfloat16)
    grad_down = outer_sum(act_low, grad_branch)
    grad_bias_down = jnp.sum(grad_branch.astype(jnp.float32), axis=0)
    grad_act = times_transpose(grad_branch, whole_down)
    grad_hidden = gelu_pull(grad_act)[0].astype(jnp.bfloat16)
    grad_up = outer_sum(normed_two_low, grad_hidden)
    grad_bias_up = jnp.sum(grad_hidden.astype(jnp.float32), axis=0)
    grad_normed_two = times_transpose(grad_hidden, whole_up)
    back_h_one, grad_gain_second, grad_shift_second = second_pull(grad_normed_two)
    grad_h_one = grad_h_two + back_h_one
    grad_attn = grad_h_one.astype(jnp.bfloat16)
    grad_proj = outer_sum(attended_low, grad_attn)
    grad_attended = times_transpose(grad_attn, whole_proj).astype(jnp.bfloat16)
    grad_heads = split_heads(grad_attended)
    row_delta = zeros_head_rows
    value_terms = []
    for number in range(seq_count):

        def block_first(number=number):
            scores, key_heads, value_heads = scores_of(number)
            soft_probs = jnp.exp(scores - log_total[..., None])
            grad_probs = jnp.einsum(
                "qhd,khd->hqk", grad_heads, value_heads, preferred_element_type=jnp.float32
            )
            part_delta = jnp.sum(soft_probs * grad_probs, axis=-1)
            value_grad = jnp.einsum(
                "hqk,qhd->khd",
                soft_probs.astype(jnp.bfloat16),
                grad_heads,
                preferred_element_type=jnp.float32,
            )
            return (part_delta, value_grad.reshape(block_rows, model_width))

        part_delta, value_grad = block_first()
        row_delta = row_delta + part_delta
        value_terms.append(value_grad)
    grad_query = zeros_heads
    key_terms = []
    for number in range(seq_count):

        def block_second(number=number):
            scores, key_heads, value_heads = scores_of(number)
            soft_probs = jnp.exp(scores - log_total[..., None])
            grad_probs = jnp.einsum(
                "qhd,khd->hqk", grad_heads, value_heads, preferred_element_type=jnp.float32
            )
            grad_scores = (soft_probs * (grad_probs - row_delta[..., None])).astype(jnp.bfloat16)
            query_part = jnp.einsum(
                "hqk,khd->qhd", grad_scores, key_heads, preferred_element_type=jnp.float32
            )
            key_part = jnp.einsum(
                "hqk,qhd->khd", grad_scores, query_heads, preferred_element_type=jnp.float32
            )
            return (query_part, key_part.reshape(block_rows, model_width))

        query_part, key_part = block_second()
        grad_query = grad_query + query_part
        key_terms.append(key_part)
    head_scale = HEAD_DIM ** (-0.5)
    grad_keys, grad_values = (
        lax.psum_scatter(
            (jnp.concatenate(key_terms, axis=0) * head_scale).astype(jnp.bfloat16),
            "seq",
            scatter_dimension=0,
            tiled=True,
        ).astype(jnp.float32),
        lax.psum_scatter(
            jnp.concatenate(value_terms, axis=0).astype(jnp.bfloat16),
            "seq",
            scatter_dimension=0,
            tiled=True,
        ).astype(jnp.float32),
    )
    grad_q_pre = query_pull(grad_query.reshape(block_rows, model_width) * head_scale)[0].astype(
        jnp.bfloat16
    )
    grad_k_pre = key_pull(grad_keys)[0].astype(jnp.bfloat16)
    grad_v_pre = grad_values.astype(jnp.bfloat16)
    stacked = jnp.stack([grad_q_pre, grad_k_pre, grad_v_pre])
    grad_qkv = jnp.einsum("td,cte->cde", normed_low, stacked, preferred_element_type=jnp.float32)
    grad_normed = jnp.einsum("cte,cde->td", stacked, whole_qkv, preferred_element_type=jnp.float32)
    back_inputs, grad_gain_first, grad_shift_first = first_pull(grad_normed)
    input_grad = (grad_h_one + back_inputs)[None]
    grad_small = jnp.concatenate(
        [
            grad_gain_first,
            grad_shift_first,
            grad_gain_second,
            grad_shift_second,
            grad_bias_down,
            grad_bias_pool,
            grad_bias_up,
        ]
    )
    all_grads = (grad_qkv, grad_proj, grad_up, grad_down, grad_pool, grad_small)
    shards = (
        lax.psum_scatter(all_grads[0], ("seq", "batch"), scatter_dimension=1, tiled=True),
        lax.psum_scatter(all_grads[1], ("seq", "batch"), scatter_dimension=0, tiled=True),
        lax.psum_scatter(all_grads[2], ("seq", "batch"), scatter_dimension=0, tiled=True),
        lax.psum_scatter(all_grads[3], ("seq", "batch"), scatter_dimension=0, tiled=True),
        lax.psum_scatter(all_grads[4], ("seq", "batch"), scatter_dimension=0, tiled=True),
        lax.psum_scatter(all_grads[5], ("seq", "batch"), scatter_dimension=0, tiled=True),
    )
    local_squares = sum((jnp.sum(portion * portion) for portion in shards))
    grad_norm = jnp.sqrt(lax.psum(local_squares, ("seq", "batch")))
    clip_scale = clip_norm / jnp.maximum(grad_norm, clip_norm)
    masters = (qkv_weight, proj_weight, up_weight, down_weight, pool_weight, small_weight)
    firsts = (qkv_first, proj_first, up_first, down_first, pool_first, small_first)
    seconds = (qkv_second, proj_second, up_second, down_second, pool_second, small_second)
    new_states = []
    for index_kind in range(6):
        step_rate = rate_vector if index_kind == 5 else rate_matrix
        decay_rate = 0.0 if index_kind == 5 else decay_weight
        new_states.append(
            adam_update(
                shards[index_kind],
                firsts[index_kind],
                seconds[index_kind],
                masters[index_kind],
                clip_scale,
                step_rate,
                decay_rate,
            )
        )
    return (
        short_rows[None],
        input_grad,
        grad_norm,
        new_states[0][0],
        new_states[0][1],
        new_states[0][2],
        new_states[1][0],
        new_states[1][1],
        new_states[1][2],
        new_states[2][0],
        new_states[2][1],
        new_states[2][2],
        new_states[3][0],
        new_states[3][1],
        new_states[3][2],
        new_states[4][0],
        new_states[4][1],
        new_states[4][2],
        new_states[5][0],
        new_states[5][1],
        new_states[5][2],
    )


MESH = pl.DeviceIdType.MESH
BF = jnp.bfloat16
F32 = jnp.float32
WIDE = 128
HEADS = 2
LOG2E = math.log2(math.e)
NN = (((1,), (0,)), ((), ()))
NT = (((1,), (1,)), ((), ()))
TN = (((0,), (0,)), ((), ()))
VMEM_LIMIT = 121 * 2**19
PROJ, UP, DOWN, POOL = range(4)
ARRAYS = 4
GELU_C = math.sqrt(2.0 / math.pi)
DOCS = 7
PAD = 16


def dot(a, b, dims=NN):
    return lax.dot_general(a, b, dims, preferred_element_type=F32)


def grid_of(mesh):
    seq, batch = mesh.shape["seq"], mesh.shape["batch"]
    return seq // 2, batch // 2, 2


def fits(mesh):
    seq, batch = mesh.shape["seq"], mesh.shape["batch"]
    return seq == 4 and batch % 2 == 0 and D % (seq * batch * 16) == 0


class Where:
    def __init__(self, nx, nz, ny):
        self.nx, self.nz, self.ny = nx, nz, ny
        self.count, self.batches = 2 * nx, nz * ny
        seq, batch = lax.axis_index("seq"), lax.axis_index("batch")
        self.seq = seq
        self.batch = batch
        self.x, self.c = lax.div(seq, 2), lax.rem(seq, 2)
        self.z, self.y = lax.div(batch, ny), lax.rem(batch, ny)
        self.xo, self.co, self.yo = 1 - self.x, 1 - self.c, 1 - self.y

    def dev(self, x=None, c=None, z=None, y=None):
        x = self.x if x is None else x
        c = self.c if c is None else c
        z = self.z if z is None else z
        y = self.y if y is None else y
        return (x * 2 + c, z * self.ny + y)

    def z_at(self, step):
        return lax.rem(self.z + step, self.nz)

    def seq_at(self, step):
        return lax.rem(self.seq + step, self.count)

    def batch_at(self, step):
        return lax.rem(self.batch + step, self.batches)

    def partner(self, stage):
        return {
            "x": self.dev(x=self.xo),
            "c": self.dev(c=self.co),
            "y": self.dev(y=self.yo),
        }[stage]

    def seq_peers(self):
        return [(self.seq_at(k), self.batch) for k in range(1, self.count)]

    def batch_peers(self):
        return [(self.seq, self.batch_at(k)) for k in range(1, self.batches)]


def remote(src, dst, send, recv, peer):
    return pltpu.make_async_remote_copy(
        src, dst, send, recv, device_id=peer, device_id_type=MESH
    )


class Links:
    def __init__(self):
        self.open = []

    def start(self, copies):
        for copy in copies:
            copy.start()
        self.open += copies
        return copies

    def finish(self):
        for copy in self.open:
            copy.wait_send()
        self.open = []


def arrive(copies):
    for copy in copies:
        copy.wait_recv()


class Gather:
    ORDERS = ("zyxc", "zxyc", "zyxc", "xzyc")

    def __init__(self, w, links, fulls, send, recv):
        self.w, self.links = w, links
        self.fulls, self.send, self.recv = fulls, send, recv
        self.copies = {}

    def start(self, a, index):
        w = self.w
        order = self.ORDERS[a]
        stage, done = order[index], order[:index]
        pick = [
            slice(None) if name in done else own
            for name, own in (("x", w.x), ("c", w.c), ("z", w.z), ("y", w.y))
        ]
        block = self.fulls[a].at[pick[0], pick[1], pick[2], pick[3]]
        if stage == "z":
            peers = [(k - 1, w.dev(z=w.z_at(k))) for k in range(1, w.nz)]
        else:
            peers = [(w.nz - 1 + "xyc".index(stage), w.partner(stage))]
        self.copies[a, index] = self.links.start([
            remote(block, block, self.send.at[a, slot], self.recv.at[a, slot], peer)
            for slot, peer in peers
        ])

    def step(self, a, index):
        arrive(self.copies[a, index])
        if index < 3:
            self.start(a, index + 1)


class Scatter:
    ORDERS = ("yx", "yx", "xy", "yx")

    def __init__(self, w, links, fulls, acc, two_out, two_in, three_out, three_in, z_out, z_in,
                 send, recv):
        self.w, self.links, self.acc = w, links, acc
        self.c_out = [full.at[:, 0] for full in fulls]
        self.c_in = [full.at[:, 1] for full in fulls]
        self.two_out, self.two_in = two_out, two_in
        self.three_out, self.three_in = three_out, three_in
        self.z_out, self.z_in = z_out, z_in
        self.send, self.recv = send, recv
        self.copies, self.make = {}, {}

    def go(self, a, index, src, dst, slot, peer):
        copies = self.links.start(
            [remote(src, dst, self.send.at[a, slot], self.recv.at[a, slot], peer)]
        )
        self.copies.setdefault((a, index), []).extend(copies)

    def begin(self, a, make):
        w = self.w
        self.make[a] = make
        shape = self.c_out[a].shape[1:]
        for x_of in range(w.nx):
            self.c_out[a][x_of] = make(x_of * 2 + w.co).reshape(shape).astype(BF)
        self.go(a, 0, self.c_out[a], self.c_in[a], 0, w.partner("c"))

    def step_two(self, a):
        w = self.w
        acc, got, out = self.acc[a], self.c_in[a], self.two_out[a]
        shape = got.shape[1:]
        arrive(self.copies[a, 0])
        if self.ORDERS[a][0] == "x":
            away = self.make[a](w.xo * 2 + w.c).reshape(shape) + got[w.xo].astype(F32)
            out[...] = away.astype(BF)
            acc[...] = self.make[a](w.seq).reshape(shape) + got[w.x].astype(F32)
        else:
            even = w.y == 0
            for x_of in range(w.nx):
                both = self.make[a](x_of * 2 + w.c).reshape(shape) + got[x_of].astype(F32)
                acc[x_of] = jnp.where(even, both[:, 0], both[:, 1])
                out[x_of] = jnp.where(even, both[:, 1], both[:, 0]).astype(BF)
        self.go(a, 1, out, self.two_in[a], 1, w.partner(self.ORDERS[a][0]))

    def step_three(self, a):
        w = self.w
        acc, more, out = self.acc[a], self.two_in[a], self.three_out[a]
        arrive(self.copies[a, 1])

        def body(n, _):
            if self.ORDERS[a][0] == "x":
                give, keep = (n, w.yo), (n, w.y)
            else:
                give, keep = (w.xo, n), (w.x, n)
            out[n] = (acc[give] + more[give].astype(F32)).astype(BF)
            acc[keep] = acc[keep] + more[keep].astype(F32)
            return 0

        lax.fori_loop(0, w.nz, body, 0)
        self.go(a, 2, out, self.three_in[a], 2, w.partner(self.ORDERS[a][1]))

    def kept(self, a, n):
        return (n, self.w.y) if self.ORDERS[a][0] == "x" else (self.w.x, n)

    def step_four(self, a):
        w = self.w
        acc, more = self.acc[a], self.three_in[a]
        arrive(self.copies[a, 2])
        for k in range(1, w.nz):
            to = w.z_at(k)
            self.z_out[a][k - 1] = (acc[self.kept(a, to)] + more[to].astype(F32)).astype(BF)
            self.go(a, 3, self.z_out[a].at[k - 1], self.z_in[a].at[k - 1], 2 + k, w.dev(z=to))
        own = self.kept(a, w.z)
        acc[own] = acc[own] + more[w.z].astype(F32)

    def last(self, a):
        arrive(self.copies[a, 3])
        total = self.acc[a][self.kept(a, self.w.z)]
        for k in range(1, self.w.nz):
            total = total + self.z_in[a][k - 1].astype(F32)
        return total


def norm_stats(values):
    center = values - jnp.mean(values, axis=-1, keepdims=True)
    spread = jnp.mean(center * center, axis=-1, keepdims=True)
    scale = lax.rsqrt(spread + norm_eps)
    return center * scale, scale


def norm_back(grad, unit, scale, gain):
    inner = grad * gain
    mean_one = jnp.mean(inner, axis=-1, keepdims=True)
    mean_two = jnp.mean(inner * unit, axis=-1, keepdims=True)
    back = scale * (inner - mean_one - unit * mean_two)
    return back, jnp.sum(grad * unit, axis=0, keepdims=True), jnp.sum(grad, axis=0, keepdims=True)


def swap_halves(values):
    lane = lax.broadcasted_iota(jnp.int32, values.shape, 1)
    return jnp.where(
        lax.rem(lane, HEAD_DIM) < HEAD_DIM // 2,
        pltpu.roll(values, WIDE - HEAD_DIM // 2, 1),
        pltpu.roll(values, HEAD_DIM // 2, 1),
    )


def in_head(lane, h):
    return (lane >= h * HEAD_DIM) & (lane < (h + 1) * HEAD_DIM)


def with_feats(base, lane, h, vector):
    one = vector.astype(BF).astype(F32)
    two = (vector - one).astype(BF).astype(F32)
    first = (1 - h) * HEAD_DIM + 8
    for n, term in enumerate((one, two, vector - one - two)):
        base = jnp.where(lane == first + n, term, base)
    return base


def document_edges(docs):
    feat = lax.rem(lax.broadcasted_iota(jnp.int32, (1, WIDE), 1), HEAD_DIM)
    lo = jnp.zeros((1, WIDE), jnp.int32)
    hi = jnp.zeros((1, WIDE), jnp.int32)
    below = jnp.zeros((1, 1), jnp.int32)
    for d in range(DOCS):
        upto = jnp.sum(jnp.where(docs <= d, 1, 0), axis=1, keepdims=True)
        lo = jnp.where(feat == d, below, lo)
        hi = jnp.where(feat == d, upto, hi)
        below = upto
    return lo, hi


def layer_buffers(nx, nz, ny, rows, ff, shapes):
    count, block = 2 * nx, rows + PAD
    batches = nz * ny
    vmem = lambda shape, kind=BF: pltpu.VMEM(shape, kind)
    wide = 3 * WIDE
    shard = shapes[0][0]
    two = [(nz, ny) if o[0] == "x" else (nx, nz) for o in Scatter.ORDERS]
    named = dict(
        fulls=[vmem((nx, 2, nz, ny) + s) for s in shapes],
        part=vmem((count, 3, shard, WIDE)),
        wq=vmem((count, nz, ny, 3, shard, WIDE)),
        small_seq=vmem((count, 16, D)),
        small_all=vmem((batches, 16, D)),
        small=vmem((16, D), F32),
        tok_all=vmem((count, rows, D)),
        normed=vmem((count, rows, D)),
        ext=vmem((3, HEADS, count * block, WIDE)),
        o_ref=vmem((count, block, WIDE), F32),
        o_low=vmem((count, block, WIDE)),
        att=vmem((count, rows, WIDE)),
        h_one=vmem((rows, D), F32),
        dh_two=vmem((D // WIDE, block, WIDE), F32),
        buf=[vmem((count, block, WIDE), F32) for _ in range(3)],
        normed_two=vmem((rows, D)),
        act=vmem((rows, ff)),
        d_hidden=vmem((rows, ff)),
        d_branch=vmem((rows, D)),
        d_attn=vmem((rows, D)),
        grouped=vmem((rows // 3, 3 * D)),
        edge=vmem((4, 16, D)),
        do_send=vmem((count, rows, WIDE)),
        do_ext=vmem((HEADS, count * block, WIDE)),
        stacked=vmem((rows, wide)),
        g_qkv=vmem((D, wide), F32),
        x_in=vmem((rows, D)),
        gq_out=vmem((batches, count, shard, wide)),
        gq_in=vmem((batches, count, shard, wide)),
        gq_seq=vmem((count, shard, wide)),
        gq_got=vmem((count, shard, wide)),
        small_grad=vmem((16, D), F32),
        sg_seq=vmem((count, 16, D), F32),
        sg_all=vmem((batches, 16, D), F32),
        norm_seq=vmem((count, 8, WIDE), F32),
        norm_all=vmem((batches, 8, WIDE), F32),
        acc=[vmem(t + s, F32) for t, s in zip(two, shapes)],
        two_out=[vmem(t + s) for t, s in zip(two, shapes)],
        two_in=[vmem(t + s) for t, s in zip(two, shapes)],
        three_out=[vmem((nz,) + s) for s in shapes],
        three_in=[vmem((nz,) + s) for s in shapes],
        z_out=[vmem((nz - 1,) + s) for s in shapes],
        z_in=[vmem((nz - 1,) + s) for s in shapes],
    )
    sems = dict(
        gather=(ARRAYS, nz + 2), scatter=(ARRAYS, nz + 2), tok=(7,), part=(count - 1,),
        wq=(batches - 1,), small_seq=(count - 1,), small_all=(batches - 1,), edge=(2,),
        o=(count, 2), do=(count - 1,), dn=(2,), x=(1,), gq=(batches - 1,), gq_seq=(count - 1,),
        sg_seq=(count - 1,), sg_all=(batches - 1,), norm_seq=(count - 1,),
        norm_all=(batches - 1,),
    )
    for name, shape in sems.items():
        named["sem_" + name] = [pltpu.SemaphoreType.DMA(shape) for _ in range(2)]
    named["ready"] = pltpu.SemaphoreType.REGULAR
    named["free"] = pltpu.SemaphoreType.REGULAR
    return named


class Bag:
    def __init__(self, template, refs):
        refs = list(refs)
        for name, value in template.items():
            if isinstance(value, list):
                setattr(self, name, [refs.pop(0) for _ in value])
            else:
                setattr(self, name, refs.pop(0))


def layer_kernel(nx, nz, ny, template, tokens, doc_ids, out_grad, qkv_w, proj_w, up_w, down_w,
                 pool_w, small_in, turn, offset, short_out, input_grad, total_qkv, total_proj,
                 total_up, total_down, total_pool, small_total, norm_out, *scratch):
    w = Where(nx, nz, ny)
    b = Bag(template, scratch)
    links = Links()
    rows = tokens.shape[0]
    block = rows + PAD
    count, batches = w.count, w.batches
    pools = rows // 3
    sub = rows // 3
    tiles = D // WIDE
    own = (w.x, w.c, w.z, w.y)

    barrier = pltpu.get_barrier_semaphore()
    peers = w.seq_peers() + w.batch_peers()
    for peer in peers:
        pl.semaphore_signal(barrier, inc=1, device_id=peer, device_id_type=MESH)
    b.small_seq[w.seq] = small_in[...]
    for d in range(count):
        b.part[d] = qkv_w[:, :, d * WIDE : (d + 1) * WIDE].astype(BF)
    b.edge[0] = out_grad[0:16]
    pl.semaphore_wait(barrier, len(peers))

    send, recv = b.sem_tok
    mine = b.tok_all.at[w.seq]

    def piece(ref, n):
        return ref.at[pl.ds(n * sub, sub)]

    small_a = links.start([
        remote(b.small_seq.at[w.seq], b.small_seq.at[w.seq], b.sem_small_seq[0].at[k],
               b.sem_small_seq[1].at[k], peer)
        for k, peer in enumerate(w.seq_peers())
    ])
    part_a = links.start([
        remote(b.part.at[w.seq_at(k + 1)], b.wq.at[w.seq, w.z, w.y], b.sem_part[0].at[k],
               b.sem_part[1].at[k], peer)
        for k, peer in enumerate(w.seq_peers())
    ])
    tok_x = links.start([
        remote(piece(tokens, n), piece(mine, n), send.at[n], recv.at[n], w.partner("x"))
        for n in range(3)
    ])
    tok_c = links.start([remote(tokens, mine, send.at[3], recv.at[3], w.partner("c"))])
    links.start([
        remote(b.edge.at[0], b.edge.at[1], b.sem_edge[0].at[0], b.sem_edge[1].at[0],
               (w.seq_at(count - 1), w.batch))
    ])
    grad_edge = links.open[-1:]
    b.wq[w.seq, w.z, w.y] = b.part[w.seq]
    shards = (proj_w, up_w, down_w, pool_w)
    for shard, full in zip(shards, b.fulls):
        full[own] = shard[...].astype(BF)
    lo, hi = document_edges(doc_ids[...])
    arrive(small_a)
    total = b.small_seq[0].astype(F32)
    for n in range(1, count):
        total = total + b.small_seq[n].astype(F32)
    b.small_all[w.batch] = total.astype(BF)
    small_b = links.start([
        remote(b.small_all.at[w.batch], b.small_all.at[w.batch], b.sem_small_all[0].at[k],
               b.sem_small_all[1].at[k], peer)
        for k, peer in enumerate(w.batch_peers())
    ])
    arrive(part_a)
    part_b = links.start([
        remote(b.wq.at[:, w.z, w.y], b.wq.at[:, w.z, w.y], b.sem_wq[0].at[k],
               b.sem_wq[1].at[k], peer)
        for k, peer in enumerate(w.batch_peers())
    ])
    gather = Gather(w, links, b.fulls, *b.sem_gather)
    gather.start(PROJ, 0)
    gather.start(UP, 0)
    gather.start(DOWN, 0)
    b.tok_all[w.seq] = tokens[...]

    lane_row = lax.broadcasted_iota(jnp.int32, (1, WIDE), 1)
    feat_row = lax.rem(lane_row, HEAD_DIM)
    pad_lane = lax.broadcasted_iota(jnp.int32, (PAD, WIDE), 1)
    for h in range(HEADS):
        for n in range(count):
            pad = pl.ds(n * block + rows, PAD)
            b.ext[0, h, pad] = jnp.zeros((PAD, WIDE), BF)
            masks = ~in_head(pad_lane, h) & (lax.rem(pad_lane, HEAD_DIM) < DOCS)
            b.ext[1, h, pad] = jnp.where(masks, masked_score, 0.0).astype(BF)
            b.ext[2, h, pad] = jnp.zeros((PAD, WIDE), BF)
            b.do_ext[h, pad] = jnp.zeros((PAD, WIDE), BF)

    arrive(small_b)
    total = b.small_all[0].astype(F32)
    for n in range(1, batches):
        total = total + b.small_all[n].astype(F32)
    b.small[...] = total
    small = b.small
    arrive(part_b)

    def qkv_weight(n):
        return b.wq[:, :, :, n].reshape(D, WIDE)

    def turning(of_block, r0):
        cos_in, sin_in = turn[0, pl.ds(r0, sub)], turn[1, pl.ds(r0, sub)]
        cos_of, sin_of = offset[0, pl.ds(of_block, 1)], offset[1, pl.ds(of_block, 1)]
        return cos_in * cos_of - sin_in * sin_of, sin_in * cos_of + cos_in * sin_of

    def project(of_block):
        weight = jnp.concatenate([qkv_weight(n) for n in range(3)], axis=1)

        def body(n, _):
            r0 = pl.multiple_of(n * sub, 16)
            unit, _ = norm_stats(b.tok_all[of_block, pl.ds(r0, sub)].astype(F32))
            normed = (unit * small[0:1] + small[1:2]).astype(BF)
            b.normed[of_block, pl.ds(r0, sub)] = normed
            qkv = dot(normed, weight)
            cosine, sine = turning(of_block, r0)
            parts = [qkv[:, m * WIDE : (m + 1) * WIDE] for m in range(3)]
            for m in range(2):
                parts[m] = parts[m] * cosine + swap_halves(parts[m]) * sine
            parts[0] = parts[0] * (LOG2E * HEAD_DIM ** -0.5)
            place = lax.broadcasted_iota(jnp.int32, (sub, WIDE), 0) + (of_block * rows + r0)
            lane = lax.broadcasted_iota(jnp.int32, (sub, WIDE), 1)
            same = (place >= lo) & (place < hi)
            ones = jnp.where((feat_row >= 8) & (feat_row < 11), 1.0, 0.0)
            q_feat = jnp.where(same, 1.0, 0.0)
            k_feat = jnp.where(feat_row < DOCS, jnp.where(same, 0.0, masked_score), ones)
            at = pl.ds(pl.multiple_of(of_block * block + r0, 16), sub)
            for h in range(HEADS):
                for m, feats in enumerate((q_feat, k_feat, 1.0)):
                    b.ext[m, h, at] = jnp.where(in_head(lane, h), parts[m], feats).astype(BF)
            return 0

        lax.fori_loop(0, 3, body, 0)

    project(w.seq)
    arrive(tok_c)
    project(w.x * 2 + w.co)
    theirs = b.tok_all.at[w.xo * 2 + w.c]
    passed = []
    for n in range(3):
        arrive(tok_x[n : n + 1])
        passed += links.start([
            remote(piece(theirs, n), piece(theirs, n), send.at[4 + n], recv.at[4 + n],
                   w.partner("c"))
        ])
    gather.start(POOL, 0)
    project(w.xo * 2 + w.c)
    arrive(passed)
    project(w.xo * 2 + w.co)

    half_rows = (block // 2, rows - block // 2)

    def attend(of_block, half):
        size = block // 2
        r0 = of_block * block + half * size
        n = min(count * block, -(-(r0 + size) // 256) * 256)
        m0 = (r0 // 128) * 128
        lane = lax.broadcasted_iota(jnp.int32, (size, WIDE), 1)
        outs = []
        for h in range(HEADS):
            q = b.ext[0, h, pl.ds(r0, size)]
            s = dot(q, b.ext[1, h, :n], NT)
            at_row = lax.broadcasted_iota(jnp.int32, (size, n - m0), 0) + r0
            at_col = lax.broadcasted_iota(jnp.int32, (size, n - m0), 1) + m0
            tail = jnp.where(at_col <= at_row, s[:, m0:], masked_score)
            s = jnp.concatenate([s[:, :m0], tail], axis=1) if m0 else tail
            top = jnp.max(s, axis=1, keepdims=True)
            p = jnp.exp2(s - top).astype(BF)
            sums = dot(p, b.ext[2, h, :n])
            outs.append(sums / pltpu.roll(sums, HEAD_DIM, 1))
            log_total = top + jnp.log2(sums)
            b.ext[0, h, pl.ds(r0, size)] = with_feats(q.astype(F32), lane, h, -log_total).astype(BF)
        both = jnp.where(lane < HEAD_DIM, outs[0], outs[1])
        b.o_ref[of_block, pl.ds(half * size, size)] = both
        b.o_low[of_block, pl.ds(half * size, size)] = both.astype(BF)

    def o_copy(of_block, half):
        at = pl.ds(half * (block // 2), half_rows[half])
        return remote(b.o_low.at[of_block, at], b.att.at[w.seq, at], b.sem_o[0].at[of_block, half],
                      b.sem_o[1].at[w.seq, half], (of_block, w.batch))

    pending = [(a, i) for i in range(4) for a in (PROJ, UP, DOWN, POOL)]
    after = {1: 2, 2: 2, 3: 2, 4: 2, 5: 3, 6: 3}
    for of_block in range(count):
        for half in range(2):
            attend(of_block, half)

            @pl.when(w.seq != of_block)
            def _(of_block=of_block, half=half):
                o_copy(of_block, half).start()

            for _ in range(after.get(of_block * 2 + half, 0)):
                gather.step(*pending.pop(0))

        @pl.when(w.seq == of_block)
        def _(of_block=of_block):
            b.att[of_block] = b.o_low[of_block, 0:rows]

    for a, index in pending:
        gather.step(a, index)

    proj = b.fulls[PROJ][...].reshape(D, D)
    pool = b.fulls[POOL][...].reshape(3 * D, D)
    first, last = w.seq == 0, w.seq == count - 1

    def lay(ref, start, value):
        for n in range(tiles):
            ref[n, pl.ds(start, value.shape[0])] = value[:, n * WIDE : (n + 1) * WIDE]

    def whole(ref, start):
        return jnp.concatenate([ref[n, pl.ds(start, rows)] for n in range(tiles)], axis=1)

    def add(ref, value):
        for n in range(tiles):
            ref[n, pl.ds(0, rows)] += value[:, n * WIDE : (n + 1) * WIDE]

    sum_one, sum_two, h_two = b.buf
    g_low = out_grad[...]
    spread = dot(g_low, pool, NT)
    for k in range(3):
        for n in range(tiles):
            at = k * D + n * WIDE
            b.dh_two[n, pl.ds(6 + k, pools, stride=3)] = spread[:, at : at + WIDE]
    arrive(grad_edge)
    beyond = jnp.where(last, 0.0, dot(b.edge[1], pool, NT))
    lay(b.dh_two, 8 + rows - 2, beyond[0:1, 0:D])
    lay(b.dh_two, 8 + rows - 1, beyond[0:1, D : 2 * D])
    b.d_branch[...] = whole(b.dh_two, 8).astype(BF)
    small_grad = b.small_grad
    small_grad[...] = jnp.zeros(small_grad.shape, F32)
    small_grad[4:5] = jnp.sum(b.d_branch[...].astype(F32), axis=0, keepdims=True)
    small_grad[5:6] = jnp.sum(g_low.astype(F32), axis=0, keepdims=True)
    sum_one[...] = jnp.zeros(sum_one.shape, F32)
    sum_two[...] = jnp.zeros(sum_two.shape, F32)

    for k in range(1, count):
        of = w.seq_at(k)
        for half in range(2):
            at = pl.ds(half * (block // 2), half_rows[half])
            remote(b.att.at[of, at], b.att.at[of, at], b.sem_o[0].at[of, half],
                   b.sem_o[1].at[of, half], (of, w.batch)).wait_recv()
    attended = jnp.concatenate([b.att[n] for n in range(count)], axis=1)
    b.h_one[...] = tokens[...].astype(F32) + dot(attended, proj)
    unit, _ = norm_stats(b.h_one[...])
    b.normed_two[...] = (unit * small[2:3] + small[3:4]).astype(BF)
    links.finish()
    for of_block in range(count):
        for half in range(2):

            @pl.when(w.seq != of_block)
            def _(of_block=of_block, half=half):
                o_copy(of_block, half).wait_send()

    for peer in w.seq_peers():
        pl.semaphore_signal(b.free, inc=1, device_id=peer, device_id_type=MESH)
    part = b.act.shape[1] // count

    def feed(n, _):
        cols = pl.ds(pl.multiple_of(n * part, part), part)
        up = b.fulls[UP][:, :, :, :, :, cols].reshape(D, part)
        down = b.fulls[DOWN][lax.div(n, 2), lax.rem(n, 2)].reshape(part, D)
        hidden = dot(b.normed_two[...], up) + small[pl.ds(6 + n, 1)]
        square = hidden * hidden
        bend = jnp.tanh(GELU_C * hidden * (1.0 + 0.044715 * square))
        half = 0.5 * (1.0 + bend)
        act_low = (hidden * half).astype(BF)
        b.act[:, cols] = act_low
        slope = half + 0.5 * hidden * (1.0 - bend * bend) * (
            GELU_C * (1.0 + 3 * 0.044715 * square)
        )
        add(sum_one, dot(act_low, down))
        d_low = (dot(b.d_branch[...], down, NT) * slope).astype(BF)
        b.d_hidden[:, cols] = d_low
        small_grad[pl.ds(6 + n, 1)] = jnp.sum(d_low.astype(F32), axis=0, keepdims=True)
        add(sum_two, dot(d_low, up, NT))
        return 0

    lax.fori_loop(0, count, feed, 0)
    h_low = (b.h_one[...] + whole(sum_one, 0) + small[4:5]).astype(BF)
    lay(h_two, 8, h_low.astype(F32))
    b.edge[2] = h_low[rows - 16 :]
    row_edge = links.start([
        remote(b.edge.at[2], b.edge.at[3], b.sem_edge[0].at[1], b.sem_edge[1].at[1],
               (w.seq_at(1), w.batch))
    ])
    unit, scale = norm_stats(b.h_one[...])
    back, small_grad[2:3], small_grad[3:4] = norm_back(whole(sum_two, 0), unit, scale, small[2:3])
    grad_one = whole(b.dh_two, 8) + back
    b.h_one[...] = grad_one
    b.d_attn[...] = grad_one.astype(BF)
    spread_back = dot(b.d_attn[...], proj, NT).astype(BF)
    for n in range(count):
        b.do_send[n] = spread_back[:, n * WIDE : (n + 1) * WIDE]
    do_all = b.o_low
    pl.semaphore_wait(b.free, count - 1)
    given = links.start([
        remote(b.do_send.at[w.seq_at(k + 1)], do_all.at[w.seq, 0:rows], b.sem_do[0].at[k],
               b.sem_do[1].at[k], peer)
        for k, peer in enumerate(w.seq_peers())
    ])
    do_all[w.seq, 0:rows] = b.do_send[w.seq]
    arrive(row_edge)
    before = jnp.where(first, 0.0, b.edge[3].astype(F32))
    lay(h_two, 0, before[8:16])
    for k in range(3):
        for n in range(tiles):
            at = k * D + n * WIDE
            b.grouped[:, at : at + WIDE] = h_two[n, pl.ds(6 + k, pools, stride=3)].astype(BF)
    short_out[...] = (dot(b.grouped[...], pool) + small[5:6]).astype(BF)

    pl.semaphore_signal(b.ready, inc=1, device_id=w.partner("c"), device_id_type=MESH)
    pl.semaphore_wait(b.ready, 1)
    scatter = Scatter(w, links, b.fulls, b.acc, b.two_out, b.two_in, b.three_out, b.three_in,
                      b.z_out, b.z_in, *b.sem_scatter)

    def columns(ref):
        width = ref.shape[1] // count
        return lambda n: ref[:, pl.ds(pl.multiple_of(n * width, WIDE), width)]

    of_act, of_grouped, of_normed = columns(b.act), columns(b.grouped), columns(b.normed_two)
    scatter.begin(DOWN, lambda n: dot(of_act(n), b.d_branch[...], TN))
    scatter.begin(UP, lambda n: dot(of_normed(n), b.d_hidden[...], TN))
    scatter.step_two(DOWN)
    scatter.begin(POOL, lambda n: dot(of_grouped(n), g_low, TN))
    scatter.step_two(UP)
    scatter.begin(PROJ, lambda n: dot(b.att[n], b.d_attn[...], TN))
    scatter.step_two(POOL)
    scatter.step_two(PROJ)

    def prepare(of_block):
        def body(n, _):
            r0 = pl.multiple_of(n * sub, 16)
            lane = lax.broadcasted_iota(jnp.int32, (sub, WIDE), 1)
            grad = do_all[of_block, pl.ds(r0, sub)].astype(F32)
            terms = grad * b.o_ref[of_block, pl.ds(r0, sub)]
            at = pl.ds(pl.multiple_of(of_block * block + r0, 16), sub)
            for h in range(HEADS):
                mine = in_head(lane, h)
                delta = jnp.sum(jnp.where(mine, terms, 0.0), axis=1, keepdims=True)
                base = jnp.where(mine, grad, 0.0)
                b.do_ext[h, at] = with_feats(base, lane, h, -delta).astype(BF)
            return 0

        lax.fori_loop(0, 3, body, 0)

    arrive(given)
    for n in range(count):
        prepare(n)
    dq, dk, dv = b.buf
    for ref in b.buf:
        ref[...] = jnp.zeros(ref.shape, F32)
    b.g_qkv[...] = jnp.zeros(b.g_qkv.shape, F32)

    def pair(q_block, k_block, on_diagonal):
        at_q = pl.ds(pl.multiple_of(q_block * block, WIDE), block)
        at_k = pl.ds(pl.multiple_of(k_block * block, WIDE), block)
        found = []
        for h in range(HEADS):
            q, k, v = b.ext[0, h, at_q], b.ext[1, h, at_k], b.ext[2, h, at_k]
            grad = b.do_ext[h, at_q]
            p = jnp.exp2(dot(k, q, NT))
            if on_diagonal:
                keys = lax.broadcasted_iota(jnp.int32, (block, block), 0)
                queries = lax.broadcasted_iota(jnp.int32, (block, block), 1)
                p = jnp.where(keys <= queries, p, 0.0)
            ds = (p * dot(v, grad, NT)).astype(BF)
            found.append((dot(ds, k, TN), dot(ds, q), dot(p.astype(BF), grad)))
        lane = lax.broadcasted_iota(jnp.int32, (block, WIDE), 1)
        for ref, at, zero, one in zip((dq, dk, dv), (q_block, k_block, k_block), *found):
            ref[at] += jnp.where(lane < HEAD_DIM, zero, one)

    backs = (HEAD_DIM ** -0.5, 1.0 / LOG2E, 1.0)

    def dn_copy(turn_of):
        n = turn_of // 2
        return remote(b.tok_all.at[n], b.tok_all.at[2 + n], b.sem_dn[0].at[n], b.sem_dn[1].at[n],
                      w.partner("c"))

    def complete(turn_of, of_block):
        def body(n, _):
            r0 = pl.multiple_of(n * sub, 16)
            cosine, sine = turning(of_block, r0)
            for m, ref in enumerate(b.buf):
                value = ref[of_block, pl.ds(r0, sub)] * backs[m]
                if m < 2:
                    value = value * cosine - swap_halves(value) * sine
                b.stacked[pl.ds(r0, sub), m * WIDE : (m + 1) * WIDE] = value.astype(BF)
            return 0

        lax.fori_loop(0, 3, body, 0)
        weight = jnp.concatenate([qkv_weight(n) for n in range(3)], axis=1)
        b.g_qkv[...] += dot(b.normed[of_block], b.stacked[...], TN)
        back = dot(b.stacked[...], weight, NT)
        keeps = lax.rem(of_block, 2) == w.c

        @pl.when(keeps)
        def _():
            lay(b.dh_two, 0, back)

        @pl.when(jnp.logical_not(keeps))
        def _():
            b.tok_all[turn_of // 2] = back.astype(BF)
            dn_copy(turn_of).start()

    def summed(turn_of):
        dn_copy(turn_of).wait_recv()
        return whole(b.dh_two, 0) + b.tok_all[2 + turn_of // 2].astype(F32)

    down_first = w.x == 0
    x_copy = []
    for turn_of in range(count):
        outer = jnp.where(down_first, count - 1 - turn_of, turn_of)
        pair(outer, outer, True)

        def inner(n, _, outer=outer, turn_of=turn_of):
            other = jnp.where(down_first, n, turn_of + 1 + n)
            pair(jnp.where(down_first, outer, other), jnp.where(down_first, other, outer), False)
            return 0

        if turn_of < count - 1:
            lax.fori_loop(0, count - 1 - turn_of, inner, 0)
        complete(turn_of, outer)
        if turn_of == 0:
            scatter.step_three(DOWN)
            scatter.step_three(UP)
        elif turn_of == 1:
            b.d_attn[...] = summed(turn_of).astype(BF)
            x_copy = links.start([
                remote(b.d_attn, b.x_in, b.sem_x[0].at[0], b.sem_x[1].at[0], w.partner("x"))
            ])
            scatter.step_three(POOL)
            scatter.step_three(PROJ)
            scatter.step_four(DOWN)
        elif turn_of == 2:
            scatter.step_four(UP)

    for n in range(batches):
        z_of, y_of = n // ny, n % ny
        rows_of = b.g_qkv[...].reshape(count, nz, ny, -1, 3 * WIDE)[:, z_of, y_of]
        b.gq_out[n] = rows_of.astype(BF)
    gq = links.start([
        remote(b.gq_out.at[w.batch_at(k + 1)], b.gq_in.at[w.batch], b.sem_gq[0].at[k],
               b.sem_gq[1].at[k], peer)
        for k, peer in enumerate(w.batch_peers())
    ])
    b.gq_in[w.batch] = b.gq_out[w.batch]

    grad_normed = summed(count - 1)
    arrive(x_copy)
    grad_normed = grad_normed + b.x_in[...].astype(F32)
    unit, scale = norm_stats(tokens[...].astype(F32))
    back, small_grad[0:1], small_grad[1:2] = norm_back(grad_normed, unit, scale, small[0:1])
    input_grad[...] = b.h_one[...] + back
    b.sg_seq[w.seq] = small_grad[...]
    sg = links.start([
        remote(b.sg_seq.at[w.seq], b.sg_seq.at[w.seq], b.sem_sg_seq[0].at[k],
               b.sem_sg_seq[1].at[k], peer)
        for k, peer in enumerate(w.seq_peers())
    ])
    arrive(gq)
    total = b.gq_in[0].astype(F32)
    for n in range(1, batches):
        total = total + b.gq_in[n].astype(F32)
    b.gq_seq[...] = total.astype(BF)
    gq = links.start([
        remote(b.gq_seq.at[w.seq_at(k + 1)], b.gq_got.at[w.seq], b.sem_gq_seq[0].at[k],
               b.sem_gq_seq[1].at[k], peer)
        for k, peer in enumerate(w.seq_peers())
    ])
    b.gq_got[w.seq] = b.gq_seq[w.seq]
    arrive(sg)
    total = b.sg_seq[0]
    for n in range(1, count):
        total = total + b.sg_seq[n]
    b.sg_all[w.batch] = total
    sg = links.start([
        remote(b.sg_all.at[w.batch], b.sg_all.at[w.batch], b.sem_sg_all[0].at[k],
               b.sem_sg_all[1].at[k], peer)
        for k, peer in enumerate(w.batch_peers())
    ])
    scatter.step_four(POOL)
    scatter.step_four(PROJ)

    squares = jnp.zeros((8, WIDE), F32)

    def gather_squares(squares, total):
        flat = jnp.sum((total * total).reshape(-1, 8, total.shape[-1]), axis=0)
        for n in range(flat.shape[1] // WIDE):
            squares = squares + flat[:, n * WIDE : (n + 1) * WIDE]
        return squares

    totals = (total_proj, total_up, total_down, total_pool)
    for a in (DOWN, UP, POOL, PROJ):
        total = scatter.last(a)
        totals[a][...] = total
        squares = gather_squares(squares, total)
    arrive(gq)
    for n in range(3):
        total = jnp.concatenate(
            [b.gq_got[m, :, n * WIDE : (n + 1) * WIDE].astype(F32) for m in range(count)], axis=1
        )
        total_qkv[n] = total
        squares = gather_squares(squares, total)
    b.norm_seq[w.seq] = squares
    norm = links.start([
        remote(b.norm_seq.at[w.seq], b.norm_seq.at[w.seq], b.sem_norm_seq[0].at[k],
               b.sem_norm_seq[1].at[k], peer)
        for k, peer in enumerate(w.seq_peers())
    ])
    arrive(sg)
    total = b.sg_all[0]
    for n in range(1, batches):
        total = total + b.sg_all[n]
    small_total[...] = total
    small_squares = gather_squares(jnp.zeros((8, WIDE), F32), total)
    arrive(norm)
    squares = b.norm_seq[0]
    for n in range(1, count):
        squares = squares + b.norm_seq[n]
    b.norm_all[w.batch] = squares
    norm = links.start([
        remote(b.norm_all.at[w.batch], b.norm_all.at[w.batch], b.sem_norm_all[0].at[k],
               b.sem_norm_all[1].at[k], peer)
        for k, peer in enumerate(w.batch_peers())
    ])
    arrive(norm)
    squares = b.norm_all[0]
    for n in range(1, batches):
        squares = squares + b.norm_all[n]
    squares = squares + small_squares
    square = jnp.sum(jnp.sum(squares, axis=1, keepdims=True), axis=0, keepdims=True)
    norm_out[...] = jnp.broadcast_to(jnp.sqrt(square), norm_out.shape)
    for turn_of in (1, 3):
        dn_copy(turn_of).wait_send()
    links.finish()


def step_kernel(norm_in, grad_in, short_in, *refs):
    states = refs[: 4 * 6]
    outs = refs[4 * 6 :]
    grad_out, short_out, norm_out = outs[:3]
    grad_out[...] = grad_in[...]
    short_out[...] = short_in[...]
    grad_norm = norm_in[0:1, 0:1]
    norm_out[...] = grad_norm
    clip = clip_norm / jnp.maximum(grad_norm, clip_norm)
    for a in range(6):
        total, weight, one, two = states[4 * a : 4 * a + 4]
        limit = clip.reshape((1,) * len(total.shape))
        rate, decay = (rate_vector, 0.0) if a == 5 else (rate_matrix, decay_weight)
        results = adam_update(total[...], one[...], two[...], weight[...], limit, rate, decay)
        for ref, value in zip(outs[3 + 3 * a : 6 + 3 * a], results):
            ref[...] = value


def rotary_tables(rows, count):
    half = HEAD_DIM // 2
    frequency = np.exp(-math.log(10000.0) * np.arange(half) / half)
    lanes = np.tile(frequency, WIDE // half)
    sign = np.tile(np.repeat([-1.0, 1.0], half), WIDE // HEAD_DIM)
    inside = np.arange(rows)[:, None] * lanes
    starts = (np.arange(8) * (np.arange(8) < count) * rows)[:, None] * lanes
    pack = lambda angle: np.stack([np.cos(angle), np.sin(angle) * sign]).astype(np.float32)
    return pack(inside), pack(starts)


def fast_local(mesh):
    nx, nz, ny = grid_of(mesh)
    count = 2 * nx
    in_vmem = pl.BlockSpec(memory_space=pltpu.VMEM)

    def call(kernel, outs, scratch, args, **params):
        return pl.pallas_call(
            kernel,
            out_shape=[jax.ShapeDtypeStruct(s, t) for s, t in outs],
            in_specs=[in_vmem] * len(args),
            out_specs=[in_vmem] * len(outs),
            scratch_shapes=scratch,
            compiler_params=pltpu.CompilerParams(vmem_limit_bytes=VMEM_LIMIT, **params),
        )(*args)

    def body(tokens, doc_ids, out_grad,
             qkv_weight, qkv_first, qkv_second,
             proj_weight, proj_first, proj_second,
             up_weight, up_first, up_second,
             down_weight, down_first, down_second,
             pool_weight, pool_first, pool_second,
             small_weight, small_first, small_second):
        rows = tokens.shape[1]
        pools = out_grad.shape[1]
        ff = up_weight.shape[1]
        shard = lax.axis_index("seq") * (nz * ny) + lax.axis_index("batch")
        own = small_weight.shape[0]
        placed = lax.dynamic_update_slice(
            jnp.zeros((16 * D,), BF), small_weight.astype(BF), (shard * own,)
        ).reshape(16, D)
        turn, offset = rotary_tables(rows, count)
        weights = (qkv_weight, proj_weight, up_weight, down_weight, pool_weight)
        shapes = [v.shape for v in weights]
        template = layer_buffers(nx, nz, ny, rows, ff, shapes[1:])
        scratch = jax.tree.leaves(list(template.values()))
        outs = [((pools, D), BF), ((rows, D), F32)] + [(s, F32) for s in shapes]
        outs += [((16, D), F32), ((8, WIDE), F32)]
        short, grad_in, *totals, small_total, norm = call(
            lambda *r: layer_kernel(nx, nz, ny, template, *r), outs, scratch,
            (tokens[0], doc_ids, out_grad[0], *weights, placed, turn, offset),
            collective_id=0, has_side_effects=True)
        small_part = lax.dynamic_slice(small_total.reshape(-1), (shard * own,), (own,))
        totals = (*totals, small_part)
        weights = (*weights, small_weight)
        firsts = (qkv_first, proj_first, up_first, down_first, pool_first, small_first)
        seconds = (qkv_second, proj_second, up_second, down_second, pool_second, small_second)
        groups = [list(group) for group in zip(totals, weights, firsts, seconds)]
        groups[5] = [v.reshape(1, own) for v in groups[5]]
        outs = [((rows, D), F32), ((pools, D), BF), ((1, 1), F32)]
        outs += [(v[0].shape, F32) for v in groups for _ in range(3)]
        grad_out, short_out, norm_out, *states = call(
            step_kernel, outs, [],
            (norm, grad_in, short, *[v for group in groups for v in group]))
        states[15:] = [v.reshape(own) for v in states[15:]]
        return (short_out[None], grad_out[None], norm_out.reshape(()), *states)

    return body


def solution(mesh):
    in_specs = (
        P("batch", "seq", None),
        P("batch", None),
        P("batch", "seq", None),
        P(None, ("seq", "batch"), None),
        P(None, ("seq", "batch"), None),
        P(None, ("seq", "batch"), None),
        P(("seq", "batch"), None),
        P(("seq", "batch"), None),
        P(("seq", "batch"), None),
        P(("seq", "batch"), None),
        P(("seq", "batch"), None),
        P(("seq", "batch"), None),
        P(("seq", "batch"), None),
        P(("seq", "batch"), None),
        P(("seq", "batch"), None),
        P(("seq", "batch"), None),
        P(("seq", "batch"), None),
        P(("seq", "batch"), None),
        P(("seq", "batch")),
        P(("seq", "batch")),
        P(("seq", "batch")),
    )
    out_specs = (
        P("batch", "seq", None),
        P("batch", "seq", None),
        P(),
        P(None, ("seq", "batch"), None),
        P(None, ("seq", "batch"), None),
        P(None, ("seq", "batch"), None),
        P(("seq", "batch"), None),
        P(("seq", "batch"), None),
        P(("seq", "batch"), None),
        P(("seq", "batch"), None),
        P(("seq", "batch"), None),
        P(("seq", "batch"), None),
        P(("seq", "batch"), None),
        P(("seq", "batch"), None),
        P(("seq", "batch"), None),
        P(("seq", "batch"), None),
        P(("seq", "batch"), None),
        P(("seq", "batch"), None),
        P(("seq", "batch")),
        P(("seq", "batch")),
        P(("seq", "batch")),
    )
    body = fast_local(mesh) if fits(mesh) else local
    return jax.shard_map(body, mesh=mesh, in_specs=in_specs, out_specs=out_specs, check_vma=False)
```

```python
import math

import jax
import jax.numpy as jnp
import numpy as np
from jax import lax
from jax.experimental import pallas as pl
from jax.experimental.pallas import tpu as pltpu
from jax.sharding import PartitionSpec as P

D = 512
HEAD_DIM = 64
STEP = 10


beta_one = 0.9
beta_two = 0.999
adam_eps = 1e-08
norm_eps = 1e-05
clip_norm = 1.0
rate_matrix = 0.05
rate_vector = 0.5
decay_weight = 0.1
masked_score = -1e30


def from_behind(block, axis, distance):
    devices = range(lax.axis_size(axis))
    route = [(i - distance, i) for i in devices if i - distance in devices]
    return lax.ppermute(block, axis, route)


def layer_norm(values, scale_gain, shift_vec):
    center = values - jnp.mean(values, axis=-1, keepdims=True)
    spread = jnp.mean(center * center, axis=-1, keepdims=True)
    return center * lax.rsqrt(spread + norm_eps) * scale_gain + shift_vec


def rotate(values, positions):
    half_dim = HEAD_DIM // 2
    head_view = values.reshape(values.shape[0], values.shape[1] // HEAD_DIM, HEAD_DIM)
    frequency = jnp.exp(-math.log(10000.0) * jnp.arange(half_dim, dtype=jnp.float32) / half_dim)
    angles = positions.astype(jnp.float32)[:, None] * frequency[None, :]
    cosine = jnp.cos(angles)[:, None, :]
    sine_part = jnp.sin(angles)[:, None, :]
    first_half = head_view[..., :half_dim]
    second_half = head_view[..., half_dim:]
    turned = jnp.concatenate(
        [
            first_half * cosine - second_half * sine_part,
            second_half * cosine + first_half * sine_part,
        ],
        axis=-1,
    )
    return turned.reshape(values.shape)


def outer_sum(left_side, right_side):
    return lax.dot_general(
        left_side, right_side, (((0,), (0,)), ((), ())), preferred_element_type=jnp.float32
    )


def times_transpose(left_side, right_side):
    return lax.dot_general(
        left_side, right_side, (((1,), (1,)), ((), ())), preferred_element_type=jnp.float32
    )


def split_heads(values):
    return values.reshape(values.shape[0], values.shape[1] // HEAD_DIM, HEAD_DIM)


def block_scores(query_heads, key_heads, query_pos, key_pos, query_doc, key_doc):
    raw_scores = jnp.einsum(
        "qhd,khd->hqk", query_heads, key_heads, preferred_element_type=jnp.float32
    ) * HEAD_DIM ** (-0.5)
    allowed = (key_pos[None, :] <= query_pos[:, None]) & (key_doc[None, :] == query_doc[:, None])
    return jnp.where(allowed[None], raw_scores, masked_score)


def adam_update(gradient, first_moment, second_moment, weight, clip_scale, step_rate, decay_rate):
    clipped = gradient * clip_scale
    first_new = beta_one * first_moment + (1.0 - beta_one) * clipped
    second_new = beta_two * second_moment + (1.0 - beta_two) * clipped * clipped
    first_hat = first_new / (1.0 - beta_one**STEP)
    second_hat = second_new / (1.0 - beta_two**STEP)
    weight_new = weight - step_rate * (
        first_hat / (jnp.sqrt(second_hat) + adam_eps) + decay_rate * weight
    )
    return (first_new, second_new, weight_new)


def local(
    tokens,
    doc_ids,
    out_grad,
    qkv_weight,
    qkv_first,
    qkv_second,
    proj_weight,
    proj_first,
    proj_second,
    up_weight,
    up_first,
    up_second,
    down_weight,
    down_first,
    down_second,
    pool_weight,
    pool_first,
    pool_second,
    small_weight,
    small_first,
    small_second,
):
    block_rows = tokens.shape[1]
    model_width = tokens.shape[2]
    seq_count = lax.axis_size("seq")
    my_block = lax.axis_index("seq")
    whole_qkv, whole_proj, whole_up, whole_down, whole_pool, whole_small = (
        lax.all_gather(qkv_weight.astype(jnp.bfloat16), ("seq", "batch"), axis=1, tiled=True),
        lax.all_gather(proj_weight.astype(jnp.bfloat16), ("seq", "batch"), axis=0, tiled=True),
        lax.all_gather(up_weight.astype(jnp.bfloat16), ("seq", "batch"), axis=0, tiled=True),
        lax.all_gather(down_weight.astype(jnp.bfloat16), ("seq", "batch"), axis=0, tiled=True),
        lax.all_gather(pool_weight.astype(jnp.bfloat16), ("seq", "batch"), axis=0, tiled=True),
        lax.all_gather(small_weight.astype(jnp.bfloat16), ("seq", "batch"), axis=0, tiled=True),
    )
    small_used = whole_small.astype(jnp.float32)
    gain_first = small_used[0:D]
    shift_first = small_used[D : 2 * D]
    gain_second = small_used[2 * D : 3 * D]
    shift_second = small_used[3 * D : 4 * D]
    bias_down = small_used[4 * D : 5 * D]
    bias_pool = small_used[5 * D : 6 * D]
    bias_up = small_used[6 * D :]
    inputs = tokens[0].astype(jnp.float32)
    doc_row = doc_ids[0]
    first_row = my_block * block_rows
    positions = first_row + jnp.arange(block_rows, dtype=jnp.int32)
    doc_mine = lax.dynamic_slice_in_dim(doc_row, first_row, block_rows)
    normed, first_pull = jax.vjp(layer_norm, inputs, gain_first, shift_first)
    normed_low = normed.astype(jnp.bfloat16)
    projected = jnp.einsum("td,cde->cte", normed_low, whole_qkv, preferred_element_type=jnp.float32)
    queries_rot, query_pull = jax.vjp(lambda values: rotate(values, positions), projected[0])
    keys_rot, key_pull = jax.vjp(lambda values: rotate(values, positions), projected[1])
    query_low = queries_rot.astype(jnp.bfloat16)
    key_low = keys_rot.astype(jnp.bfloat16)
    value_low = projected[2].astype(jnp.bfloat16)
    keys_all, values_all = (
        lax.all_gather(key_low, "seq", axis=0, tiled=True),
        lax.all_gather(value_low, "seq", axis=0, tiled=True),
    )
    query_heads = split_heads(query_low)
    head_count = query_heads.shape[1]
    zeros_head_rows = jnp.zeros((head_count, block_rows), jnp.float32)
    zeros_heads = jnp.zeros((block_rows, head_count, HEAD_DIM), jnp.float32)

    def scores_of(number):
        start_row = number * block_rows
        key_heads = split_heads(keys_all[start_row : start_row + block_rows])
        value_heads = split_heads(values_all[start_row : start_row + block_rows])
        key_pos = start_row + jnp.arange(block_rows, dtype=jnp.int32)
        key_doc = doc_row[start_row : start_row + block_rows]
        scores = block_scores(query_heads, key_heads, positions, key_pos, doc_mine, key_doc)
        return (scores, key_heads, value_heads)

    running_max = jnp.full((head_count, block_rows), masked_score, jnp.float32)
    running_sum = zeros_head_rows
    for number in range(seq_count):

        def block_stats(number=number):
            scores = scores_of(number)[0]
            block_max = jnp.max(scores, axis=-1)
            return (block_max, jnp.sum(jnp.exp(scores - block_max[..., None]), axis=-1))

        block_max, block_sum = block_stats()
        new_max = jnp.maximum(running_max, block_max)
        running_sum = running_sum * jnp.exp(running_max - new_max) + block_sum * jnp.exp(
            block_max - new_max
        )
        running_max = new_max
    log_total = running_max + jnp.log(running_sum)
    attended = zeros_heads
    for number in range(seq_count):

        def block_output(number=number):
            scores, key_heads, value_heads = scores_of(number)
            soft_probs = jnp.exp(scores - log_total[..., None]).astype(jnp.bfloat16)
            return jnp.einsum(
                "hqk,khd->qhd", soft_probs, value_heads, preferred_element_type=jnp.float32
            )

        attended = attended + block_output()
    attended_low = attended.reshape(block_rows, model_width).astype(jnp.bfloat16)
    h_one = inputs + jnp.dot(attended_low, whole_proj, preferred_element_type=jnp.float32)
    normed_two, second_pull = jax.vjp(layer_norm, h_one, gain_second, shift_second)
    normed_two_low = normed_two.astype(jnp.bfloat16)
    hidden_pre = jnp.dot(normed_two_low, whole_up, preferred_element_type=jnp.float32) + bias_up
    activated, gelu_pull = jax.vjp(jax.nn.gelu, hidden_pre)
    act_low = activated.astype(jnp.bfloat16)
    h_two = h_one + jnp.dot(act_low, whole_down, preferred_element_type=jnp.float32) + bias_down
    h_two_low = h_two.astype(jnp.bfloat16)
    prev_rows = from_behind(h_two_low[block_rows - 2 :], "seq", 1)
    shifted = jnp.concatenate([prev_rows, h_two_low[: block_rows - 2]], axis=0)
    grouped = shifted.reshape(block_rows // 3, 3 * model_width)
    short_rows = (
        jnp.dot(grouped, whole_pool, preferred_element_type=jnp.float32) + bias_pool
    ).astype(jnp.bfloat16)
    out_rows = out_grad[0]
    grad_pool = outer_sum(grouped, out_rows)
    grad_bias_pool = jnp.sum(out_rows.astype(jnp.float32), axis=0)
    spread_rows = times_transpose(out_rows, whole_pool).reshape(block_rows, model_width)
    returned = from_behind(spread_rows[:2], "seq", -1)
    grad_h_two = jnp.concatenate([spread_rows[2:], returned], axis=0)
    grad_branch = grad_h_two.astype(jnp.bfloat16)
    grad_down = outer_sum(act_low, grad_branch)
    grad_bias_down = jnp.sum(grad_branch.astype(jnp.float32), axis=0)
    grad_act = times_transpose(grad_branch, whole_down)
    grad_hidden = gelu_pull(grad_act)[0].astype(jnp.bfloat16)
    grad_up = outer_sum(normed_two_low, grad_hidden)
    grad_bias_up = jnp.sum(grad_hidden.astype(jnp.float32), axis=0)
    grad_normed_two = times_transpose(grad_hidden, whole_up)
    back_h_one, grad_gain_second, grad_shift_second = second_pull(grad_normed_two)
    grad_h_one = grad_h_two + back_h_one
    grad_attn = grad_h_one.astype(jnp.bfloat16)
    grad_proj = outer_sum(attended_low, grad_attn)
    grad_attended = times_transpose(grad_attn, whole_proj).astype(jnp.bfloat16)
    grad_heads = split_heads(grad_attended)
    row_delta = zeros_head_rows
    value_terms = []
    for number in range(seq_count):

        def block_first(number=number):
            scores, key_heads, value_heads = scores_of(number)
            soft_probs = jnp.exp(scores - log_total[..., None])
            grad_probs = jnp.einsum(
                "qhd,khd->hqk", grad_heads, value_heads, preferred_element_type=jnp.float32
            )
            part_delta = jnp.sum(soft_probs * grad_probs, axis=-1)
            value_grad = jnp.einsum(
                "hqk,qhd->khd",
                soft_probs.astype(jnp.bfloat16),
                grad_heads,
                preferred_element_type=jnp.float32,
            )
            return (part_delta, value_grad.reshape(block_rows, model_width))

        part_delta, value_grad = block_first()
        row_delta = row_delta + part_delta
        value_terms.append(value_grad)
    grad_query = zeros_heads
    key_terms = []
    for number in range(seq_count):

        def block_second(number=number):
            scores, key_heads, value_heads = scores_of(number)
            soft_probs = jnp.exp(scores - log_total[..., None])
            grad_probs = jnp.einsum(
                "qhd,khd->hqk", grad_heads, value_heads, preferred_element_type=jnp.float32
            )
            grad_scores = (soft_probs * (grad_probs - row_delta[..., None])).astype(jnp.bfloat16)
            query_part = jnp.einsum(
                "hqk,khd->qhd", grad_scores, key_heads, preferred_element_type=jnp.float32
            )
            key_part = jnp.einsum(
                "hqk,qhd->khd", grad_scores, query_heads, preferred_element_type=jnp.float32
            )
            return (query_part, key_part.reshape(block_rows, model_width))

        query_part, key_part = block_second()
        grad_query = grad_query + query_part
        key_terms.append(key_part)
    head_scale = HEAD_DIM ** (-0.5)
    grad_keys, grad_values = (
        lax.psum_scatter(
            (jnp.concatenate(key_terms, axis=0) * head_scale).astype(jnp.bfloat16),
            "seq",
            scatter_dimension=0,
            tiled=True,
        ).astype(jnp.float32),
        lax.psum_scatter(
            jnp.concatenate(value_terms, axis=0).astype(jnp.bfloat16),
            "seq",
            scatter_dimension=0,
            tiled=True,
        ).astype(jnp.float32),
    )
    grad_q_pre = query_pull(grad_query.reshape(block_rows, model_width) * head_scale)[0].astype(
        jnp.bfloat16
    )
    grad_k_pre = key_pull(grad_keys)[0].astype(jnp.bfloat16)
    grad_v_pre = grad_values.astype(jnp.bfloat16)
    stacked = jnp.stack([grad_q_pre, grad_k_pre, grad_v_pre])
    grad_qkv = jnp.einsum("td,cte->cde", normed_low, stacked, preferred_element_type=jnp.float32)
    grad_normed = jnp.einsum("cte,cde->td", stacked, whole_qkv, preferred_element_type=jnp.float32)
    back_inputs, grad_gain_first, grad_shift_first = first_pull(grad_normed)
    input_grad = (grad_h_one + back_inputs)[None]
    grad_small = jnp.concatenate(
        [
            grad_gain_first,
            grad_shift_first,
            grad_gain_second,
            grad_shift_second,
            grad_bias_down,
            grad_bias_pool,
            grad_bias_up,
        ]
    )
    all_grads = (grad_qkv, grad_proj, grad_up, grad_down, grad_pool, grad_small)
    shards = (
        lax.psum_scatter(all_grads[0], ("seq", "batch"), scatter_dimension=1, tiled=True),
        lax.psum_scatter(all_grads[1], ("seq", "batch"), scatter_dimension=0, tiled=True),
        lax.psum_scatter(all_grads[2], ("seq", "batch"), scatter_dimension=0, tiled=True),
        lax.psum_scatter(all_grads[3], ("seq", "batch"), scatter_dimension=0, tiled=True),
        lax.psum_scatter(all_grads[4], ("seq", "batch"), scatter_dimension=0, tiled=True),
        lax.psum_scatter(all_grads[5], ("seq", "batch"), scatter_dimension=0, tiled=True),
    )
    local_squares = sum((jnp.sum(portion * portion) for portion in shards))
    grad_norm = jnp.sqrt(lax.psum(local_squares, ("seq", "batch")))
    clip_scale = clip_norm / jnp.maximum(grad_norm, clip_norm)
    masters = (qkv_weight, proj_weight, up_weight, down_weight, pool_weight, small_weight)
    firsts = (qkv_first, proj_first, up_first, down_first, pool_first, small_first)
    seconds = (qkv_second, proj_second, up_second, down_second, pool_second, small_second)
    new_states = []
    for index_kind in range(6):
        step_rate = rate_vector if index_kind == 5 else rate_matrix
        decay_rate = 0.0 if index_kind == 5 else decay_weight
        new_states.append(
            adam_update(
                shards[index_kind],
                firsts[index_kind],
                seconds[index_kind],
                masters[index_kind],
                clip_scale,
                step_rate,
                decay_rate,
            )
        )
    return (
        short_rows[None],
        input_grad,
        grad_norm,
        new_states[0][0],
        new_states[0][1],
        new_states[0][2],
        new_states[1][0],
        new_states[1][1],
        new_states[1][2],
        new_states[2][0],
        new_states[2][1],
        new_states[2][2],
        new_states[3][0],
        new_states[3][1],
        new_states[3][2],
        new_states[4][0],
        new_states[4][1],
        new_states[4][2],
        new_states[5][0],
        new_states[5][1],
        new_states[5][2],
    )


MESH = pl.DeviceIdType.MESH
BF = jnp.bfloat16
F32 = jnp.float32
WIDE = 128
HEADS = 2
LOG2E = math.log2(math.e)
NN = (((1,), (0,)), ((), ()))
NT = (((1,), (1,)), ((), ()))
TN = (((0,), (0,)), ((), ()))
VMEM_LIMIT = 121 * 2**19
PROJ, UP, DOWN, POOL = range(4)
ARRAYS = 4
GELU_C = math.sqrt(2.0 / math.pi)
DOCS = 7
PAD = 16


def dot(a, b, dims=NN):
    return lax.dot_general(a, b, dims, preferred_element_type=F32)


def grid_of(mesh):
    seq, batch = mesh.shape["seq"], mesh.shape["batch"]
    return seq // 2, batch // 2, 2


def fits(mesh):
    seq, batch = mesh.shape["seq"], mesh.shape["batch"]
    return seq == 4 and batch % 2 == 0 and D % (seq * batch * 16) == 0


class Where:
    def __init__(self, nx, nz, ny):
        self.nx, self.nz, self.ny = nx, nz, ny
        self.count, self.batches = 2 * nx, nz * ny
        seq, batch = lax.axis_index("seq"), lax.axis_index("batch")
        self.seq = seq
        self.batch = batch
        self.x, self.c = lax.div(seq, 2), lax.rem(seq, 2)
        self.z, self.y = lax.div(batch, ny), lax.rem(batch, ny)
        self.xo, self.co, self.yo = 1 - self.x, 1 - self.c, 1 - self.y

    def dev(self, x=None, c=None, z=None, y=None):
        x = self.x if x is None else x
        c = self.c if c is None else c
        z = self.z if z is None else z
        y = self.y if y is None else y
        return (x * 2 + c, z * self.ny + y)

    def z_at(self, step):
        return lax.rem(self.z + step, self.nz)

    def seq_at(self, step):
        return lax.rem(self.seq + step, self.count)

    def batch_at(self, step):
        return lax.rem(self.batch + step, self.batches)

    def partner(self, stage):
        return {
            "x": self.dev(x=self.xo),
            "c": self.dev(c=self.co),
            "y": self.dev(y=self.yo),
        }[stage]

    def seq_peers(self):
        return [(self.seq_at(k), self.batch) for k in range(1, self.count)]

    def batch_peers(self):
        return [(self.seq, self.batch_at(k)) for k in range(1, self.batches)]


def remote(src, dst, send, recv, peer):
    return pltpu.make_async_remote_copy(
        src, dst, send, recv, device_id=peer, device_id_type=MESH
    )


class Links:
    def __init__(self):
        self.open = []

    def start(self, copies):
        for copy in copies:
            copy.start()
        self.open += copies
        return copies

    def close(self, copies):
        for copy in copies:
            copy.wait_send()
        self.open = [other for other in self.open if all(other is not copy for copy in copies)]

    def finish(self):
        self.close(list(self.open))


def arrive(copies):
    for copy in copies:
        copy.wait_recv()


class Gather:
    def __init__(self, w, links, fulls, pieces, send, recv):
        self.w, self.links = w, links
        self.fulls, self.pieces, self.send, self.recv = fulls, pieces, send, recv
        self.copies = {}

    def start(self, n, index):
        w = self.w
        a, order, at_rows, at_cols = self.pieces[n]
        stage, done = order[index], order[:index]
        pick = [
            slice(None) if name in done else own
            for name, own in (("x", w.x), ("c", w.c), ("z", w.z), ("y", w.y))
        ]
        block = self.fulls[a].at[pick[0], pick[1], pick[2], pick[3], at_rows, at_cols]
        if stage == "z":
            peers = [(k - 1, w.dev(z=w.z_at(k))) for k in range(1, w.nz)]
        else:
            peers = [(w.nz - 1 + "xyc".index(stage), w.partner(stage))]
        self.copies[n, index] = self.links.start([
            remote(block, block, self.send.at[n, slot], self.recv.at[n, slot], peer)
            for slot, peer in peers
        ])

    def step(self, n, index):
        arrive(self.copies[n, index])
        if index < 3:
            self.start(n, index + 1)


def gather_pieces(shapes):
    def part(a, axis, lo, hi):
        size = shapes[a][axis]
        return slice(size * lo // 4 // 16 * 16, size * hi // 4 // 16 * 16)

    every = slice(None)
    return [
        (PROJ, "zyxc", every, every),
        (UP, "zxyc", every, part(UP, 1, 0, 2)),
        (UP, "zyxc", every, part(UP, 1, 2, 4)),
        (DOWN, "zyxc", part(DOWN, 0, 0, 2), every),
        (DOWN, "zxyc", part(DOWN, 0, 2, 4), every),
        (POOL, "zyxc", part(POOL, 0, 0, 2), every),
        (POOL, "zxyc", part(POOL, 0, 2, 4), every),
    ]


PIECES = 7
GATHER_EARLY = 2
GATHER_STEPS = (
    ((0, 0), (1, 0)),
    ((2, 0),),
    ((3, 0), (0, 1)),
    ((1, 1), (4, 0)),
    (),
    ((5, 0), (2, 1)),
    ((0, 2),),
    ((6, 0), (3, 1)),
    ((0, 3), (4, 1)),
    ((1, 2), (5, 1)),
    ((2, 2), (1, 3), (6, 1)),
    ((4, 2), (2, 3)),
    ((3, 2), (4, 3), (3, 3), (5, 2), (6, 2), (5, 3), (6, 3)),
)


class Scatter:
    ORDERS = ("yzx", "zyx", "yxz", "yzx")

    def __init__(self, w, links, fulls, got, send, recv):
        self.w, self.links = w, links
        self.sums = [full.at[:, 0] for full in fulls]
        self.c_in = [full.at[:, 1] for full in fulls]
        self.got = got
        self.send, self.recv = send, recv
        self.copies, self.make = {}, {}

    @classmethod
    def shapes(cls, a, shard, nx, nz, ny):
        sizes = {"x": nx, "z": nz, "y": ny}
        found, rest = [], "xzy"
        for stage in cls.ORDERS[a]:
            rest = rest.replace(stage, "")
            lead = (nz - 1,) if stage == "z" else ()
            found.append(lead + tuple(sizes[n] for n in rest) + shard)
        return found

    def pick(self, a, index, at):
        order = self.ORDERS[a]
        own = {"x": self.w.x, "z": self.w.z, "y": self.w.y}
        return tuple(
            at if n == order[index] else (own[n] if n in order[:index] else slice(None))
            for n in "xzy"
        )

    def begin(self, a, make):
        w = self.w
        self.make[a] = make
        shape = self.sums[a].shape[1:]
        for x_of in range(w.nx):
            self.sums[a][x_of] = make(x_of * 2 + w.co).reshape(shape).astype(BF)
        self.copies[a, "c"] = self.links.start([
            remote(self.sums[a], self.c_in[a], self.send.at[a, 0], self.recv.at[a, 0],
                   w.partner("c"))
        ])

    def start(self, a, index):
        w, stage = self.w, self.ORDERS[a][index]
        into = self.got[index][a]
        if stage == "z":
            moves = [
                (w.z_at(k), into.at[k - 1], 2 + k, w.dev(z=w.z_at(k))) for k in range(1, w.nz)
            ]
        else:
            moves = [(w.xo if stage == "x" else w.yo, into, "xy".index(stage) + 1,
                      w.partner(stage))]
        self.copies[a, index] = self.links.start([
            remote(self.sums[a].at[self.pick(a, index, at)], to, self.send.at[a, slot],
                   self.recv.at[a, slot], peer)
            for at, to, slot, peer in moves
        ])

    def total(self, a, index):
        w, stage = self.w, self.ORDERS[a][index]
        arrive(self.copies[a, index])
        here = self.pick(a, index, {"x": w.x, "z": w.z, "y": w.y}[stage])
        into = self.got[index][a]
        value = self.sums[a][here].astype(F32)
        if stage == "z":
            for k in range(w.nz - 1):
                value = value + into[k].astype(F32)
        else:
            value = value + into[...].astype(F32)
        return here, value

    def step(self, a, index):
        w = self.w
        if index == 0:
            arrive(self.copies[a, "c"])
            self.links.close(self.copies[a, "c"])
            shape = self.sums[a].shape[1:]
            for x_of in range(w.nx):
                value = self.make[a](x_of * 2 + w.c).reshape(shape)
                self.sums[a][x_of] = (value + self.c_in[a][x_of].astype(F32)).astype(BF)
        else:
            here, value = self.total(a, index - 1)
            self.sums[a][here] = value.astype(BF)
        self.start(a, index)

    def last(self, a):
        return self.total(a, 2)[1]


def norm_stats(values):
    center = values - jnp.mean(values, axis=-1, keepdims=True)
    spread = jnp.mean(center * center, axis=-1, keepdims=True)
    scale = lax.rsqrt(spread + norm_eps)
    return center * scale, scale


def norm_back(grad, unit, scale, gain):
    inner = grad * gain
    mean_one = jnp.mean(inner, axis=-1, keepdims=True)
    mean_two = jnp.mean(inner * unit, axis=-1, keepdims=True)
    back = scale * (inner - mean_one - unit * mean_two)
    return back, jnp.sum(grad * unit, axis=0, keepdims=True), jnp.sum(grad, axis=0, keepdims=True)


def swap_halves(values):
    lane = lax.broadcasted_iota(jnp.int32, values.shape, 1)
    return jnp.where(
        lax.rem(lane, HEAD_DIM) < HEAD_DIM // 2,
        pltpu.roll(values, WIDE - HEAD_DIM // 2, 1),
        pltpu.roll(values, HEAD_DIM // 2, 1),
    )


def in_head(lane, h):
    return (lane >= h * HEAD_DIM) & (lane < (h + 1) * HEAD_DIM)


def with_feats(base, lane, h, vector):
    one = vector.astype(BF).astype(F32)
    two = (vector - one).astype(BF).astype(F32)
    first = (1 - h) * HEAD_DIM + 8
    for n, term in enumerate((one, two, vector - one - two)):
        base = jnp.where(lane == first + n, term, base)
    return base


def document_edges(docs):
    feat = lax.rem(lax.broadcasted_iota(jnp.int32, (1, WIDE), 1), HEAD_DIM)
    lo = jnp.zeros((1, WIDE), jnp.int32)
    hi = jnp.zeros((1, WIDE), jnp.int32)
    below = jnp.zeros((1, 1), jnp.int32)
    for d in range(DOCS):
        upto = jnp.sum(jnp.where(docs <= d, 1, 0), axis=1, keepdims=True)
        lo = jnp.where(feat == d, below, lo)
        hi = jnp.where(feat == d, upto, hi)
        below = upto
    return lo, hi


def layer_buffers(nx, nz, ny, rows, ff, shapes):
    count, block = 2 * nx, rows + PAD
    batches = nz * ny
    vmem = lambda shape, kind=BF: pltpu.VMEM(shape, kind)
    wide = 3 * WIDE
    shard = shapes[0][0]
    scatter = [Scatter.shapes(a, s, nx, nz, ny) for a, s in enumerate(shapes)]
    named = dict(
        fulls=[vmem((nx, 2, nz, ny) + s) for s in shapes],
        part=vmem((count, 3, shard, WIDE)),
        wq=vmem((count, nz, ny, 3, shard, WIDE)),
        small_seq=vmem((count, 16, D)),
        small_all=vmem((batches, 16, D)),
        small=vmem((16, D), F32),
        wide_row=vmem((8, 2 * D), F32),
        tok_all=vmem((count, rows, D)),
        normed=vmem((count, rows, D)),
        ext=vmem((3, HEADS, count * block, WIDE)),
        o_ref=vmem((count, block, WIDE), F32),
        o_low=vmem((count, block, WIDE)),
        att=vmem((count, rows, WIDE)),
        h_one=vmem((rows, D), F32),
        dh_two=vmem((D // WIDE * block, WIDE), F32),
        buf=[vmem((count * block, WIDE), F32) for _ in range(3)],
        normed_two=vmem((rows, D)),
        act=vmem((rows, ff)),
        d_hidden=vmem((rows, ff)),
        d_branch=vmem((rows, D)),
        d_attn=vmem((rows, D)),
        grouped=vmem((rows // 3, 3 * D)),
        edge=vmem((4, 16, D)),
        do_send=vmem((count, rows, WIDE)),
        dq_turned=vmem((WIDE, count * block), F32),
        do_ext=vmem((HEADS, count * block, WIDE)),
        stacked=vmem((rows, wide)),
        g_qkv=vmem((D, wide), F32),
        x_in=vmem((rows, D)),
        gq_out=vmem((batches, count, shard, wide)),
        gq_in=vmem((batches, count, shard, wide)),
        gq_seq=vmem((count, shard, wide)),
        gq_got=vmem((count, shard, wide)),
        small_grad=vmem((16, D), F32),
        sg_seq=vmem((count, 16, D), F32),
        sg_all=vmem((batches, 16, D), F32),
        norm_seq=vmem((count, 8, WIDE), F32),
        norm_all=vmem((batches, 8, WIDE), F32),
        got_one=[vmem(found[0]) for found in scatter],
        got_two=[vmem(found[1]) for found in scatter],
        got_three=[vmem(found[2]) for found in scatter],
    )
    sems = dict(
        gather=(PIECES, nz + 2), scatter=(ARRAYS, nz + 2), tok=(7,), part=(count - 1,),
        wq=(batches - 1,), small_seq=(count - 1,), small_all=(batches - 1,), edge=(2,),
        o=(count, 2), do=(count - 1,), dn=(2,), x=(1,), gq=(batches - 1,), gq_seq=(count - 1,),
        sg_seq=(count - 1,), sg_all=(batches - 1,), norm_seq=(count - 1,),
        norm_all=(batches - 1,),
    )
    for name, shape in sems.items():
        named["sem_" + name] = [pltpu.SemaphoreType.DMA(shape) for _ in range(2)]
    named["ready"] = pltpu.SemaphoreType.REGULAR
    named["free"] = pltpu.SemaphoreType.REGULAR
    return named


SWEEP_STEPS = (
    ((DOWN, 1),),
    ((POOL, 1), (PROJ, 1)),
    ((UP, 1), (DOWN, 2)),
    (),
)


class Bag:
    def __init__(self, template, refs):
        refs = list(refs)
        for name, value in template.items():
            if isinstance(value, list):
                setattr(self, name, [refs.pop(0) for _ in value])
            else:
                setattr(self, name, refs.pop(0))


def layer_kernel(nx, nz, ny, template, tokens, doc_ids, out_grad, qkv_w, proj_w, up_w, down_w,
                 pool_w, small_in, turn, offset, short_out, input_grad, total_qkv, total_proj,
                 total_up, total_down, total_pool, total_small, norm_out, *scratch):
    w = Where(nx, nz, ny)
    b = Bag(template, scratch)
    links = Links()
    rows = tokens.shape[0]
    block = rows + PAD
    count, batches = w.count, w.batches
    pools = rows // 3
    sub = rows // 3
    tiles = D // WIDE
    own = (w.x, w.c, w.z, w.y)

    barrier = pltpu.get_barrier_semaphore()
    peers = w.seq_peers() + w.batch_peers()
    for peer in peers:
        pl.semaphore_signal(barrier, inc=1, device_id=peer, device_id_type=MESH)
    own_small = small_in.shape[1]
    small_first = (w.seq * batches + w.batch) * own_small
    small_row, small_lane = lax.div(small_first, D), lax.rem(small_first, D)
    b.wide_row[...] = jnp.zeros(b.wide_row.shape, F32)
    b.wide_row[0:1, 0:own_small] = small_in[...]
    moved = pltpu.roll(b.wide_row[...], small_lane, 1)
    b.small[...] = jnp.zeros(b.small.shape, F32)
    b.small[pl.ds(small_row, 1)] = moved[0:1, 0:D]
    b.small[pl.ds(small_row + 1, 1)] = moved[0:1, D:]
    b.small_seq[w.seq] = b.small[...].astype(BF)
    for d in range(count):
        b.part[d] = qkv_w[:, :, d * WIDE : (d + 1) * WIDE].astype(BF)
    b.edge[0] = out_grad[0:16]
    shards = (proj_w, up_w, down_w, pool_w)
    for shard, full in zip(shards, b.fulls):
        full[own] = shard[...].astype(BF)
    gather = Gather(w, links, b.fulls, gather_pieces([s.shape for s in shards]), *b.sem_gather)
    pl.semaphore_wait(barrier, len(peers))

    send, recv = b.sem_tok
    mine = b.tok_all.at[w.seq]

    def piece(ref, n):
        return ref.at[pl.ds(n * sub, sub)]

    small_a = links.start([
        remote(b.small_seq.at[w.seq], b.small_seq.at[w.seq], b.sem_small_seq[0].at[k],
               b.sem_small_seq[1].at[k], peer)
        for k, peer in enumerate(w.seq_peers())
    ])
    part_a = links.start([
        remote(b.part.at[w.seq_at(k + 1)], b.wq.at[w.seq, w.z, w.y], b.sem_part[0].at[k],
               b.sem_part[1].at[k], peer)
        for k, peer in enumerate(w.seq_peers())
    ])
    tok_x = links.start([
        remote(piece(tokens, n), piece(mine, n), send.at[n], recv.at[n], w.partner("x"))
        for n in range(3)
    ])
    for n in range(GATHER_EARLY):
        gather.start(n, 0)
    tok_c = links.start([remote(tokens, mine, send.at[3], recv.at[3], w.partner("c"))])
    links.start([
        remote(b.edge.at[0], b.edge.at[1], b.sem_edge[0].at[0], b.sem_edge[1].at[0],
               (w.seq_at(count - 1), w.batch))
    ])
    grad_edge = links.open[-1:]
    b.wq[w.seq, w.z, w.y] = b.part[w.seq]
    lo, hi = document_edges(doc_ids[...])
    arrive(small_a)
    total = b.small_seq[0].astype(F32)
    for n in range(1, count):
        total = total + b.small_seq[n].astype(F32)
    b.small_all[w.batch] = total.astype(BF)
    small_b = links.start([
        remote(b.small_all.at[w.batch], b.small_all.at[w.batch], b.sem_small_all[0].at[k],
               b.sem_small_all[1].at[k], peer)
        for k, peer in enumerate(w.batch_peers())
    ])
    arrive(part_a)
    part_b = links.start([
        remote(b.wq.at[:, w.z, w.y], b.wq.at[:, w.z, w.y], b.sem_wq[0].at[k],
               b.sem_wq[1].at[k], peer)
        for k, peer in enumerate(w.batch_peers())
    ])
    for n in range(GATHER_EARLY, PIECES):
        gather.start(n, 0)
    b.tok_all[w.seq] = tokens[...]

    lane_row = lax.broadcasted_iota(jnp.int32, (1, WIDE), 1)
    feat_row = lax.rem(lane_row, HEAD_DIM)
    pad_lane = lax.broadcasted_iota(jnp.int32, (PAD, WIDE), 1)
    for h in range(HEADS):
        for n in range(count):
            pad = pl.ds(n * block + rows, PAD)
            b.ext[0, h, pad] = jnp.zeros((PAD, WIDE), BF)
            masks = ~in_head(pad_lane, h) & (lax.rem(pad_lane, HEAD_DIM) < DOCS)
            b.ext[1, h, pad] = jnp.where(masks, masked_score, 0.0).astype(BF)
            b.ext[2, h, pad] = jnp.zeros((PAD, WIDE), BF)
            b.do_ext[h, pad] = jnp.zeros((PAD, WIDE), BF)

    arrive(small_b)
    total = b.small_all[0].astype(F32)
    for n in range(1, batches):
        total = total + b.small_all[n].astype(F32)
    b.small[...] = total
    small = b.small
    arrive(part_b)

    def qkv_weight(n):
        return b.wq[:, :, :, n].reshape(D, WIDE)

    def turning(of_block, r0):
        cos_in, sin_in = turn[0, pl.ds(r0, sub)], turn[1, pl.ds(r0, sub)]
        cos_of, sin_of = offset[0, pl.ds(of_block, 1)], offset[1, pl.ds(of_block, 1)]
        return cos_in * cos_of - sin_in * sin_of, sin_in * cos_of + cos_in * sin_of

    def project(of_block):
        weight = jnp.concatenate([qkv_weight(n) for n in range(3)], axis=1)

        def body(n, _):
            r0 = pl.multiple_of(n * sub, 16)
            unit, _ = norm_stats(b.tok_all[of_block, pl.ds(r0, sub)].astype(F32))
            normed = (unit * small[0:1] + small[1:2]).astype(BF)
            b.normed[of_block, pl.ds(r0, sub)] = normed
            qkv = dot(normed, weight)
            cosine, sine = turning(of_block, r0)
            parts = [qkv[:, m * WIDE : (m + 1) * WIDE] for m in range(3)]
            for m in range(2):
                parts[m] = parts[m] * cosine + swap_halves(parts[m]) * sine
            parts[0] = parts[0] * (LOG2E * HEAD_DIM ** -0.5)
            place = lax.broadcasted_iota(jnp.int32, (sub, WIDE), 0) + (of_block * rows + r0)
            lane = lax.broadcasted_iota(jnp.int32, (sub, WIDE), 1)
            same = (place >= lo) & (place < hi)
            ones = jnp.where((feat_row >= 8) & (feat_row < 11), 1.0, 0.0)
            q_feat = jnp.where(same, 1.0, 0.0)
            k_feat = jnp.where(feat_row < DOCS, jnp.where(same, 0.0, masked_score), ones)
            at = pl.ds(pl.multiple_of(of_block * block + r0, 16), sub)
            for h in range(HEADS):
                for m, feats in enumerate((q_feat, k_feat, 1.0)):
                    b.ext[m, h, at] = jnp.where(in_head(lane, h), parts[m], feats).astype(BF)
            return 0

        lax.fori_loop(0, 3, body, 0)

    pending = list(GATHER_STEPS)

    def advance():
        for n, index in pending.pop(0):
            gather.step(n, index)

    project(w.seq)
    advance()
    arrive(tok_c)
    project(w.x * 2 + w.co)
    advance()
    theirs = b.tok_all.at[w.xo * 2 + w.c]
    passed = []
    for n in range(3):
        arrive(tok_x[n : n + 1])
        passed += links.start([
            remote(piece(theirs, n), piece(theirs, n), send.at[4 + n], recv.at[4 + n],
                   w.partner("c"))
        ])
    project(w.xo * 2 + w.c)
    advance()
    arrive(passed)
    project(w.xo * 2 + w.co)
    advance()

    half_rows = (block // 2, rows - block // 2)

    def attend(of_block, half):
        size = block // 2
        r0 = of_block * block + half * size
        n = min(count * block, -(-(r0 + size) // 256) * 256)
        m0 = (r0 // 128) * 128
        lane = lax.broadcasted_iota(jnp.int32, (size, WIDE), 1)
        at_row = lax.broadcasted_iota(jnp.int32, (size, n - m0), 0) + r0
        at_col = lax.broadcasted_iota(jnp.int32, (size, n - m0), 1) + m0
        queries = [b.ext[0, h, pl.ds(r0, size)] for h in range(HEADS)]
        scores = [dot(queries[h], b.ext[1, h, :n], NT) for h in range(HEADS)]
        outs = []
        for h in range(HEADS):
            s = scores[h]
            tail = jnp.where(at_col <= at_row, s[:, m0:], masked_score)
            s = jnp.concatenate([s[:, :m0], tail], axis=1) if m0 else tail
            top = jnp.max(s, axis=1, keepdims=True)
            p = jnp.exp2(s - top).astype(BF)
            sums = dot(p, b.ext[2, h, :n])
            outs.append(sums / pltpu.roll(sums, HEAD_DIM, 1))
            log_total = top + jnp.log2(sums)
            q_new = with_feats(queries[h].astype(F32), lane, h, -log_total)
            b.ext[0, h, pl.ds(r0, size)] = q_new.astype(BF)
        both = jnp.where(lane < HEAD_DIM, outs[0], outs[1])
        b.o_ref[of_block, pl.ds(half * size, size)] = both
        b.o_low[of_block, pl.ds(half * size, size)] = both.astype(BF)

    def o_copy(of_block, half):
        at = pl.ds(half * (block // 2), half_rows[half])
        return remote(b.o_low.at[of_block, at], b.att.at[w.seq, at], b.sem_o[0].at[of_block, half],
                      b.sem_o[1].at[w.seq, half], (of_block, w.batch))

    for of_block in range(count):
        for half in range(2):
            attend(of_block, half)

            @pl.when(w.seq != of_block)
            def _(of_block=of_block, half=half):
                o_copy(of_block, half).start()

            advance()

        @pl.when(w.seq == of_block)
        def _(of_block=of_block):
            b.att[of_block] = b.o_low[of_block, 0:rows]

    advance()

    proj = b.fulls[PROJ][...].reshape(D, D)
    pool = b.fulls[POOL][...].reshape(3 * D, D)
    first, last = w.seq == 0, w.seq == count - 1

    def lay(ref, start, value):
        for n in range(tiles):
            ref[pl.ds(n * block + start, value.shape[0])] = value[:, n * WIDE : (n + 1) * WIDE]

    def whole(ref, start):
        return jnp.concatenate(
            [ref[pl.ds(n * block + start, rows)] for n in range(tiles)], axis=1
        )

    def add(ref, value):
        for n in range(tiles):
            ref[pl.ds(n * block, rows)] += value[:, n * WIDE : (n + 1) * WIDE]

    sum_one, sum_two, h_two = b.buf
    g_low = out_grad[...]
    spread = dot(g_low, pool, NT)
    for k in range(3):
        for n in range(tiles):
            at = k * D + n * WIDE
            b.dh_two[pl.ds(n * block + 6 + k, pools, stride=3)] = spread[:, at : at + WIDE]
    arrive(grad_edge)
    beyond = jnp.where(last, 0.0, dot(b.edge[1], pool, NT))
    lay(b.dh_two, 8 + rows - 2, beyond[0:1, 0:D])
    lay(b.dh_two, 8 + rows - 1, beyond[0:1, D : 2 * D])
    b.d_branch[...] = whole(b.dh_two, 8).astype(BF)
    small_grad = b.small_grad
    small_grad[...] = jnp.zeros(small_grad.shape, F32)
    small_grad[4:5] = jnp.sum(b.d_branch[...].astype(F32), axis=0, keepdims=True)
    small_grad[5:6] = jnp.sum(g_low.astype(F32), axis=0, keepdims=True)
    sum_one[...] = jnp.zeros(sum_one.shape, F32)
    sum_two[...] = jnp.zeros(sum_two.shape, F32)

    for k in range(1, count):
        of = w.seq_at(k)
        for half in range(2):
            at = pl.ds(half * (block // 2), half_rows[half])
            remote(b.att.at[of, at], b.att.at[of, at], b.sem_o[0].at[of, half],
                   b.sem_o[1].at[of, half], (of, w.batch)).wait_recv()
    attended = jnp.concatenate([b.att[n] for n in range(count)], axis=1)
    b.h_one[...] = tokens[...].astype(F32) + dot(attended, proj)
    unit, _ = norm_stats(b.h_one[...])
    b.normed_two[...] = (unit * small[2:3] + small[3:4]).astype(BF)
    links.finish()
    for of_block in range(count):
        for half in range(2):

            @pl.when(w.seq != of_block)
            def _(of_block=of_block, half=half):
                o_copy(of_block, half).wait_send()

    for peer in w.seq_peers():
        pl.semaphore_signal(b.free, inc=1, device_id=peer, device_id_type=MESH)
    part = b.act.shape[1] // count

    def feed(n, _):
        cols = pl.ds(pl.multiple_of(n * part, part), part)
        up = b.fulls[UP][:, :, :, :, :, cols].reshape(D, part)
        down = b.fulls[DOWN][lax.div(n, 2), lax.rem(n, 2)].reshape(part, D)
        hidden = dot(b.normed_two[...], up) + small[pl.ds(6 + n, 1)]
        square = hidden * hidden
        bend = jnp.tanh(GELU_C * hidden * (1.0 + 0.044715 * square))
        half = 0.5 * (1.0 + bend)
        act_low = (hidden * half).astype(BF)
        b.act[:, cols] = act_low
        slope = half + 0.5 * hidden * (1.0 - bend * bend) * (
            GELU_C * (1.0 + 3 * 0.044715 * square)
        )
        add(sum_one, dot(act_low, down))
        d_low = (dot(b.d_branch[...], down, NT) * slope).astype(BF)
        b.d_hidden[:, cols] = d_low
        small_grad[pl.ds(6 + n, 1)] = jnp.sum(d_low.astype(F32), axis=0, keepdims=True)
        add(sum_two, dot(d_low, up, NT))
        return 0

    lax.fori_loop(0, count, feed, 0)
    h_low = (b.h_one[...] + whole(sum_one, 0) + small[4:5]).astype(BF)
    lay(h_two, 8, h_low.astype(F32))
    b.edge[2] = h_low[rows - 16 :]
    row_edge = links.start([
        remote(b.edge.at[2], b.edge.at[3], b.sem_edge[0].at[1], b.sem_edge[1].at[1],
               (w.seq_at(1), w.batch))
    ])
    unit, scale = norm_stats(b.h_one[...])
    back, small_grad[2:3], small_grad[3:4] = norm_back(whole(sum_two, 0), unit, scale, small[2:3])
    grad_one = whole(b.dh_two, 8) + back
    b.h_one[...] = grad_one
    b.d_attn[...] = grad_one.astype(BF)
    spread_back = dot(b.d_attn[...], proj, NT).astype(BF)
    for n in range(count):
        b.do_send[n] = spread_back[:, n * WIDE : (n + 1) * WIDE]
    do_all = b.o_low
    pl.semaphore_wait(b.free, count - 1)
    given = links.start([
        remote(b.do_send.at[w.seq_at(k + 1)], do_all.at[w.seq, 0:rows], b.sem_do[0].at[k],
               b.sem_do[1].at[k], peer)
        for k, peer in enumerate(w.seq_peers())
    ])
    do_all[w.seq, 0:rows] = b.do_send[w.seq]

    def tell_core():
        pl.semaphore_signal(b.ready, inc=1, device_id=w.partner("c"), device_id_type=MESH)
        pl.semaphore_wait(b.ready, 1)

    tell_core()
    scatter = Scatter(w, links, b.fulls, (b.got_one, b.got_two, b.got_three), *b.sem_scatter)

    def columns(ref):
        width = ref.shape[1] // count
        return lambda n: ref[:, pl.ds(pl.multiple_of(n * width, WIDE), width)]

    of_act, of_grouped, of_normed = columns(b.act), columns(b.grouped), columns(b.normed_two)
    scatter.begin(DOWN, lambda n: dot(of_act(n), b.d_branch[...], TN))
    scatter.begin(UP, lambda n: dot(of_normed(n), b.d_hidden[...], TN))
    scatter.step(DOWN, 0)
    arrive(row_edge)
    before = jnp.where(first, 0.0, b.edge[3].astype(F32))
    lay(h_two, 0, before[8:16])
    for k in range(3):
        for n in range(tiles):
            at = k * D + n * WIDE
            rows_of = h_two[pl.ds(n * block + 6 + k, pools, stride=3)]
            b.grouped[:, at : at + WIDE] = rows_of.astype(BF)
    short_out[...] = (dot(b.grouped[...], pool) + small[5:6]).astype(BF)
    tell_core()
    scatter.begin(POOL, lambda n: dot(of_grouped(n), g_low, TN))
    scatter.begin(PROJ, lambda n: dot(b.att[n], b.d_attn[...], TN))
    scatter.step(UP, 0)
    scatter.step(POOL, 0)
    scatter.step(PROJ, 0)

    def prepare(of_block):
        def body(n, _):
            r0 = pl.multiple_of(n * sub, 16)
            lane = lax.broadcasted_iota(jnp.int32, (sub, WIDE), 1)
            grad = do_all[of_block, pl.ds(r0, sub)].astype(F32)
            terms = grad * b.o_ref[of_block, pl.ds(r0, sub)]
            at = pl.ds(pl.multiple_of(of_block * block + r0, 16), sub)
            for h in range(HEADS):
                mine = in_head(lane, h)
                delta = jnp.sum(jnp.where(mine, terms, 0.0), axis=1, keepdims=True)
                base = jnp.where(mine, grad, 0.0)
                b.do_ext[h, at] = with_feats(base, lane, h, -delta).astype(BF)
            return 0

        lax.fori_loop(0, 3, body, 0)

    arrive(given)
    for n in range(count):
        prepare(n)
    dq, dk, dv = b.buf
    for ref in b.buf:
        ref[...] = jnp.zeros(ref.shape, F32)
    b.g_qkv[...] = jnp.zeros(b.g_qkv.shape, F32)
    b.dq_turned[...] = jnp.zeros(b.dq_turned.shape, F32)

    def pair(q_first, k_first, size, on_diagonal):
        at_q = pl.ds(pl.multiple_of(q_first, WIDE), size)
        at_k = pl.ds(pl.multiple_of(k_first, WIDE), size)
        probs = [dot(b.ext[1, h, at_k], b.ext[0, h, at_q], NT) for h in range(HEADS)]
        slopes = [dot(b.ext[2, h, at_k], b.do_ext[h, at_q], NT) for h in range(HEADS)]
        found = []
        for h in range(HEADS):
            p = jnp.exp2(probs[h])
            if on_diagonal:
                keys = lax.broadcasted_iota(jnp.int32, (size, size), 0)
                queries = lax.broadcasted_iota(jnp.int32, (size, size), 1)
                p = jnp.where(keys <= queries, p, 0.0)
            ds = (p * slopes[h]).astype(BF)
            found.append((dot(b.ext[1, h, at_k], ds, TN), dot(ds, b.ext[0, h, at_q]),
                          dot(p.astype(BF), b.do_ext[h, at_q])))
        lane = lax.broadcasted_iota(jnp.int32, (size, WIDE), 1)
        for ref, zero, one in zip((dk, dv), *[f[1:] for f in found]):
            ref[at_k] += jnp.where(lane < HEAD_DIM, zero, one)
        row = lax.broadcasted_iota(jnp.int32, (WIDE, size), 0)
        b.dq_turned[:, at_q] += jnp.where(row < HEAD_DIM, found[0][0], found[1][0])

    backs = (HEAD_DIM ** -0.5, 1.0 / LOG2E, 1.0)

    def dn_copy(turn_of):
        n = turn_of // 2
        return remote(b.tok_all.at[n], b.tok_all.at[2 + n], b.sem_dn[0].at[n], b.sem_dn[1].at[n],
                      w.partner("c"))

    def complete(turn_of, of_block):
        span = pl.ds(pl.multiple_of(of_block * block, WIDE), block)
        dq[span] = b.dq_turned[:, span].T

        def body(n, _):
            r0 = pl.multiple_of(n * sub, 16)
            cosine, sine = turning(of_block, r0)
            at = pl.ds(pl.multiple_of(of_block * block + r0, 16), sub)
            for m, ref in enumerate(b.buf):
                value = ref[at] * backs[m]
                if m < 2:
                    value = value * cosine - swap_halves(value) * sine
                b.stacked[pl.ds(r0, sub), m * WIDE : (m + 1) * WIDE] = value.astype(BF)
            return 0

        lax.fori_loop(0, 3, body, 0)
        weight = jnp.concatenate([qkv_weight(n) for n in range(3)], axis=1)
        b.g_qkv[...] += dot(b.normed[of_block], b.stacked[...], TN)
        back = dot(b.stacked[...], weight, NT)
        keeps = lax.rem(of_block, 2) == w.c

        @pl.when(keeps)
        def _():
            lay(b.dh_two, 0, back)

        @pl.when(jnp.logical_not(keeps))
        def _():
            b.tok_all[turn_of // 2] = back.astype(BF)
            dn_copy(turn_of).start()

    def summed(turn_of):
        dn_copy(turn_of).wait_recv()
        return whole(b.dh_two, 0) + b.tok_all[2 + turn_of // 2].astype(F32)

    down_first = w.x == 0
    x_copy = []
    for turn_of in range(count):
        outer = jnp.where(down_first, count - 1 - turn_of, turn_of)
        pair(outer * block, outer * block, block, True)

        def inner(n, _, outer=outer, turn_of=turn_of):
            other = jnp.where(down_first, n, turn_of + 1 + n)
            pair(jnp.where(down_first, outer, other) * block,
                 jnp.where(down_first, other, outer) * block, block, False)
            return 0

        if turn_of < count - 1:
            lax.fori_loop(0, count - 1 - turn_of, inner, 0)
        complete(turn_of, outer)
        if turn_of == count // 2 - 1:
            b.d_attn[...] = summed(turn_of).astype(BF)
            x_copy = links.start([
                remote(b.d_attn, b.x_in, b.sem_x[0].at[0], b.sem_x[1].at[0], w.partner("x"))
            ])
        for a, index in SWEEP_STEPS[turn_of]:
            scatter.step(a, index)

    def gather_squares(squares, total):
        flat = jnp.sum((total * total).reshape(-1, 8, total.shape[-1]), axis=0)
        for n in range(flat.shape[1] // WIDE):
            squares = squares + flat[:, n * WIDE : (n + 1) * WIDE]
        return squares

    for n in range(batches):
        z_of, y_of = n // ny, n % ny
        rows_of = b.g_qkv[...].reshape(count, nz, ny, -1, 3 * WIDE)[:, z_of, y_of]
        b.gq_out[n] = rows_of.astype(BF)
    gq = links.start([
        remote(b.gq_out.at[w.batch_at(k + 1)], b.gq_in.at[w.batch], b.sem_gq[0].at[k],
               b.sem_gq[1].at[k], peer)
        for k, peer in enumerate(w.batch_peers())
    ])
    b.gq_in[w.batch] = b.gq_out[w.batch]
    for a in (POOL, UP, PROJ):
        scatter.step(a, 2)

    grad_normed = summed(count - 1)
    arrive(x_copy)
    grad_normed = grad_normed + b.x_in[...].astype(F32)
    unit, scale = norm_stats(tokens[...].astype(F32))
    back, small_grad[0:1], small_grad[1:2] = norm_back(grad_normed, unit, scale, small[0:1])
    input_grad[...] = b.h_one[...] + back
    b.sg_seq[w.seq] = small_grad[...]
    sg = links.start([
        remote(b.sg_seq.at[w.seq], b.sg_seq.at[w.seq], b.sem_sg_seq[0].at[k],
               b.sem_sg_seq[1].at[k], peer)
        for k, peer in enumerate(w.seq_peers())
    ])
    arrive(gq)
    total = b.gq_in[0].astype(F32)
    for n in range(1, batches):
        total = total + b.gq_in[n].astype(F32)
    b.gq_seq[...] = total.astype(BF)
    squares = gather_squares(jnp.zeros((8, WIDE), F32), total)
    gq = links.start([
        remote(b.gq_seq.at[w.seq_at(k + 1)], b.gq_got.at[w.seq], b.sem_gq_seq[0].at[k],
               b.sem_gq_seq[1].at[k], peer)
        for k, peer in enumerate(w.seq_peers())
    ])
    b.gq_got[w.seq] = b.gq_seq[w.seq]
    arrive(sg)
    total = b.sg_seq[0]
    for n in range(1, count):
        total = total + b.sg_seq[n]
    b.sg_all[w.batch] = total
    sg = links.start([
        remote(b.sg_all.at[w.batch], b.sg_all.at[w.batch], b.sem_sg_all[0].at[k],
               b.sem_sg_all[1].at[k], peer)
        for k, peer in enumerate(w.batch_peers())
    ])

    totals = (total_proj, total_up, total_down, total_pool)
    for a in (DOWN, UP, POOL, PROJ):
        total = scatter.last(a)
        totals[a][...] = total
        squares = gather_squares(squares, total)
    b.norm_seq[w.seq] = squares
    norm = links.start([
        remote(b.norm_seq.at[w.seq], b.norm_seq.at[w.seq], b.sem_norm_seq[0].at[k],
               b.sem_norm_seq[1].at[k], peer)
        for k, peer in enumerate(w.seq_peers())
    ])
    arrive(gq)
    for n in range(3):
        total = jnp.concatenate(
            [b.gq_got[m, :, n * WIDE : (n + 1) * WIDE].astype(F32) for m in range(count)], axis=1
        )
        total_qkv[n] = total
    arrive(sg)
    total = b.sg_all[0]
    for n in range(1, batches):
        total = total + b.sg_all[n]
    small_grad[...] = total
    b.wide_row[0:1, 0:D] = small_grad[pl.ds(small_row, 1)]
    b.wide_row[0:1, D:] = small_grad[pl.ds(small_row + 1, 1)]
    moved = pltpu.roll(b.wide_row[...], 2 * D - small_lane, 1)
    total_small[...] = moved[0:1, 0:own_small]
    small_squares = gather_squares(jnp.zeros((8, WIDE), F32), total)
    arrive(norm)
    squares = b.norm_seq[0]
    for n in range(1, count):
        squares = squares + b.norm_seq[n]
    b.norm_all[w.batch] = squares
    norm = links.start([
        remote(b.norm_all.at[w.batch], b.norm_all.at[w.batch], b.sem_norm_all[0].at[k],
               b.sem_norm_all[1].at[k], peer)
        for k, peer in enumerate(w.batch_peers())
    ])
    arrive(norm)
    squares = b.norm_all[0]
    for n in range(1, batches):
        squares = squares + b.norm_all[n]
    squares = squares + small_squares
    square = jnp.sum(jnp.sum(squares, axis=1, keepdims=True), axis=0, keepdims=True)
    norm_out[...] = jnp.broadcast_to(jnp.sqrt(square), norm_out.shape)
    for turn_of in (1, 3):
        dn_copy(turn_of).wait_send()
    links.finish()


def step_kernel(norm_in, grad_in, short_in, *refs):
    states = refs[: 4 * 6]
    outs = refs[4 * 6 :]
    grad_out, short_out, norm_out = outs[:3]
    grad_out[...] = grad_in[...]
    short_out[...] = short_in[...]
    grad_norm = norm_in[0:1, 0:1]
    norm_out[...] = grad_norm
    clip = clip_norm / jnp.maximum(grad_norm, clip_norm)
    for a in range(6):
        total, weight, one, two = states[4 * a : 4 * a + 4]
        limit = clip.reshape((1,) * len(total.shape))
        rate, decay = (rate_vector, 0.0) if a == 5 else (rate_matrix, decay_weight)
        results = adam_update(total[...], one[...], two[...], weight[...], limit, rate, decay)
        for ref, value in zip(outs[3 + 3 * a : 6 + 3 * a], results):
            ref[...] = value


def rotary_tables(rows, count):
    half = HEAD_DIM // 2
    frequency = np.exp(-math.log(10000.0) * np.arange(half) / half)
    lanes = np.tile(frequency, WIDE // half)
    sign = np.tile(np.repeat([-1.0, 1.0], half), WIDE // HEAD_DIM)
    inside = np.arange(rows)[:, None] * lanes
    starts = (np.arange(8) * (np.arange(8) < count) * rows)[:, None] * lanes
    pack = lambda angle: np.stack([np.cos(angle), np.sin(angle) * sign]).astype(np.float32)
    return pack(inside), pack(starts)


def fast_local(mesh):
    nx, nz, ny = grid_of(mesh)
    count = 2 * nx
    in_vmem = pl.BlockSpec(memory_space=pltpu.VMEM)

    def call(kernel, outs, scratch, args, **params):
        return pl.pallas_call(
            kernel,
            out_shape=[jax.ShapeDtypeStruct(s, t) for s, t in outs],
            in_specs=[in_vmem] * len(args),
            out_specs=[in_vmem] * len(outs),
            scratch_shapes=scratch,
            compiler_params=pltpu.CompilerParams(vmem_limit_bytes=VMEM_LIMIT, **params),
        )(*args)

    def body(tokens, doc_ids, out_grad,
             qkv_weight, qkv_first, qkv_second,
             proj_weight, proj_first, proj_second,
             up_weight, up_first, up_second,
             down_weight, down_first, down_second,
             pool_weight, pool_first, pool_second,
             small_weight, small_first, small_second):
        rows = tokens.shape[1]
        pools = out_grad.shape[1]
        ff = up_weight.shape[1]
        own = small_weight.shape[0]
        turn, offset = rotary_tables(rows, count)
        weights = (qkv_weight, proj_weight, up_weight, down_weight, pool_weight)
        shapes = [v.shape for v in weights]
        template = layer_buffers(nx, nz, ny, rows, ff, shapes[1:])
        scratch = jax.tree.leaves(list(template.values()))
        outs = [((pools, D), BF), ((rows, D), F32)] + [(s, F32) for s in shapes]
        outs += [((1, own), F32), ((8, WIDE), F32)]
        short, grad_in, *totals, norm = call(
            lambda *r: layer_kernel(nx, nz, ny, template, *r), outs, scratch,
            (tokens[0], doc_ids, out_grad[0], *weights, small_weight.reshape(1, own), turn, offset),
            collective_id=0, has_side_effects=True)
        weights = (*weights, small_weight)
        firsts = (qkv_first, proj_first, up_first, down_first, pool_first, small_first)
        seconds = (qkv_second, proj_second, up_second, down_second, pool_second, small_second)
        groups = [list(group) for group in zip(totals, weights, firsts, seconds)]
        groups[5] = [v.reshape(1, own) for v in groups[5]]
        outs = [((rows, D), F32), ((pools, D), BF), ((1, 1), F32)]
        outs += [(v[0].shape, F32) for v in groups for _ in range(3)]
        grad_out, short_out, norm_out, *states = call(
            step_kernel, outs, [],
            (norm, grad_in, short, *[v for group in groups for v in group]))
        states[15:] = [v.reshape(own) for v in states[15:]]
        return (short_out[None], grad_out[None], norm_out.reshape(()), *states)

    return body


def solution(mesh):
    in_specs = (
        P("batch", "seq", None),
        P("batch", None),
        P("batch", "seq", None),
        P(None, ("seq", "batch"), None),
        P(None, ("seq", "batch"), None),
        P(None, ("seq", "batch"), None),
        P(("seq", "batch"), None),
        P(("seq", "batch"), None),
        P(("seq", "batch"), None),
        P(("seq", "batch"), None),
        P(("seq", "batch"), None),
        P(("seq", "batch"), None),
        P(("seq", "batch"), None),
        P(("seq", "batch"), None),
        P(("seq", "batch"), None),
        P(("seq", "batch"), None),
        P(("seq", "batch"), None),
        P(("seq", "batch"), None),
        P(("seq", "batch")),
        P(("seq", "batch")),
        P(("seq", "batch")),
    )
    out_specs = (
        P("batch", "seq", None),
        P("batch", "seq", None),
        P(),
        P(None, ("seq", "batch"), None),
        P(None, ("seq", "batch"), None),
        P(None, ("seq", "batch"), None),
        P(("seq", "batch"), None),
        P(("seq", "batch"), None),
        P(("seq", "batch"), None),
        P(("seq", "batch"), None),
        P(("seq", "batch"), None),
        P(("seq", "batch"), None),
        P(("seq", "batch"), None),
        P(("seq", "batch"), None),
        P(("seq", "batch"), None),
        P(("seq", "batch"), None),
        P(("seq", "batch"), None),
        P(("seq", "batch"), None),
        P(("seq", "batch")),
        P(("seq", "batch")),
        P(("seq", "batch")),
    )
    body = fast_local(mesh) if fits(mesh) else local
    return jax.shard_map(body, mesh=mesh, in_specs=in_specs, out_specs=out_specs, check_vma=False)
```

```python
import math

import jax
import jax.numpy as jnp
import numpy as np
from jax import lax
from jax.experimental import pallas as pl
from jax.experimental.pallas import tpu as pltpu
from jax.sharding import PartitionSpec as P

D = 512
HEAD_DIM = 64
STEP = 10


beta_one = 0.9
beta_two = 0.999
adam_eps = 1e-08
norm_eps = 1e-05
clip_norm = 1.0
rate_matrix = 0.05
rate_vector = 0.5
decay_weight = 0.1
masked_score = -1e30


def from_behind(block, axis, distance):
    devices = range(lax.axis_size(axis))
    route = [(i - distance, i) for i in devices if i - distance in devices]
    return lax.ppermute(block, axis, route)


def layer_norm(values, scale_gain, shift_vec):
    center = values - jnp.mean(values, axis=-1, keepdims=True)
    spread = jnp.mean(center * center, axis=-1, keepdims=True)
    return center * lax.rsqrt(spread + norm_eps) * scale_gain + shift_vec


def rotate(values, positions):
    half_dim = HEAD_DIM // 2
    head_view = values.reshape(values.shape[0], values.shape[1] // HEAD_DIM, HEAD_DIM)
    frequency = jnp.exp(-math.log(10000.0) * jnp.arange(half_dim, dtype=jnp.float32) / half_dim)
    angles = positions.astype(jnp.float32)[:, None] * frequency[None, :]
    cosine = jnp.cos(angles)[:, None, :]
    sine_part = jnp.sin(angles)[:, None, :]
    first_half = head_view[..., :half_dim]
    second_half = head_view[..., half_dim:]
    turned = jnp.concatenate(
        [
            first_half * cosine - second_half * sine_part,
            second_half * cosine + first_half * sine_part,
        ],
        axis=-1,
    )
    return turned.reshape(values.shape)


def outer_sum(left_side, right_side):
    return lax.dot_general(
        left_side, right_side, (((0,), (0,)), ((), ())), preferred_element_type=jnp.float32
    )


def times_transpose(left_side, right_side):
    return lax.dot_general(
        left_side, right_side, (((1,), (1,)), ((), ())), preferred_element_type=jnp.float32
    )


def split_heads(values):
    return values.reshape(values.shape[0], values.shape[1] // HEAD_DIM, HEAD_DIM)


def block_scores(query_heads, key_heads, query_pos, key_pos, query_doc, key_doc):
    raw_scores = jnp.einsum(
        "qhd,khd->hqk", query_heads, key_heads, preferred_element_type=jnp.float32
    ) * HEAD_DIM ** (-0.5)
    allowed = (key_pos[None, :] <= query_pos[:, None]) & (key_doc[None, :] == query_doc[:, None])
    return jnp.where(allowed[None], raw_scores, masked_score)


def adam_update(gradient, first_moment, second_moment, weight, clip_scale, step_rate, decay_rate):
    clipped = gradient * clip_scale
    first_new = beta_one * first_moment + (1.0 - beta_one) * clipped
    second_new = beta_two * second_moment + (1.0 - beta_two) * clipped * clipped
    first_hat = first_new / (1.0 - beta_one**STEP)
    second_hat = second_new / (1.0 - beta_two**STEP)
    weight_new = weight - step_rate * (
        first_hat / (jnp.sqrt(second_hat) + adam_eps) + decay_rate * weight
    )
    return (first_new, second_new, weight_new)


def local(
    tokens,
    doc_ids,
    out_grad,
    qkv_weight,
    qkv_first,
    qkv_second,
    proj_weight,
    proj_first,
    proj_second,
    up_weight,
    up_first,
    up_second,
    down_weight,
    down_first,
    down_second,
    pool_weight,
    pool_first,
    pool_second,
    small_weight,
    small_first,
    small_second,
):
    block_rows = tokens.shape[1]
    model_width = tokens.shape[2]
    seq_count = lax.axis_size("seq")
    my_block = lax.axis_index("seq")
    whole_qkv, whole_proj, whole_up, whole_down, whole_pool, whole_small = (
        lax.all_gather(qkv_weight.astype(jnp.bfloat16), ("seq", "batch"), axis=1, tiled=True),
        lax.all_gather(proj_weight.astype(jnp.bfloat16), ("seq", "batch"), axis=0, tiled=True),
        lax.all_gather(up_weight.astype(jnp.bfloat16), ("seq", "batch"), axis=0, tiled=True),
        lax.all_gather(down_weight.astype(jnp.bfloat16), ("seq", "batch"), axis=0, tiled=True),
        lax.all_gather(pool_weight.astype(jnp.bfloat16), ("seq", "batch"), axis=0, tiled=True),
        lax.all_gather(small_weight.astype(jnp.bfloat16), ("seq", "batch"), axis=0, tiled=True),
    )
    small_used = whole_small.astype(jnp.float32)
    gain_first = small_used[0:D]
    shift_first = small_used[D : 2 * D]
    gain_second = small_used[2 * D : 3 * D]
    shift_second = small_used[3 * D : 4 * D]
    bias_down = small_used[4 * D : 5 * D]
    bias_pool = small_used[5 * D : 6 * D]
    bias_up = small_used[6 * D :]
    inputs = tokens[0].astype(jnp.float32)
    doc_row = doc_ids[0]
    first_row = my_block * block_rows
    positions = first_row + jnp.arange(block_rows, dtype=jnp.int32)
    doc_mine = lax.dynamic_slice_in_dim(doc_row, first_row, block_rows)
    normed, first_pull = jax.vjp(layer_norm, inputs, gain_first, shift_first)
    normed_low = normed.astype(jnp.bfloat16)
    projected = jnp.einsum("td,cde->cte", normed_low, whole_qkv, preferred_element_type=jnp.float32)
    queries_rot, query_pull = jax.vjp(lambda values: rotate(values, positions), projected[0])
    keys_rot, key_pull = jax.vjp(lambda values: rotate(values, positions), projected[1])
    query_low = queries_rot.astype(jnp.bfloat16)
    key_low = keys_rot.astype(jnp.bfloat16)
    value_low = projected[2].astype(jnp.bfloat16)
    keys_all, values_all = (
        lax.all_gather(key_low, "seq", axis=0, tiled=True),
        lax.all_gather(value_low, "seq", axis=0, tiled=True),
    )
    query_heads = split_heads(query_low)
    head_count = query_heads.shape[1]
    zeros_head_rows = jnp.zeros((head_count, block_rows), jnp.float32)
    zeros_heads = jnp.zeros((block_rows, head_count, HEAD_DIM), jnp.float32)

    def scores_of(number):
        start_row = number * block_rows
        key_heads = split_heads(keys_all[start_row : start_row + block_rows])
        value_heads = split_heads(values_all[start_row : start_row + block_rows])
        key_pos = start_row + jnp.arange(block_rows, dtype=jnp.int32)
        key_doc = doc_row[start_row : start_row + block_rows]
        scores = block_scores(query_heads, key_heads, positions, key_pos, doc_mine, key_doc)
        return (scores, key_heads, value_heads)

    running_max = jnp.full((head_count, block_rows), masked_score, jnp.float32)
    running_sum = zeros_head_rows
    for number in range(seq_count):

        def block_stats(number=number):
            scores = scores_of(number)[0]
            block_max = jnp.max(scores, axis=-1)
            return (block_max, jnp.sum(jnp.exp(scores - block_max[..., None]), axis=-1))

        block_max, block_sum = block_stats()
        new_max = jnp.maximum(running_max, block_max)
        running_sum = running_sum * jnp.exp(running_max - new_max) + block_sum * jnp.exp(
            block_max - new_max
        )
        running_max = new_max
    log_total = running_max + jnp.log(running_sum)
    attended = zeros_heads
    for number in range(seq_count):

        def block_output(number=number):
            scores, key_heads, value_heads = scores_of(number)
            soft_probs = jnp.exp(scores - log_total[..., None]).astype(jnp.bfloat16)
            return jnp.einsum(
                "hqk,khd->qhd", soft_probs, value_heads, preferred_element_type=jnp.float32
            )

        attended = attended + block_output()
    attended_low = attended.reshape(block_rows, model_width).astype(jnp.bfloat16)
    h_one = inputs + jnp.dot(attended_low, whole_proj, preferred_element_type=jnp.float32)
    normed_two, second_pull = jax.vjp(layer_norm, h_one, gain_second, shift_second)
    normed_two_low = normed_two.astype(jnp.bfloat16)
    hidden_pre = jnp.dot(normed_two_low, whole_up, preferred_element_type=jnp.float32) + bias_up
    activated, gelu_pull = jax.vjp(jax.nn.gelu, hidden_pre)
    act_low = activated.astype(jnp.bfloat16)
    h_two = h_one + jnp.dot(act_low, whole_down, preferred_element_type=jnp.float32) + bias_down
    h_two_low = h_two.astype(jnp.bfloat16)
    prev_rows = from_behind(h_two_low[block_rows - 2 :], "seq", 1)
    shifted = jnp.concatenate([prev_rows, h_two_low[: block_rows - 2]], axis=0)
    grouped = shifted.reshape(block_rows // 3, 3 * model_width)
    short_rows = (
        jnp.dot(grouped, whole_pool, preferred_element_type=jnp.float32) + bias_pool
    ).astype(jnp.bfloat16)
    out_rows = out_grad[0]
    grad_pool = outer_sum(grouped, out_rows)
    grad_bias_pool = jnp.sum(out_rows.astype(jnp.float32), axis=0)
    spread_rows = times_transpose(out_rows, whole_pool).reshape(block_rows, model_width)
    returned = from_behind(spread_rows[:2], "seq", -1)
    grad_h_two = jnp.concatenate([spread_rows[2:], returned], axis=0)
    grad_branch = grad_h_two.astype(jnp.bfloat16)
    grad_down = outer_sum(act_low, grad_branch)
    grad_bias_down = jnp.sum(grad_branch.astype(jnp.float32), axis=0)
    grad_act = times_transpose(grad_branch, whole_down)
    grad_hidden = gelu_pull(grad_act)[0].astype(jnp.bfloat16)
    grad_up = outer_sum(normed_two_low, grad_hidden)
    grad_bias_up = jnp.sum(grad_hidden.astype(jnp.float32), axis=0)
    grad_normed_two = times_transpose(grad_hidden, whole_up)
    back_h_one, grad_gain_second, grad_shift_second = second_pull(grad_normed_two)
    grad_h_one = grad_h_two + back_h_one
    grad_attn = grad_h_one.astype(jnp.bfloat16)
    grad_proj = outer_sum(attended_low, grad_attn)
    grad_attended = times_transpose(grad_attn, whole_proj).astype(jnp.bfloat16)
    grad_heads = split_heads(grad_attended)
    row_delta = zeros_head_rows
    value_terms = []
    for number in range(seq_count):

        def block_first(number=number):
            scores, key_heads, value_heads = scores_of(number)
            soft_probs = jnp.exp(scores - log_total[..., None])
            grad_probs = jnp.einsum(
                "qhd,khd->hqk", grad_heads, value_heads, preferred_element_type=jnp.float32
            )
            part_delta = jnp.sum(soft_probs * grad_probs, axis=-1)
            value_grad = jnp.einsum(
                "hqk,qhd->khd",
                soft_probs.astype(jnp.bfloat16),
                grad_heads,
                preferred_element_type=jnp.float32,
            )
            return (part_delta, value_grad.reshape(block_rows, model_width))

        part_delta, value_grad = block_first()
        row_delta = row_delta + part_delta
        value_terms.append(value_grad)
    grad_query = zeros_heads
    key_terms = []
    for number in range(seq_count):

        def block_second(number=number):
            scores, key_heads, value_heads = scores_of(number)
            soft_probs = jnp.exp(scores - log_total[..., None])
            grad_probs = jnp.einsum(
                "qhd,khd->hqk", grad_heads, value_heads, preferred_element_type=jnp.float32
            )
            grad_scores = (soft_probs * (grad_probs - row_delta[..., None])).astype(jnp.bfloat16)
            query_part = jnp.einsum(
                "hqk,khd->qhd", grad_scores, key_heads, preferred_element_type=jnp.float32
            )
            key_part = jnp.einsum(
                "hqk,qhd->khd", grad_scores, query_heads, preferred_element_type=jnp.float32
            )
            return (query_part, key_part.reshape(block_rows, model_width))

        query_part, key_part = block_second()
        grad_query = grad_query + query_part
        key_terms.append(key_part)
    head_scale = HEAD_DIM ** (-0.5)
    grad_keys, grad_values = (
        lax.psum_scatter(
            (jnp.concatenate(key_terms, axis=0) * head_scale).astype(jnp.bfloat16),
            "seq",
            scatter_dimension=0,
            tiled=True,
        ).astype(jnp.float32),
        lax.psum_scatter(
            jnp.concatenate(value_terms, axis=0).astype(jnp.bfloat16),
            "seq",
            scatter_dimension=0,
            tiled=True,
        ).astype(jnp.float32),
    )
    grad_q_pre = query_pull(grad_query.reshape(block_rows, model_width) * head_scale)[0].astype(
        jnp.bfloat16
    )
    grad_k_pre = key_pull(grad_keys)[0].astype(jnp.bfloat16)
    grad_v_pre = grad_values.astype(jnp.bfloat16)
    stacked = jnp.stack([grad_q_pre, grad_k_pre, grad_v_pre])
    grad_qkv = jnp.einsum("td,cte->cde", normed_low, stacked, preferred_element_type=jnp.float32)
    grad_normed = jnp.einsum("cte,cde->td", stacked, whole_qkv, preferred_element_type=jnp.float32)
    back_inputs, grad_gain_first, grad_shift_first = first_pull(grad_normed)
    input_grad = (grad_h_one + back_inputs)[None]
    grad_small = jnp.concatenate(
        [
            grad_gain_first,
            grad_shift_first,
            grad_gain_second,
            grad_shift_second,
            grad_bias_down,
            grad_bias_pool,
            grad_bias_up,
        ]
    )
    all_grads = (grad_qkv, grad_proj, grad_up, grad_down, grad_pool, grad_small)
    shards = (
        lax.psum_scatter(all_grads[0], ("seq", "batch"), scatter_dimension=1, tiled=True),
        lax.psum_scatter(all_grads[1], ("seq", "batch"), scatter_dimension=0, tiled=True),
        lax.psum_scatter(all_grads[2], ("seq", "batch"), scatter_dimension=0, tiled=True),
        lax.psum_scatter(all_grads[3], ("seq", "batch"), scatter_dimension=0, tiled=True),
        lax.psum_scatter(all_grads[4], ("seq", "batch"), scatter_dimension=0, tiled=True),
        lax.psum_scatter(all_grads[5], ("seq", "batch"), scatter_dimension=0, tiled=True),
    )
    local_squares = sum((jnp.sum(portion * portion) for portion in shards))
    grad_norm = jnp.sqrt(lax.psum(local_squares, ("seq", "batch")))
    clip_scale = clip_norm / jnp.maximum(grad_norm, clip_norm)
    masters = (qkv_weight, proj_weight, up_weight, down_weight, pool_weight, small_weight)
    firsts = (qkv_first, proj_first, up_first, down_first, pool_first, small_first)
    seconds = (qkv_second, proj_second, up_second, down_second, pool_second, small_second)
    new_states = []
    for index_kind in range(6):
        step_rate = rate_vector if index_kind == 5 else rate_matrix
        decay_rate = 0.0 if index_kind == 5 else decay_weight
        new_states.append(
            adam_update(
                shards[index_kind],
                firsts[index_kind],
                seconds[index_kind],
                masters[index_kind],
                clip_scale,
                step_rate,
                decay_rate,
            )
        )
    return (
        short_rows[None],
        input_grad,
        grad_norm,
        new_states[0][0],
        new_states[0][1],
        new_states[0][2],
        new_states[1][0],
        new_states[1][1],
        new_states[1][2],
        new_states[2][0],
        new_states[2][1],
        new_states[2][2],
        new_states[3][0],
        new_states[3][1],
        new_states[3][2],
        new_states[4][0],
        new_states[4][1],
        new_states[4][2],
        new_states[5][0],
        new_states[5][1],
        new_states[5][2],
    )


MESH = pl.DeviceIdType.MESH
BF = jnp.bfloat16
F32 = jnp.float32
WIDE = 128
HEADS = 2
LOG2E = math.log2(math.e)
NN = (((1,), (0,)), ((), ()))
NT = (((1,), (1,)), ((), ()))
TN = (((0,), (0,)), ((), ()))
VMEM_LIMIT = 121 * 2**19
PROJ, UP, DOWN, POOL = range(4)
ARRAYS = 4
GELU_C = math.sqrt(2.0 / math.pi)
DOCS = 7
PAD = 16


def dot(a, b, dims=NN):
    return lax.dot_general(a, b, dims, preferred_element_type=F32)


def grid_of(mesh):
    seq, batch = mesh.shape["seq"], mesh.shape["batch"]
    return seq // 2, batch // 2, 2


def fits(mesh):
    seq, batch = mesh.shape["seq"], mesh.shape["batch"]
    return seq == 4 and batch % 2 == 0 and D % (seq * batch * 16) == 0


class Where:
    def __init__(self, nx, nz, ny):
        self.nx, self.nz, self.ny = nx, nz, ny
        self.count, self.batches = 2 * nx, nz * ny
        seq, batch = lax.axis_index("seq"), lax.axis_index("batch")
        self.seq = seq
        self.batch = batch
        self.x, self.c = lax.div(seq, 2), lax.rem(seq, 2)
        self.z, self.y = lax.div(batch, ny), lax.rem(batch, ny)
        self.xo, self.co, self.yo = 1 - self.x, 1 - self.c, 1 - self.y

    def dev(self, x=None, c=None, z=None, y=None):
        x = self.x if x is None else x
        c = self.c if c is None else c
        z = self.z if z is None else z
        y = self.y if y is None else y
        return (x * 2 + c, z * self.ny + y)

    def z_at(self, step):
        return lax.rem(self.z + step, self.nz)

    def seq_at(self, step):
        return lax.rem(self.seq + step, self.count)

    def batch_at(self, step):
        return lax.rem(self.batch + step, self.batches)

    def partner(self, stage):
        return {
            "x": self.dev(x=self.xo),
            "c": self.dev(c=self.co),
            "y": self.dev(y=self.yo),
        }[stage]

    def seq_peers(self):
        return [(self.seq_at(k), self.batch) for k in range(1, self.count)]

    def batch_peers(self):
        return [(self.seq, self.batch_at(k)) for k in range(1, self.batches)]


def remote(src, dst, send, recv, peer):
    return pltpu.make_async_remote_copy(
        src, dst, send, recv, device_id=peer, device_id_type=MESH
    )


class Links:
    def __init__(self):
        self.open = []

    def start(self, copies):
        for copy in copies:
            copy.start()
        self.open += copies
        return copies

    def close(self, copies):
        for copy in copies:
            copy.wait_send()
        self.open = [other for other in self.open if all(other is not copy for copy in copies)]

    def finish(self):
        self.close(list(self.open))


def arrive(copies):
    for copy in copies:
        copy.wait_recv()


class Gather:
    def __init__(self, w, links, fulls, pieces, send, recv):
        self.w, self.links = w, links
        self.fulls, self.pieces, self.send, self.recv = fulls, pieces, send, recv
        self.copies = {}

    def start(self, n, index):
        w = self.w
        a, order, at_rows, at_cols = self.pieces[n]
        stage, done = order[index], order[:index]
        pick = [
            slice(None) if name in done else own
            for name, own in (("x", w.x), ("c", w.c), ("z", w.z), ("y", w.y))
        ]
        block = self.fulls[a].at[pick[0], pick[1], pick[2], pick[3], at_rows, at_cols]
        if stage == "z":
            peers = [(k - 1, w.dev(z=w.z_at(k))) for k in range(1, w.nz)]
        else:
            peers = [(w.nz - 1 + "xyc".index(stage), w.partner(stage))]
        self.copies[n, index] = self.links.start([
            remote(block, block, self.send.at[n, slot], self.recv.at[n, slot], peer)
            for slot, peer in peers
        ])

    def step(self, n, index):
        arrive(self.copies[n, index])
        if index < 3:
            self.start(n, index + 1)


def gather_pieces(shapes):
    def part(a, axis, lo, hi):
        size = shapes[a][axis]
        return slice(size * lo // 4 // 16 * 16, size * hi // 4 // 16 * 16)

    every = slice(None)
    return [
        (PROJ, "zxyc", every, every),
        (UP, "zyxc", every, part(UP, 1, 0, 2)),
        (UP, "zyxc", every, part(UP, 1, 2, 4)),
        (DOWN, "zxyc", part(DOWN, 0, 0, 2), every),
        (DOWN, "zxyc", part(DOWN, 0, 2, 4), every),
        (POOL, "zyxc", part(POOL, 0, 0, 2), every),
        (POOL, "zxyc", part(POOL, 0, 2, 4), every),
    ]


PIECES = 7
GATHER_EARLY = 2
GATHER_STEPS = (
    ((0, 0), (1, 0), (2, 0), (3, 0), (4, 0)),
    ((5, 0),),
    ((6, 0), (0, 1)),
    ((1, 1),),
    ((3, 1),),
    ((2, 1),),
    ((5, 1),),
    ((4, 1), (0, 2)),
    ((6, 1), (0, 3)),
    ((3, 2),),
    ((1, 2), (3, 3)),
    ((4, 2), (1, 3)),
    ((2, 2), (4, 3), (2, 3)),
    ((6, 2), (5, 2)),
    ((6, 3), (5, 3)),
)


class Scatter:
    ORDERS = ("yzx", "zyx", "yxz", "yzx")

    def __init__(self, w, links, fulls, got, send, recv):
        self.w, self.links = w, links
        self.sums = [full.at[:, 0] for full in fulls]
        self.c_in = [full.at[:, 1] for full in fulls]
        self.got = got
        self.send, self.recv = send, recv
        self.copies, self.make = {}, {}

    @classmethod
    def shapes(cls, a, shard, nx, nz, ny):
        sizes = {"x": nx, "z": nz, "y": ny}
        found, rest = [], "xzy"
        for stage in cls.ORDERS[a]:
            rest = rest.replace(stage, "")
            lead = (nz - 1,) if stage == "z" else ()
            found.append(lead + tuple(sizes[n] for n in rest) + shard)
        return found

    def pick(self, a, index, at):
        order = self.ORDERS[a]
        own = {"x": self.w.x, "z": self.w.z, "y": self.w.y}
        return tuple(
            at if n == order[index] else (own[n] if n in order[:index] else slice(None))
            for n in "xzy"
        )

    def begin(self, a, make):
        w = self.w
        self.make[a] = make
        shape = self.sums[a].shape[1:]
        for x_of in range(w.nx):
            self.sums[a][x_of] = make(x_of * 2 + w.co).reshape(shape).astype(BF)
        self.copies[a, "c"] = self.links.start([
            remote(self.sums[a], self.c_in[a], self.send.at[a, 0], self.recv.at[a, 0],
                   w.partner("c"))
        ])

    def start(self, a, index):
        w, stage = self.w, self.ORDERS[a][index]
        into = self.got[index][a]
        if stage == "z":
            moves = [
                (w.z_at(k), into.at[k - 1], 2 + k, w.dev(z=w.z_at(k))) for k in range(1, w.nz)
            ]
        else:
            moves = [(w.xo if stage == "x" else w.yo, into, "xy".index(stage) + 1,
                      w.partner(stage))]
        self.copies[a, index] = self.links.start([
            remote(self.sums[a].at[self.pick(a, index, at)], to, self.send.at[a, slot],
                   self.recv.at[a, slot], peer)
            for at, to, slot, peer in moves
        ])

    def total(self, a, index):
        w, stage = self.w, self.ORDERS[a][index]
        arrive(self.copies[a, index])
        here = self.pick(a, index, {"x": w.x, "z": w.z, "y": w.y}[stage])
        into = self.got[index][a]
        value = self.sums[a][here].astype(F32)
        if stage == "z":
            for k in range(w.nz - 1):
                value = value + into[k].astype(F32)
        else:
            value = value + into[...].astype(F32)
        return here, value

    def step(self, a, index):
        w = self.w
        if index == 0:
            arrive(self.copies[a, "c"])
            self.links.close(self.copies[a, "c"])
            shape = self.sums[a].shape[1:]
            for x_of in range(w.nx):
                value = self.make[a](x_of * 2 + w.c).reshape(shape)
                self.sums[a][x_of] = (value + self.c_in[a][x_of].astype(F32)).astype(BF)
        else:
            here, value = self.total(a, index - 1)
            self.sums[a][here] = value.astype(BF)
        self.start(a, index)

    def last(self, a):
        return self.total(a, 2)[1]


def norm_stats(values):
    center = values - jnp.mean(values, axis=-1, keepdims=True)
    spread = jnp.mean(center * center, axis=-1, keepdims=True)
    scale = lax.rsqrt(spread + norm_eps)
    return center * scale, scale


def norm_back(grad, unit, scale, gain):
    inner = grad * gain
    mean_one = jnp.mean(inner, axis=-1, keepdims=True)
    mean_two = jnp.mean(inner * unit, axis=-1, keepdims=True)
    back = scale * (inner - mean_one - unit * mean_two)
    return back, jnp.sum(grad * unit, axis=0, keepdims=True), jnp.sum(grad, axis=0, keepdims=True)


def swap_halves(values):
    lane = lax.broadcasted_iota(jnp.int32, values.shape, 1)
    return jnp.where(
        lax.rem(lane, HEAD_DIM) < HEAD_DIM // 2,
        pltpu.roll(values, WIDE - HEAD_DIM // 2, 1),
        pltpu.roll(values, HEAD_DIM // 2, 1),
    )


def in_head(lane, h):
    return (lane >= h * HEAD_DIM) & (lane < (h + 1) * HEAD_DIM)


def with_feats(base, lane, h, vector):
    one = vector.astype(BF).astype(F32)
    two = (vector - one).astype(BF).astype(F32)
    first = (1 - h) * HEAD_DIM + 8
    for n, term in enumerate((one, two, vector - one - two)):
        base = jnp.where(lane == first + n, term, base)
    return base


def document_edges(docs):
    feat = lax.rem(lax.broadcasted_iota(jnp.int32, (1, WIDE), 1), HEAD_DIM)
    lo = jnp.zeros((1, WIDE), jnp.int32)
    hi = jnp.zeros((1, WIDE), jnp.int32)
    below = jnp.zeros((1, 1), jnp.int32)
    for d in range(DOCS):
        upto = jnp.sum(jnp.where(docs <= d, 1, 0), axis=1, keepdims=True)
        lo = jnp.where(feat == d, below, lo)
        hi = jnp.where(feat == d, upto, hi)
        below = upto
    return lo, hi


def layer_buffers(nx, nz, ny, rows, ff, shapes):
    count, block = 2 * nx, rows + PAD
    batches = nz * ny
    vmem = lambda shape, kind=BF: pltpu.VMEM(shape, kind)
    wide = 3 * WIDE
    shard = shapes[0][0]
    scatter = [Scatter.shapes(a, s, nx, nz, ny) for a, s in enumerate(shapes)]
    named = dict(
        fulls=[vmem((nx, 2, nz, ny) + s) for s in shapes],
        part=vmem((count, 3, shard, WIDE)),
        wq=vmem((count, nz, ny, 3, shard, WIDE)),
        small_seq=vmem((count, 16, D)),
        small_all=vmem((nz + ny, 16, D)),
        small=vmem((16, D), F32),
        wide_row=vmem((8, 2 * D), F32),
        tok_all=vmem((count, rows, D)),
        normed=vmem((count, rows, D)),
        ext=vmem((3, HEADS, count * block, WIDE)),
        o_ref=vmem((count, block, WIDE), F32),
        o_low=vmem((count, block, WIDE)),
        att=vmem((count, rows, WIDE)),
        h_one=vmem((rows, D), F32),
        dh_two=vmem((D // WIDE * block, WIDE), F32),
        buf=[vmem((count * block, WIDE), F32) for _ in range(3)],
        normed_two=vmem((rows, D)),
        act=vmem((rows, ff)),
        d_hidden=vmem((rows, ff)),
        d_branch=vmem((rows, D)),
        d_attn=vmem((rows, D)),
        grouped=vmem((rows // 3, 3 * D)),
        edge=vmem((4, 16, D)),
        do_send=vmem((count, rows, WIDE)),
        dq_turned=vmem((WIDE, count * block), F32),
        do_ext=vmem((HEADS, count * block, WIDE)),
        stacked=vmem((rows, wide)),
        g_qkv=vmem((D, wide), F32),
        x_in=vmem((rows, D)),
        gq_out=vmem((batches, count, shard, wide)),
        gq_in=vmem((batches, count, shard, wide)),
        gq_seq=vmem((count, shard, wide)),
        gq_got=vmem((count, shard, wide)),
        small_grad=vmem((16, D), F32),
        sg_seq=vmem((count, 16, D), F32),
        sg_all=vmem((batches, 16, D), F32),
        late_seq=vmem((count, 8, WIDE), F32),
        late_all=vmem((batches, 8, WIDE), F32),
        norm_seq=vmem((count, 8, WIDE), F32),
        norm_all=vmem((batches, 8, WIDE), F32),
        got_one=[vmem(found[0]) for found in scatter],
        got_two=[vmem(found[1]) for found in scatter],
        got_three=[vmem(found[2]) for found in scatter],
    )
    sems = dict(
        gather=(PIECES, nz + 2), scatter=(ARRAYS, nz + 2), tok=(7,), part=(count - 1,),
        wq=(nz + 1,), small_seq=(count - 1,), small_all=(nz + 1,), edge=(2,),
        o=(count, 2), do=(count - 1,), dn=(2,), x=(1,), gq=(batches - 1,), gq_seq=(count - 1,),
        sg_seq=(count - 1,), sg_all=(batches - 1,), late_seq=(count - 1,),
        late_all=(batches - 1,), norm_seq=(count - 1,),
        norm_all=(batches - 1,),
    )
    for name, shape in sems.items():
        named["sem_" + name] = [pltpu.SemaphoreType.DMA(shape) for _ in range(2)]
    named["ready"] = pltpu.SemaphoreType.REGULAR
    named["free"] = pltpu.SemaphoreType.REGULAR
    return named


SWEEP_STEPS = (
    ((DOWN, 1),),
    ((POOL, 1), (PROJ, 1)),
    ((UP, 1), (DOWN, 2)),
    (),
)


class Bag:
    def __init__(self, template, refs):
        refs = list(refs)
        for name, value in template.items():
            if isinstance(value, list):
                setattr(self, name, [refs.pop(0) for _ in value])
            else:
                setattr(self, name, refs.pop(0))


def layer_kernel(nx, nz, ny, template, tokens, doc_ids, out_grad, qkv_w, proj_w, up_w, down_w,
                 pool_w, small_in, turn, offset, short_out, input_grad, total_qkv, total_proj,
                 total_up, total_down, total_pool, total_small, norm_out, *scratch):
    w = Where(nx, nz, ny)
    b = Bag(template, scratch)
    links = Links()
    rows = tokens.shape[0]
    block = rows + PAD
    count, batches = w.count, w.batches
    pools = rows // 3
    sub = rows // 3
    tiles = D // WIDE
    own = (w.x, w.c, w.z, w.y)

    barrier = pltpu.get_barrier_semaphore()
    peers = w.seq_peers() + w.batch_peers()
    for peer in peers:
        pl.semaphore_signal(barrier, inc=1, device_id=peer, device_id_type=MESH)
    own_small = small_in.shape[1]
    small_first = (w.seq * batches + w.batch) * own_small
    small_row, small_lane = lax.div(small_first, D), lax.rem(small_first, D)
    b.wide_row[...] = jnp.zeros(b.wide_row.shape, F32)
    b.wide_row[0:1, 0:own_small] = small_in[...]
    moved = pltpu.roll(b.wide_row[...], small_lane, 1)
    b.small[...] = jnp.zeros(b.small.shape, F32)
    b.small[pl.ds(small_row, 1)] = moved[0:1, 0:D]
    b.small[pl.ds(small_row + 1, 1)] = moved[0:1, D:]
    b.small_seq[w.seq] = b.small[...].astype(BF)
    for d in range(count):
        b.part[d] = qkv_w[:, :, d * WIDE : (d + 1) * WIDE].astype(BF)
    b.edge[0] = out_grad[0:16]
    shards = (proj_w, up_w, down_w, pool_w)
    for shard, full in zip(shards, b.fulls):
        full[own] = shard[...].astype(BF)
    gather = Gather(w, links, b.fulls, gather_pieces([s.shape for s in shards]), *b.sem_gather)
    pl.semaphore_wait(barrier, len(peers))

    send, recv = b.sem_tok
    mine = b.tok_all.at[w.seq]

    def piece(ref, n):
        return ref.at[pl.ds(n * sub, sub)]

    small_a = links.start([
        remote(b.small_seq.at[w.seq], b.small_seq.at[w.seq], b.sem_small_seq[0].at[k],
               b.sem_small_seq[1].at[k], peer)
        for k, peer in enumerate(w.seq_peers())
    ])
    part_a = links.start([
        remote(b.part.at[w.seq_at(k + 1)], b.wq.at[w.seq, w.z, w.y], b.sem_part[0].at[k],
               b.sem_part[1].at[k], peer)
        for k, peer in enumerate(w.seq_peers())
    ])
    tok_x = links.start([
        remote(piece(tokens, n), piece(mine, n), send.at[n], recv.at[n], w.partner("x"))
        for n in range(3)
    ])
    for n in range(GATHER_EARLY):
        gather.start(n, 0)
    tok_c = links.start([remote(tokens, mine, send.at[3], recv.at[3], w.partner("c"))])
    links.start([
        remote(b.edge.at[0], b.edge.at[1], b.sem_edge[0].at[0], b.sem_edge[1].at[0],
               (w.seq_at(count - 1), w.batch))
    ])
    grad_edge = links.open[-1:]
    b.wq[w.seq, w.z, w.y] = b.part[w.seq]
    lo, hi = document_edges(doc_ids[...])
    arrive(small_a)
    total = b.small_seq[0].astype(F32)
    for n in range(1, count):
        total = total + b.small_seq[n].astype(F32)
    b.small_all[w.z] = total.astype(BF)
    z_peers = [w.dev(z=w.z_at(k)) for k in range(1, nz)]
    small_b = links.start([
        remote(b.small_all.at[w.z], b.small_all.at[w.z], b.sem_small_all[0].at[k],
               b.sem_small_all[1].at[k], peer)
        for k, peer in enumerate(z_peers)
    ])
    arrive(part_a)
    part_b = links.start([
        remote(b.wq.at[:, w.z, w.y], b.wq.at[:, w.z, w.y], b.sem_wq[0].at[k],
               b.sem_wq[1].at[k], peer)
        for k, peer in enumerate(z_peers)
    ])
    for n in range(GATHER_EARLY, PIECES):
        gather.start(n, 0)
    b.tok_all[w.seq] = tokens[...]

    lane_row = lax.broadcasted_iota(jnp.int32, (1, WIDE), 1)
    feat_row = lax.rem(lane_row, HEAD_DIM)
    pad_lane = lax.broadcasted_iota(jnp.int32, (PAD, WIDE), 1)
    for h in range(HEADS):
        for n in range(count):
            pad = pl.ds(n * block + rows, PAD)
            b.ext[0, h, pad] = jnp.zeros((PAD, WIDE), BF)
            masks = ~in_head(pad_lane, h) & (lax.rem(pad_lane, HEAD_DIM) < DOCS)
            b.ext[1, h, pad] = jnp.where(masks, masked_score, 0.0).astype(BF)
            b.ext[2, h, pad] = jnp.zeros((PAD, WIDE), BF)
            b.do_ext[h, pad] = jnp.zeros((PAD, WIDE), BF)

    arrive(small_b)
    total = b.small_all[0].astype(F32)
    for n in range(1, nz):
        total = total + b.small_all[n].astype(F32)
    b.small_all[nz + w.y] = total.astype(BF)
    small_c = links.start([
        remote(b.small_all.at[nz + w.y], b.small_all.at[nz + w.y], b.sem_small_all[0].at[nz],
               b.sem_small_all[1].at[nz], w.partner("y"))
    ])
    arrive(part_b)
    part_c = links.start([
        remote(b.wq.at[:, :, w.y], b.wq.at[:, :, w.y], b.sem_wq[0].at[nz], b.sem_wq[1].at[nz],
               w.partner("y"))
    ])
    arrive(small_c)
    b.small[...] = b.small_all[nz].astype(F32) + b.small_all[nz + 1].astype(F32)
    small = b.small
    arrive(part_c)

    def qkv_weight(n):
        return b.wq[:, :, :, n].reshape(D, WIDE)

    def turning(of_block, r0):
        cos_in, sin_in = turn[0, pl.ds(r0, sub)], turn[1, pl.ds(r0, sub)]
        cos_of, sin_of = offset[0, pl.ds(of_block, 1)], offset[1, pl.ds(of_block, 1)]
        return cos_in * cos_of - sin_in * sin_of, sin_in * cos_of + cos_in * sin_of

    def project(of_block):
        weight = jnp.concatenate([qkv_weight(n) for n in range(3)], axis=1)

        def body(n, _):
            r0 = pl.multiple_of(n * sub, 16)
            unit, _ = norm_stats(b.tok_all[of_block, pl.ds(r0, sub)].astype(F32))
            normed = (unit * small[0:1] + small[1:2]).astype(BF)
            b.normed[of_block, pl.ds(r0, sub)] = normed
            qkv = dot(normed, weight)
            cosine, sine = turning(of_block, r0)
            parts = [qkv[:, m * WIDE : (m + 1) * WIDE] for m in range(3)]
            for m in range(2):
                parts[m] = parts[m] * cosine + swap_halves(parts[m]) * sine
            parts[0] = parts[0] * (LOG2E * HEAD_DIM ** -0.5)
            place = lax.broadcasted_iota(jnp.int32, (sub, WIDE), 0) + (of_block * rows + r0)
            lane = lax.broadcasted_iota(jnp.int32, (sub, WIDE), 1)
            same = (place >= lo) & (place < hi)
            ones = jnp.where((feat_row >= 8) & (feat_row < 11), 1.0, 0.0)
            q_feat = jnp.where(same, 1.0, 0.0)
            k_feat = jnp.where(feat_row < DOCS, jnp.where(same, 0.0, masked_score), ones)
            at = pl.ds(pl.multiple_of(of_block * block + r0, 16), sub)
            for h in range(HEADS):
                for m, feats in enumerate((q_feat, k_feat, 1.0)):
                    b.ext[m, h, at] = jnp.where(in_head(lane, h), parts[m], feats).astype(BF)
            return 0

        lax.fori_loop(0, 3, body, 0)

    pending = list(GATHER_STEPS)

    def advance():
        for n, index in pending.pop(0):
            gather.step(n, index)

    project(w.seq)
    advance()
    arrive(tok_c)
    project(w.x * 2 + w.co)
    advance()
    theirs = b.tok_all.at[w.xo * 2 + w.c]
    passed = []
    for n in range(3):
        arrive(tok_x[n : n + 1])
        passed += links.start([
            remote(piece(theirs, n), piece(theirs, n), send.at[4 + n], recv.at[4 + n],
                   w.partner("c"))
        ])
    project(w.xo * 2 + w.c)
    advance()
    arrive(passed)
    project(w.xo * 2 + w.co)
    advance()

    half_rows = (block // 2, rows - block // 2)

    def attend(of_block, half):
        size = block // 2
        r0 = of_block * block + half * size
        n = min(count * block, -(-(r0 + size) // 256) * 256)
        m0 = (r0 // 128) * 128
        lane = lax.broadcasted_iota(jnp.int32, (size, WIDE), 1)
        at_row = lax.broadcasted_iota(jnp.int32, (size, n - m0), 0) + r0
        at_col = lax.broadcasted_iota(jnp.int32, (size, n - m0), 1) + m0
        queries = [b.ext[0, h, pl.ds(r0, size)] for h in range(HEADS)]
        scores = [dot(queries[h], b.ext[1, h, :n], NT) for h in range(HEADS)]
        outs = []
        for h in range(HEADS):
            s = scores[h]
            tail = jnp.where(at_col <= at_row, s[:, m0:], masked_score)
            s = jnp.concatenate([s[:, :m0], tail], axis=1) if m0 else tail
            top = jnp.max(s, axis=1, keepdims=True)
            p = jnp.exp2(s - top).astype(BF)
            sums = dot(p, b.ext[2, h, :n])
            outs.append(sums / pltpu.roll(sums, HEAD_DIM, 1))
            log_total = top + jnp.log2(sums)
            q_new = with_feats(queries[h].astype(F32), lane, h, -log_total)
            b.ext[0, h, pl.ds(r0, size)] = q_new.astype(BF)
        both = jnp.where(lane < HEAD_DIM, outs[0], outs[1])
        b.o_ref[of_block, pl.ds(half * size, size)] = both
        b.o_low[of_block, pl.ds(half * size, size)] = both.astype(BF)

    def o_copy(of_block, half):
        at = pl.ds(half * (block // 2), half_rows[half])
        return remote(b.o_low.at[of_block, at], b.att.at[w.seq, at], b.sem_o[0].at[of_block, half],
                      b.sem_o[1].at[w.seq, half], (of_block, w.batch))

    for of_block in range(count):
        for half in range(2):
            attend(of_block, half)

            @pl.when(w.seq != of_block)
            def _(of_block=of_block, half=half):
                o_copy(of_block, half).start()

            advance()

        @pl.when(w.seq == of_block)
        def _(of_block=of_block):
            b.att[of_block] = b.o_low[of_block, 0:rows]

    advance()


    first, last = w.seq == 0, w.seq == count - 1

    def lay(ref, start, value):
        for n in range(tiles):
            ref[pl.ds(n * block + start, value.shape[0])] = value[:, n * WIDE : (n + 1) * WIDE]

    def whole(ref, start):
        return jnp.concatenate(
            [ref[pl.ds(n * block + start, rows)] for n in range(tiles)], axis=1
        )

    def add(ref, value):
        for n in range(tiles):
            ref[pl.ds(n * block, rows)] += value[:, n * WIDE : (n + 1) * WIDE]

    sum_one, sum_two, h_two = b.buf
    sum_one[...] = jnp.zeros(sum_one.shape, F32)
    sum_two[...] = jnp.zeros(sum_two.shape, F32)

    for k in range(1, count):
        of = w.seq_at(k)
        for half in range(2):
            at = pl.ds(half * (block // 2), half_rows[half])
            remote(b.att.at[of, at], b.att.at[of, at], b.sem_o[0].at[of, half],
                   b.sem_o[1].at[of, half], (of, w.batch)).wait_recv()
    attended = jnp.concatenate([b.att[n] for n in range(count)], axis=1)
    b.h_one[...] = tokens[...].astype(F32) + dot(attended, b.fulls[PROJ][...].reshape(D, D))
    unit, _ = norm_stats(b.h_one[...])
    b.normed_two[...] = (unit * small[2:3] + small[3:4]).astype(BF)
    advance()
    part = b.act.shape[1] // count

    def parts_of(n):
        cols = pl.ds(pl.multiple_of(n * part, part), part)
        up = b.fulls[UP][:, :, :, :, :, cols].reshape(D, part)
        down = b.fulls[DOWN][lax.div(n, 2), lax.rem(n, 2)].reshape(part, D)
        return cols, up, down

    def feed(n, _):
        cols, up, down = parts_of(n)
        hidden = dot(b.normed_two[...], up) + small[pl.ds(6 + n, 1)]
        square = hidden * hidden
        bend = jnp.tanh(GELU_C * hidden * (1.0 + 0.044715 * square))
        half = 0.5 * (1.0 + bend)
        act_low = (hidden * half).astype(BF)
        b.act[:, cols] = act_low
        slope = half + 0.5 * hidden * (1.0 - bend * bend) * (
            GELU_C * (1.0 + 3 * 0.044715 * square)
        )
        b.d_hidden[:, cols] = slope.astype(BF)
        add(sum_one, dot(act_low, down))
        return 0

    lax.fori_loop(0, count, feed, 0)
    h_low = (b.h_one[...] + whole(sum_one, 0) + small[4:5]).astype(BF)
    lay(h_two, 8, h_low.astype(F32))
    b.edge[2] = h_low[rows - 16 :]
    row_edge = links.start([
        remote(b.edge.at[2], b.edge.at[3], b.sem_edge[0].at[1], b.sem_edge[1].at[1],
               (w.seq_at(1), w.batch))
    ])
    advance()

    pool = b.fulls[POOL][...].reshape(3 * D, D)
    g_low = out_grad[...]
    spread = dot(g_low, pool, NT)
    for k in range(3):
        for n in range(tiles):
            at = k * D + n * WIDE
            b.dh_two[pl.ds(n * block + 6 + k, pools, stride=3)] = spread[:, at : at + WIDE]
    arrive(grad_edge)
    beyond = jnp.where(last, 0.0, dot(b.edge[1], pool, NT))
    lay(b.dh_two, 8 + rows - 2, beyond[0:1, 0:D])
    lay(b.dh_two, 8 + rows - 1, beyond[0:1, D : 2 * D])
    b.d_branch[...] = whole(b.dh_two, 8).astype(BF)
    small_grad = b.small_grad
    small_grad[...] = jnp.zeros(small_grad.shape, F32)
    small_grad[4:5] = jnp.sum(b.d_branch[...].astype(F32), axis=0, keepdims=True)
    small_grad[5:6] = jnp.sum(g_low.astype(F32), axis=0, keepdims=True)
    links.finish()
    for of_block in range(count):
        for half in range(2):

            @pl.when(w.seq != of_block)
            def _(of_block=of_block, half=half):
                o_copy(of_block, half).wait_send()

    for peer in w.seq_peers():
        pl.semaphore_signal(b.free, inc=1, device_id=peer, device_id_type=MESH)

    def feed_back(n, _):
        cols, up, down = parts_of(n)
        slope = b.d_hidden[:, cols].astype(F32)
        d_low = (dot(b.d_branch[...], down, NT) * slope).astype(BF)
        b.d_hidden[:, cols] = d_low
        small_grad[pl.ds(6 + n, 1)] = jnp.sum(d_low.astype(F32), axis=0, keepdims=True)
        add(sum_two, dot(d_low, up, NT))
        return 0

    lax.fori_loop(0, count, feed_back, 0)
    unit, scale = norm_stats(b.h_one[...])
    back, small_grad[2:3], small_grad[3:4] = norm_back(whole(sum_two, 0), unit, scale, small[2:3])
    grad_one = whole(b.dh_two, 8) + back
    b.h_one[...] = grad_one
    b.d_attn[...] = grad_one.astype(BF)
    spread_back = dot(b.d_attn[...], b.fulls[PROJ][...].reshape(D, D), NT).astype(BF)
    for n in range(count):
        b.do_send[n] = spread_back[:, n * WIDE : (n + 1) * WIDE]
    do_all = b.o_low
    pl.semaphore_wait(b.free, count - 1)
    given = links.start([
        remote(b.do_send.at[w.seq_at(k + 1)], do_all.at[w.seq, 0:rows], b.sem_do[0].at[k],
               b.sem_do[1].at[k], peer)
        for k, peer in enumerate(w.seq_peers())
    ])
    do_all[w.seq, 0:rows] = b.do_send[w.seq]
    b.sg_seq[w.seq] = small_grad[...]
    sg = links.start([
        remote(b.sg_seq.at[w.seq], b.sg_seq.at[w.seq], b.sem_sg_seq[0].at[k],
               b.sem_sg_seq[1].at[k], peer)
        for k, peer in enumerate(w.seq_peers())
    ])

    def tell_core():
        pl.semaphore_signal(b.ready, inc=1, device_id=w.partner("c"), device_id_type=MESH)
        pl.semaphore_wait(b.ready, 1)

    tell_core()
    scatter = Scatter(w, links, b.fulls, (b.got_one, b.got_two, b.got_three), *b.sem_scatter)

    def columns(ref):
        width = ref.shape[1] // count
        return lambda n: ref[:, pl.ds(pl.multiple_of(n * width, WIDE), width)]

    of_act, of_grouped, of_normed = columns(b.act), columns(b.grouped), columns(b.normed_two)
    scatter.begin(DOWN, lambda n: dot(of_act(n), b.d_branch[...], TN))
    scatter.begin(UP, lambda n: dot(of_normed(n), b.d_hidden[...], TN))
    scatter.step(DOWN, 0)
    arrive(row_edge)
    before = jnp.where(first, 0.0, b.edge[3].astype(F32))
    lay(h_two, 0, before[8:16])
    for k in range(3):
        for n in range(tiles):
            at = k * D + n * WIDE
            rows_of = h_two[pl.ds(n * block + 6 + k, pools, stride=3)]
            b.grouped[:, at : at + WIDE] = rows_of.astype(BF)
    short_out[...] = (dot(b.grouped[...], pool) + small[5:6]).astype(BF)
    tell_core()
    scatter.begin(POOL, lambda n: dot(of_grouped(n), g_low, TN))
    scatter.begin(PROJ, lambda n: dot(b.att[n], b.d_attn[...], TN))
    scatter.step(UP, 0)
    scatter.step(POOL, 0)
    scatter.step(PROJ, 0)

    def prepare(of_block):
        def body(n, _):
            r0 = pl.multiple_of(n * sub, 16)
            lane = lax.broadcasted_iota(jnp.int32, (sub, WIDE), 1)
            grad = do_all[of_block, pl.ds(r0, sub)].astype(F32)
            terms = grad * b.o_ref[of_block, pl.ds(r0, sub)]
            at = pl.ds(pl.multiple_of(of_block * block + r0, 16), sub)
            for h in range(HEADS):
                mine = in_head(lane, h)
                delta = jnp.sum(jnp.where(mine, terms, 0.0), axis=1, keepdims=True)
                base = jnp.where(mine, grad, 0.0)
                b.do_ext[h, at] = with_feats(base, lane, h, -delta).astype(BF)
            return 0

        lax.fori_loop(0, 3, body, 0)

    arrive(given)
    for n in range(count):
        prepare(n)
    dq, dk, dv = b.buf
    for ref in b.buf:
        ref[...] = jnp.zeros(ref.shape, F32)
    b.g_qkv[...] = jnp.zeros(b.g_qkv.shape, F32)
    b.dq_turned[...] = jnp.zeros(b.dq_turned.shape, F32)

    def pair(q_first, k_first, size, on_diagonal):
        at_q = pl.ds(pl.multiple_of(q_first, WIDE), size)
        at_k = pl.ds(pl.multiple_of(k_first, WIDE), size)
        probs = [dot(b.ext[1, h, at_k], b.ext[0, h, at_q], NT) for h in range(HEADS)]
        slopes = [dot(b.ext[2, h, at_k], b.do_ext[h, at_q], NT) for h in range(HEADS)]
        found = []
        for h in range(HEADS):
            p = jnp.exp2(probs[h])
            if on_diagonal:
                keys = lax.broadcasted_iota(jnp.int32, (size, size), 0)
                queries = lax.broadcasted_iota(jnp.int32, (size, size), 1)
                p = jnp.where(keys <= queries, p, 0.0)
            ds = (p * slopes[h]).astype(BF)
            found.append((dot(b.ext[1, h, at_k], ds, TN), dot(ds, b.ext[0, h, at_q]),
                          dot(p.astype(BF), b.do_ext[h, at_q])))
        lane = lax.broadcasted_iota(jnp.int32, (size, WIDE), 1)
        for ref, zero, one in zip((dk, dv), *[f[1:] for f in found]):
            ref[at_k] += jnp.where(lane < HEAD_DIM, zero, one)
        row = lax.broadcasted_iota(jnp.int32, (WIDE, size), 0)
        b.dq_turned[:, at_q] += jnp.where(row < HEAD_DIM, found[0][0], found[1][0])

    backs = (HEAD_DIM ** -0.5, 1.0 / LOG2E, 1.0)

    def dn_copy(turn_of):
        n = turn_of // 2
        return remote(b.tok_all.at[n], b.tok_all.at[2 + n], b.sem_dn[0].at[n], b.sem_dn[1].at[n],
                      w.partner("c"))

    def complete(turn_of, of_block):
        span = pl.ds(pl.multiple_of(of_block * block, WIDE), block)
        dq[span] = b.dq_turned[:, span].T

        def body(n, _):
            r0 = pl.multiple_of(n * sub, 16)
            cosine, sine = turning(of_block, r0)
            at = pl.ds(pl.multiple_of(of_block * block + r0, 16), sub)
            for m, ref in enumerate(b.buf):
                value = ref[at] * backs[m]
                if m < 2:
                    value = value * cosine - swap_halves(value) * sine
                b.stacked[pl.ds(r0, sub), m * WIDE : (m + 1) * WIDE] = value.astype(BF)
            return 0

        lax.fori_loop(0, 3, body, 0)
        weight = jnp.concatenate([qkv_weight(n) for n in range(3)], axis=1)
        b.g_qkv[...] += dot(b.normed[of_block], b.stacked[...], TN)
        back = dot(b.stacked[...], weight, NT)
        keeps = lax.rem(of_block, 2) == w.c

        @pl.when(keeps)
        def _():
            lay(b.dh_two, 0, back)

        @pl.when(jnp.logical_not(keeps))
        def _():
            b.tok_all[turn_of // 2] = back.astype(BF)
            dn_copy(turn_of).start()

    def summed(turn_of):
        dn_copy(turn_of).wait_recv()
        return whole(b.dh_two, 0) + b.tok_all[2 + turn_of // 2].astype(F32)

    down_first = w.x == 0
    x_copy = []
    for turn_of in range(count):
        outer = jnp.where(down_first, count - 1 - turn_of, turn_of)
        pair(outer * block, outer * block, block, True)

        def inner(n, _, outer=outer, turn_of=turn_of):
            other = jnp.where(down_first, n, turn_of + 1 + n)
            pair(jnp.where(down_first, outer, other) * block,
                 jnp.where(down_first, other, outer) * block, block, False)
            return 0

        if turn_of < count - 1:
            lax.fori_loop(0, count - 1 - turn_of, inner, 0)
        complete(turn_of, outer)
        if turn_of == count // 2 - 1:
            b.d_attn[...] = summed(turn_of).astype(BF)
            x_copy = links.start([
                remote(b.d_attn, b.x_in, b.sem_x[0].at[0], b.sem_x[1].at[0], w.partner("x"))
            ])
        for a, index in SWEEP_STEPS[turn_of]:
            scatter.step(a, index)
        if turn_of == 2:
            arrive(sg)
            total = b.sg_seq[0]
            for n in range(1, count):
                total = total + b.sg_seq[n]
            b.sg_all[w.batch] = total
            sg = links.start([
                remote(b.sg_all.at[w.batch], b.sg_all.at[w.batch], b.sem_sg_all[0].at[k],
                       b.sem_sg_all[1].at[k], peer)
                for k, peer in enumerate(w.batch_peers())
            ])

    def gather_squares(squares, total):
        flat = jnp.sum((total * total).reshape(-1, 8, total.shape[-1]), axis=0)
        for n in range(flat.shape[1] // WIDE):
            squares = squares + flat[:, n * WIDE : (n + 1) * WIDE]
        return squares

    for n in range(batches):
        z_of, y_of = n // ny, n % ny
        rows_of = b.g_qkv[...].reshape(count, nz, ny, -1, 3 * WIDE)[:, z_of, y_of]
        b.gq_out[n] = rows_of.astype(BF)
    gq = links.start([
        remote(b.gq_out.at[w.batch_at(k + 1)], b.gq_in.at[w.batch], b.sem_gq[0].at[k],
               b.sem_gq[1].at[k], peer)
        for k, peer in enumerate(w.batch_peers())
    ])
    b.gq_in[w.batch] = b.gq_out[w.batch]
    for a in (POOL, UP, PROJ):
        scatter.step(a, 2)

    grad_normed = summed(count - 1)
    arrive(x_copy)
    grad_normed = grad_normed + b.x_in[...].astype(F32)
    unit, scale = norm_stats(tokens[...].astype(F32))
    back, small_grad[0:1], small_grad[1:2] = norm_back(grad_normed, unit, scale, small[0:1])
    input_grad[...] = b.h_one[...] + back
    late = jnp.concatenate(
        [small_grad[r : r + 1, n * WIDE : (n + 1) * WIDE] for r in range(2) for n in range(tiles)],
        axis=0,
    )
    b.late_seq[w.seq] = late
    late_sum = links.start([
        remote(b.late_seq.at[w.seq], b.late_seq.at[w.seq], b.sem_late_seq[0].at[k],
               b.sem_late_seq[1].at[k], peer)
        for k, peer in enumerate(w.seq_peers())
    ])
    arrive(gq)
    total = b.gq_in[0].astype(F32)
    for n in range(1, batches):
        total = total + b.gq_in[n].astype(F32)
    b.gq_seq[...] = total.astype(BF)
    squares = gather_squares(jnp.zeros((8, WIDE), F32), total)
    gq = links.start([
        remote(b.gq_seq.at[w.seq_at(k + 1)], b.gq_got.at[w.seq], b.sem_gq_seq[0].at[k],
               b.sem_gq_seq[1].at[k], peer)
        for k, peer in enumerate(w.seq_peers())
    ])
    b.gq_got[w.seq] = b.gq_seq[w.seq]
    arrive(late_sum)
    total = b.late_seq[0]
    for n in range(1, count):
        total = total + b.late_seq[n]
    b.late_all[w.batch] = total
    late_sum = links.start([
        remote(b.late_all.at[w.batch], b.late_all.at[w.batch], b.sem_late_all[0].at[k],
               b.sem_late_all[1].at[k], peer)
        for k, peer in enumerate(w.batch_peers())
    ])
    totals = (total_proj, total_up, total_down, total_pool)
    for a in (DOWN, UP, POOL, PROJ):
        total = scatter.last(a)
        totals[a][...] = total
        squares = gather_squares(squares, total)
    b.norm_seq[w.seq] = squares
    norm = links.start([
        remote(b.norm_seq.at[w.seq], b.norm_seq.at[w.seq], b.sem_norm_seq[0].at[k],
               b.sem_norm_seq[1].at[k], peer)
        for k, peer in enumerate(w.seq_peers())
    ])
    arrive(gq)
    for n in range(3):
        total = jnp.concatenate(
            [b.gq_got[m, :, n * WIDE : (n + 1) * WIDE].astype(F32) for m in range(count)], axis=1
        )
        total_qkv[n] = total
    arrive(sg)
    total = b.sg_all[0]
    for n in range(1, batches):
        total = total + b.sg_all[n]
    arrive(late_sum)
    late = b.late_all[0]
    for n in range(1, batches):
        late = late + b.late_all[n]
    small_grad[...] = total
    for r in range(2):
        small_grad[r : r + 1] = jnp.concatenate(
            [late[r * tiles + n : r * tiles + n + 1] for n in range(tiles)], axis=1
        )
    b.wide_row[0:1, 0:D] = small_grad[pl.ds(small_row, 1)]
    b.wide_row[0:1, D:] = small_grad[pl.ds(small_row + 1, 1)]
    moved = pltpu.roll(b.wide_row[...], 2 * D - small_lane, 1)
    total_small[...] = moved[0:1, 0:own_small]
    small_squares = gather_squares(jnp.zeros((8, WIDE), F32), small_grad[...])
    arrive(norm)
    squares = b.norm_seq[0]
    for n in range(1, count):
        squares = squares + b.norm_seq[n]
    b.norm_all[w.batch] = squares
    norm = links.start([
        remote(b.norm_all.at[w.batch], b.norm_all.at[w.batch], b.sem_norm_all[0].at[k],
               b.sem_norm_all[1].at[k], peer)
        for k, peer in enumerate(w.batch_peers())
    ])
    arrive(norm)
    squares = b.norm_all[0]
    for n in range(1, batches):
        squares = squares + b.norm_all[n]
    squares = squares + small_squares
    square = jnp.sum(jnp.sum(squares, axis=1, keepdims=True), axis=0, keepdims=True)
    norm_out[...] = jnp.broadcast_to(jnp.sqrt(square), norm_out.shape)
    for turn_of in (1, 3):
        dn_copy(turn_of).wait_send()
    links.finish()


def step_kernel(norm_in, grad_in, short_in, *refs):
    states = refs[: 4 * 6]
    outs = refs[4 * 6 :]
    grad_out, short_out, norm_out = outs[:3]
    grad_out[...] = grad_in[...]
    short_out[...] = short_in[...]
    grad_norm = norm_in[0:1, 0:1]
    norm_out[...] = grad_norm
    clip = clip_norm / jnp.maximum(grad_norm, clip_norm)
    for a in range(6):
        total, weight, one, two = states[4 * a : 4 * a + 4]
        limit = clip.reshape((1,) * len(total.shape))
        rate, decay = (rate_vector, 0.0) if a == 5 else (rate_matrix, decay_weight)
        results = adam_update(total[...], one[...], two[...], weight[...], limit, rate, decay)
        for ref, value in zip(outs[3 + 3 * a : 6 + 3 * a], results):
            ref[...] = value


def rotary_tables(rows, count):
    half = HEAD_DIM // 2
    frequency = np.exp(-math.log(10000.0) * np.arange(half) / half)
    lanes = np.tile(frequency, WIDE // half)
    sign = np.tile(np.repeat([-1.0, 1.0], half), WIDE // HEAD_DIM)
    inside = np.arange(rows)[:, None] * lanes
    starts = (np.arange(8) * (np.arange(8) < count) * rows)[:, None] * lanes
    pack = lambda angle: np.stack([np.cos(angle), np.sin(angle) * sign]).astype(np.float32)
    return pack(inside), pack(starts)


def fast_local(mesh):
    nx, nz, ny = grid_of(mesh)
    count = 2 * nx
    in_vmem = pl.BlockSpec(memory_space=pltpu.VMEM)

    def call(kernel, outs, scratch, args, **params):
        return pl.pallas_call(
            kernel,
            out_shape=[jax.ShapeDtypeStruct(s, t) for s, t in outs],
            in_specs=[in_vmem] * len(args),
            out_specs=[in_vmem] * len(outs),
            scratch_shapes=scratch,
            compiler_params=pltpu.CompilerParams(vmem_limit_bytes=VMEM_LIMIT, **params),
        )(*args)

    def body(tokens, doc_ids, out_grad,
             qkv_weight, qkv_first, qkv_second,
             proj_weight, proj_first, proj_second,
             up_weight, up_first, up_second,
             down_weight, down_first, down_second,
             pool_weight, pool_first, pool_second,
             small_weight, small_first, small_second):
        rows = tokens.shape[1]
        pools = out_grad.shape[1]
        ff = up_weight.shape[1]
        own = small_weight.shape[0]
        turn, offset = rotary_tables(rows, count)
        weights = (qkv_weight, proj_weight, up_weight, down_weight, pool_weight)
        shapes = [v.shape for v in weights]
        template = layer_buffers(nx, nz, ny, rows, ff, shapes[1:])
        scratch = jax.tree.leaves(list(template.values()))
        outs = [((pools, D), BF), ((rows, D), F32)] + [(s, F32) for s in shapes]
        outs += [((1, own), F32), ((8, WIDE), F32)]
        short, grad_in, *totals, norm = call(
            lambda *r: layer_kernel(nx, nz, ny, template, *r), outs, scratch,
            (tokens[0], doc_ids, out_grad[0], *weights, small_weight.reshape(1, own), turn, offset),
            collective_id=0, has_side_effects=True)
        weights = (*weights, small_weight)
        firsts = (qkv_first, proj_first, up_first, down_first, pool_first, small_first)
        seconds = (qkv_second, proj_second, up_second, down_second, pool_second, small_second)
        groups = [list(group) for group in zip(totals, weights, firsts, seconds)]
        groups[5] = [v.reshape(1, own) for v in groups[5]]
        outs = [((rows, D), F32), ((pools, D), BF), ((1, 1), F32)]
        outs += [(v[0].shape, F32) for v in groups for _ in range(3)]
        grad_out, short_out, norm_out, *states = call(
            step_kernel, outs, [],
            (norm, grad_in, short, *[v for group in groups for v in group]))
        states[15:] = [v.reshape(own) for v in states[15:]]
        return (short_out[None], grad_out[None], norm_out.reshape(()), *states)

    return body


def solution(mesh):
    in_specs = (
        P("batch", "seq", None),
        P("batch", None),
        P("batch", "seq", None),
        P(None, ("seq", "batch"), None),
        P(None, ("seq", "batch"), None),
        P(None, ("seq", "batch"), None),
        P(("seq", "batch"), None),
        P(("seq", "batch"), None),
        P(("seq", "batch"), None),
        P(("seq", "batch"), None),
        P(("seq", "batch"), None),
        P(("seq", "batch"), None),
        P(("seq", "batch"), None),
        P(("seq", "batch"), None),
        P(("seq", "batch"), None),
        P(("seq", "batch"), None),
        P(("seq", "batch"), None),
        P(("seq", "batch"), None),
        P(("seq", "batch")),
        P(("seq", "batch")),
        P(("seq", "batch")),
    )
    out_specs = (
        P("batch", "seq", None),
        P("batch", "seq", None),
        P(),
        P(None, ("seq", "batch"), None),
        P(None, ("seq", "batch"), None),
        P(None, ("seq", "batch"), None),
        P(("seq", "batch"), None),
        P(("seq", "batch"), None),
        P(("seq", "batch"), None),
        P(("seq", "batch"), None),
        P(("seq", "batch"), None),
        P(("seq", "batch"), None),
        P(("seq", "batch"), None),
        P(("seq", "batch"), None),
        P(("seq", "batch"), None),
        P(("seq", "batch"), None),
        P(("seq", "batch"), None),
        P(("seq", "batch"), None),
        P(("seq", "batch")),
        P(("seq", "batch")),
        P(("seq", "batch")),
    )
    body = fast_local(mesh) if fits(mesh) else local
    return jax.shard_map(body, mesh=mesh, in_specs=in_specs, out_specs=out_specs, check_vma=False)
```

```python
import math

import jax
import jax.numpy as jnp
import numpy as np
from jax import lax
from jax.experimental import pallas as pl
from jax.experimental.pallas import tpu as pltpu
from jax.sharding import PartitionSpec as P

D = 512
HEAD_DIM = 64
STEP = 10


beta_one = 0.9
beta_two = 0.999
adam_eps = 1e-08
norm_eps = 1e-05
clip_norm = 1.0
rate_matrix = 0.05
rate_vector = 0.5
decay_weight = 0.1
masked_score = -1e30


def from_behind(block, axis, distance):
    devices = range(lax.axis_size(axis))
    route = [(i - distance, i) for i in devices if i - distance in devices]
    return lax.ppermute(block, axis, route)


def layer_norm(values, scale_gain, shift_vec):
    center = values - jnp.mean(values, axis=-1, keepdims=True)
    spread = jnp.mean(center * center, axis=-1, keepdims=True)
    return center * lax.rsqrt(spread + norm_eps) * scale_gain + shift_vec


def rotate(values, positions):
    half_dim = HEAD_DIM // 2
    head_view = values.reshape(values.shape[0], values.shape[1] // HEAD_DIM, HEAD_DIM)
    frequency = jnp.exp(-math.log(10000.0) * jnp.arange(half_dim, dtype=jnp.float32) / half_dim)
    angles = positions.astype(jnp.float32)[:, None] * frequency[None, :]
    cosine = jnp.cos(angles)[:, None, :]
    sine_part = jnp.sin(angles)[:, None, :]
    first_half = head_view[..., :half_dim]
    second_half = head_view[..., half_dim:]
    turned = jnp.concatenate(
        [
            first_half * cosine - second_half * sine_part,
            second_half * cosine + first_half * sine_part,
        ],
        axis=-1,
    )
    return turned.reshape(values.shape)


def outer_sum(left_side, right_side):
    return lax.dot_general(
        left_side, right_side, (((0,), (0,)), ((), ())), preferred_element_type=jnp.float32
    )


def times_transpose(left_side, right_side):
    return lax.dot_general(
        left_side, right_side, (((1,), (1,)), ((), ())), preferred_element_type=jnp.float32
    )


def split_heads(values):
    return values.reshape(values.shape[0], values.shape[1] // HEAD_DIM, HEAD_DIM)


def block_scores(query_heads, key_heads, query_pos, key_pos, query_doc, key_doc):
    raw_scores = jnp.einsum(
        "qhd,khd->hqk", query_heads, key_heads, preferred_element_type=jnp.float32
    ) * HEAD_DIM ** (-0.5)
    allowed = (key_pos[None, :] <= query_pos[:, None]) & (key_doc[None, :] == query_doc[:, None])
    return jnp.where(allowed[None], raw_scores, masked_score)


def adam_update(gradient, first_moment, second_moment, weight, clip_scale, step_rate, decay_rate):
    clipped = gradient * clip_scale
    first_new = beta_one * first_moment + (1.0 - beta_one) * clipped
    second_new = beta_two * second_moment + (1.0 - beta_two) * clipped * clipped
    first_hat = first_new / (1.0 - beta_one**STEP)
    second_hat = second_new / (1.0 - beta_two**STEP)
    weight_new = weight - step_rate * (
        first_hat / (jnp.sqrt(second_hat) + adam_eps) + decay_rate * weight
    )
    return (first_new, second_new, weight_new)


def local(
    tokens,
    doc_ids,
    out_grad,
    qkv_weight,
    qkv_first,
    qkv_second,
    proj_weight,
    proj_first,
    proj_second,
    up_weight,
    up_first,
    up_second,
    down_weight,
    down_first,
    down_second,
    pool_weight,
    pool_first,
    pool_second,
    small_weight,
    small_first,
    small_second,
):
    block_rows = tokens.shape[1]
    model_width = tokens.shape[2]
    seq_count = lax.axis_size("seq")
    my_block = lax.axis_index("seq")
    whole_qkv, whole_proj, whole_up, whole_down, whole_pool, whole_small = (
        lax.all_gather(qkv_weight.astype(jnp.bfloat16), ("seq", "batch"), axis=1, tiled=True),
        lax.all_gather(proj_weight.astype(jnp.bfloat16), ("seq", "batch"), axis=0, tiled=True),
        lax.all_gather(up_weight.astype(jnp.bfloat16), ("seq", "batch"), axis=0, tiled=True),
        lax.all_gather(down_weight.astype(jnp.bfloat16), ("seq", "batch"), axis=0, tiled=True),
        lax.all_gather(pool_weight.astype(jnp.bfloat16), ("seq", "batch"), axis=0, tiled=True),
        lax.all_gather(small_weight.astype(jnp.bfloat16), ("seq", "batch"), axis=0, tiled=True),
    )
    small_used = whole_small.astype(jnp.float32)
    gain_first = small_used[0:D]
    shift_first = small_used[D : 2 * D]
    gain_second = small_used[2 * D : 3 * D]
    shift_second = small_used[3 * D : 4 * D]
    bias_down = small_used[4 * D : 5 * D]
    bias_pool = small_used[5 * D : 6 * D]
    bias_up = small_used[6 * D :]
    inputs = tokens[0].astype(jnp.float32)
    doc_row = doc_ids[0]
    first_row = my_block * block_rows
    positions = first_row + jnp.arange(block_rows, dtype=jnp.int32)
    doc_mine = lax.dynamic_slice_in_dim(doc_row, first_row, block_rows)
    normed, first_pull = jax.vjp(layer_norm, inputs, gain_first, shift_first)
    normed_low = normed.astype(jnp.bfloat16)
    projected = jnp.einsum("td,cde->cte", normed_low, whole_qkv, preferred_element_type=jnp.float32)
    queries_rot, query_pull = jax.vjp(lambda values: rotate(values, positions), projected[0])
    keys_rot, key_pull = jax.vjp(lambda values: rotate(values, positions), projected[1])
    query_low = queries_rot.astype(jnp.bfloat16)
    key_low = keys_rot.astype(jnp.bfloat16)
    value_low = projected[2].astype(jnp.bfloat16)
    keys_all, values_all = (
        lax.all_gather(key_low, "seq", axis=0, tiled=True),
        lax.all_gather(value_low, "seq", axis=0, tiled=True),
    )
    query_heads = split_heads(query_low)
    head_count = query_heads.shape[1]
    zeros_head_rows = jnp.zeros((head_count, block_rows), jnp.float32)
    zeros_heads = jnp.zeros((block_rows, head_count, HEAD_DIM), jnp.float32)

    def scores_of(number):
        start_row = number * block_rows
        key_heads = split_heads(keys_all[start_row : start_row + block_rows])
        value_heads = split_heads(values_all[start_row : start_row + block_rows])
        key_pos = start_row + jnp.arange(block_rows, dtype=jnp.int32)
        key_doc = doc_row[start_row : start_row + block_rows]
        scores = block_scores(query_heads, key_heads, positions, key_pos, doc_mine, key_doc)
        return (scores, key_heads, value_heads)

    running_max = jnp.full((head_count, block_rows), masked_score, jnp.float32)
    running_sum = zeros_head_rows
    for number in range(seq_count):

        def block_stats(number=number):
            scores = scores_of(number)[0]
            block_max = jnp.max(scores, axis=-1)
            return (block_max, jnp.sum(jnp.exp(scores - block_max[..., None]), axis=-1))

        block_max, block_sum = block_stats()
        new_max = jnp.maximum(running_max, block_max)
        running_sum = running_sum * jnp.exp(running_max - new_max) + block_sum * jnp.exp(
            block_max - new_max
        )
        running_max = new_max
    log_total = running_max + jnp.log(running_sum)
    attended = zeros_heads
    for number in range(seq_count):

        def block_output(number=number):
            scores, key_heads, value_heads = scores_of(number)
            soft_probs = jnp.exp(scores - log_total[..., None]).astype(jnp.bfloat16)
            return jnp.einsum(
                "hqk,khd->qhd", soft_probs, value_heads, preferred_element_type=jnp.float32
            )

        attended = attended + block_output()
    attended_low = attended.reshape(block_rows, model_width).astype(jnp.bfloat16)
    h_one = inputs + jnp.dot(attended_low, whole_proj, preferred_element_type=jnp.float32)
    normed_two, second_pull = jax.vjp(layer_norm, h_one, gain_second, shift_second)
    normed_two_low = normed_two.astype(jnp.bfloat16)
    hidden_pre = jnp.dot(normed_two_low, whole_up, preferred_element_type=jnp.float32) + bias_up
    activated, gelu_pull = jax.vjp(jax.nn.gelu, hidden_pre)
    act_low = activated.astype(jnp.bfloat16)
    h_two = h_one + jnp.dot(act_low, whole_down, preferred_element_type=jnp.float32) + bias_down
    h_two_low = h_two.astype(jnp.bfloat16)
    prev_rows = from_behind(h_two_low[block_rows - 2 :], "seq", 1)
    shifted = jnp.concatenate([prev_rows, h_two_low[: block_rows - 2]], axis=0)
    grouped = shifted.reshape(block_rows // 3, 3 * model_width)
    short_rows = (
        jnp.dot(grouped, whole_pool, preferred_element_type=jnp.float32) + bias_pool
    ).astype(jnp.bfloat16)
    out_rows = out_grad[0]
    grad_pool = outer_sum(grouped, out_rows)
    grad_bias_pool = jnp.sum(out_rows.astype(jnp.float32), axis=0)
    spread_rows = times_transpose(out_rows, whole_pool).reshape(block_rows, model_width)
    returned = from_behind(spread_rows[:2], "seq", -1)
    grad_h_two = jnp.concatenate([spread_rows[2:], returned], axis=0)
    grad_branch = grad_h_two.astype(jnp.bfloat16)
    grad_down = outer_sum(act_low, grad_branch)
    grad_bias_down = jnp.sum(grad_branch.astype(jnp.float32), axis=0)
    grad_act = times_transpose(grad_branch, whole_down)
    grad_hidden = gelu_pull(grad_act)[0].astype(jnp.bfloat16)
    grad_up = outer_sum(normed_two_low, grad_hidden)
    grad_bias_up = jnp.sum(grad_hidden.astype(jnp.float32), axis=0)
    grad_normed_two = times_transpose(grad_hidden, whole_up)
    back_h_one, grad_gain_second, grad_shift_second = second_pull(grad_normed_two)
    grad_h_one = grad_h_two + back_h_one
    grad_attn = grad_h_one.astype(jnp.bfloat16)
    grad_proj = outer_sum(attended_low, grad_attn)
    grad_attended = times_transpose(grad_attn, whole_proj).astype(jnp.bfloat16)
    grad_heads = split_heads(grad_attended)
    row_delta = zeros_head_rows
    value_terms = []
    for number in range(seq_count):

        def block_first(number=number):
            scores, key_heads, value_heads = scores_of(number)
            soft_probs = jnp.exp(scores - log_total[..., None])
            grad_probs = jnp.einsum(
                "qhd,khd->hqk", grad_heads, value_heads, preferred_element_type=jnp.float32
            )
            part_delta = jnp.sum(soft_probs * grad_probs, axis=-1)
            value_grad = jnp.einsum(
                "hqk,qhd->khd",
                soft_probs.astype(jnp.bfloat16),
                grad_heads,
                preferred_element_type=jnp.float32,
            )
            return (part_delta, value_grad.reshape(block_rows, model_width))

        part_delta, value_grad = block_first()
        row_delta = row_delta + part_delta
        value_terms.append(value_grad)
    grad_query = zeros_heads
    key_terms = []
    for number in range(seq_count):

        def block_second(number=number):
            scores, key_heads, value_heads = scores_of(number)
            soft_probs = jnp.exp(scores - log_total[..., None])
            grad_probs = jnp.einsum(
                "qhd,khd->hqk", grad_heads, value_heads, preferred_element_type=jnp.float32
            )
            grad_scores = (soft_probs * (grad_probs - row_delta[..., None])).astype(jnp.bfloat16)
            query_part = jnp.einsum(
                "hqk,khd->qhd", grad_scores, key_heads, preferred_element_type=jnp.float32
            )
            key_part = jnp.einsum(
                "hqk,qhd->khd", grad_scores, query_heads, preferred_element_type=jnp.float32
            )
            return (query_part, key_part.reshape(block_rows, model_width))

        query_part, key_part = block_second()
        grad_query = grad_query + query_part
        key_terms.append(key_part)
    head_scale = HEAD_DIM ** (-0.5)
    grad_keys, grad_values = (
        lax.psum_scatter(
            (jnp.concatenate(key_terms, axis=0) * head_scale).astype(jnp.bfloat16),
            "seq",
            scatter_dimension=0,
            tiled=True,
        ).astype(jnp.float32),
        lax.psum_scatter(
            jnp.concatenate(value_terms, axis=0).astype(jnp.bfloat16),
            "seq",
            scatter_dimension=0,
            tiled=True,
        ).astype(jnp.float32),
    )
    grad_q_pre = query_pull(grad_query.reshape(block_rows, model_width) * head_scale)[0].astype(
        jnp.bfloat16
    )
    grad_k_pre = key_pull(grad_keys)[0].astype(jnp.bfloat16)
    grad_v_pre = grad_values.astype(jnp.bfloat16)
    stacked = jnp.stack([grad_q_pre, grad_k_pre, grad_v_pre])
    grad_qkv = jnp.einsum("td,cte->cde", normed_low, stacked, preferred_element_type=jnp.float32)
    grad_normed = jnp.einsum("cte,cde->td", stacked, whole_qkv, preferred_element_type=jnp.float32)
    back_inputs, grad_gain_first, grad_shift_first = first_pull(grad_normed)
    input_grad = (grad_h_one + back_inputs)[None]
    grad_small = jnp.concatenate(
        [
            grad_gain_first,
            grad_shift_first,
            grad_gain_second,
            grad_shift_second,
            grad_bias_down,
            grad_bias_pool,
            grad_bias_up,
        ]
    )
    all_grads = (grad_qkv, grad_proj, grad_up, grad_down, grad_pool, grad_small)
    shards = (
        lax.psum_scatter(all_grads[0], ("seq", "batch"), scatter_dimension=1, tiled=True),
        lax.psum_scatter(all_grads[1], ("seq", "batch"), scatter_dimension=0, tiled=True),
        lax.psum_scatter(all_grads[2], ("seq", "batch"), scatter_dimension=0, tiled=True),
        lax.psum_scatter(all_grads[3], ("seq", "batch"), scatter_dimension=0, tiled=True),
        lax.psum_scatter(all_grads[4], ("seq", "batch"), scatter_dimension=0, tiled=True),
        lax.psum_scatter(all_grads[5], ("seq", "batch"), scatter_dimension=0, tiled=True),
    )
    local_squares = sum((jnp.sum(portion * portion) for portion in shards))
    grad_norm = jnp.sqrt(lax.psum(local_squares, ("seq", "batch")))
    clip_scale = clip_norm / jnp.maximum(grad_norm, clip_norm)
    masters = (qkv_weight, proj_weight, up_weight, down_weight, pool_weight, small_weight)
    firsts = (qkv_first, proj_first, up_first, down_first, pool_first, small_first)
    seconds = (qkv_second, proj_second, up_second, down_second, pool_second, small_second)
    new_states = []
    for index_kind in range(6):
        step_rate = rate_vector if index_kind == 5 else rate_matrix
        decay_rate = 0.0 if index_kind == 5 else decay_weight
        new_states.append(
            adam_update(
                shards[index_kind],
                firsts[index_kind],
                seconds[index_kind],
                masters[index_kind],
                clip_scale,
                step_rate,
                decay_rate,
            )
        )
    return (
        short_rows[None],
        input_grad,
        grad_norm,
        new_states[0][0],
        new_states[0][1],
        new_states[0][2],
        new_states[1][0],
        new_states[1][1],
        new_states[1][2],
        new_states[2][0],
        new_states[2][1],
        new_states[2][2],
        new_states[3][0],
        new_states[3][1],
        new_states[3][2],
        new_states[4][0],
        new_states[4][1],
        new_states[4][2],
        new_states[5][0],
        new_states[5][1],
        new_states[5][2],
    )


MESH = pl.DeviceIdType.MESH
BF = jnp.bfloat16
F32 = jnp.float32
WIDE = 128
HEADS = 2
LOG2E = math.log2(math.e)
NN = (((1,), (0,)), ((), ()))
NT = (((1,), (1,)), ((), ()))
TN = (((0,), (0,)), ((), ()))
VMEM_LIMIT = 121 * 2**19
PROJ, UP, DOWN, POOL = range(4)
ARRAYS = 4
GELU_C = math.sqrt(2.0 / math.pi)
DOCS = 7
PAD = 16


def dot(a, b, dims=NN):
    return lax.dot_general(a, b, dims, preferred_element_type=F32)


def grid_of(mesh):
    seq, batch = mesh.shape["seq"], mesh.shape["batch"]
    return seq // 2, batch // 2, 2


def fits(mesh):
    seq, batch = mesh.shape["seq"], mesh.shape["batch"]
    return seq == 4 and batch % 2 == 0 and D % (seq * batch * 16) == 0


class Where:
    def __init__(self, nx, nz, ny):
        self.nx, self.nz, self.ny = nx, nz, ny
        self.count, self.batches = 2 * nx, nz * ny
        seq, batch = lax.axis_index("seq"), lax.axis_index("batch")
        self.seq = seq
        self.batch = batch
        self.x, self.c = lax.div(seq, 2), lax.rem(seq, 2)
        self.z, self.y = lax.div(batch, ny), lax.rem(batch, ny)
        self.xo, self.co, self.yo = 1 - self.x, 1 - self.c, 1 - self.y

    def dev(self, x=None, c=None, z=None, y=None):
        x = self.x if x is None else x
        c = self.c if c is None else c
        z = self.z if z is None else z
        y = self.y if y is None else y
        return (x * 2 + c, z * self.ny + y)

    def z_at(self, step):
        return lax.rem(self.z + step, self.nz)

    def seq_at(self, step):
        return lax.rem(self.seq + step, self.count)

    def batch_at(self, step):
        return lax.rem(self.batch + step, self.batches)

    def partner(self, stage):
        return {
            "x": self.dev(x=self.xo),
            "c": self.dev(c=self.co),
            "y": self.dev(y=self.yo),
        }[stage]

    def seq_peers(self):
        return [(self.seq_at(k), self.batch) for k in range(1, self.count)]

    def batch_peers(self):
        return [(self.seq, self.batch_at(k)) for k in range(1, self.batches)]


def remote(src, dst, send, recv, peer):
    return pltpu.make_async_remote_copy(
        src, dst, send, recv, device_id=peer, device_id_type=MESH
    )


class Links:
    def __init__(self):
        self.open = []

    def start(self, copies):
        for copy in copies:
            copy.start()
        self.open += copies
        return copies

    def close(self, copies):
        for copy in copies:
            copy.wait_send()
        self.open = [other for other in self.open if all(other is not copy for copy in copies)]

    def finish(self):
        self.close(list(self.open))


def arrive(copies):
    for copy in copies:
        copy.wait_recv()


class Gather:
    def __init__(self, w, links, fulls, pieces, send, recv):
        self.w, self.links = w, links
        self.fulls, self.pieces, self.send, self.recv = fulls, pieces, send, recv
        self.copies = {}

    def start(self, n, index):
        w = self.w
        a, order, at_rows, at_cols = self.pieces[n]
        stage, done = order[index], order[:index]
        pick = [
            slice(None) if name in done else own
            for name, own in (("x", w.x), ("c", w.c), ("z", w.z), ("y", w.y))
        ]
        block = self.fulls[a].at[pick[0], pick[1], pick[2], pick[3], at_rows, at_cols]
        if stage == "z":
            peers = [(k - 1, w.dev(z=w.z_at(k))) for k in range(1, w.nz)]
        else:
            peers = [(w.nz - 1 + "xyc".index(stage), w.partner(stage))]
        self.copies[n, index] = self.links.start([
            remote(block, block, self.send.at[n, slot], self.recv.at[n, slot], peer)
            for slot, peer in peers
        ])

    def step(self, n, index):
        arrive(self.copies[n, index])
        if index < 3:
            self.start(n, index + 1)


def gather_pieces(shapes):
    def part(a, axis, lo, hi):
        size = shapes[a][axis]
        return slice(size * lo // 4 // 16 * 16, size * hi // 4 // 16 * 16)

    every = slice(None)
    return [
        (PROJ, "zxyc", every, every),
        (UP, "zyxc", every, part(UP, 1, 0, 2)),
        (UP, "zyxc", every, part(UP, 1, 2, 4)),
        (DOWN, "zxyc", part(DOWN, 0, 0, 2), every),
        (DOWN, "zxyc", part(DOWN, 0, 2, 4), every),
        (POOL, "zyxc", part(POOL, 0, 0, 2), every),
        (POOL, "zxyc", part(POOL, 0, 2, 4), every),
    ]


PIECES = 7
GATHER_EARLY = 2
GATHER_STEPS = (
    ((0, 0), (1, 0), (2, 0), (3, 0), (4, 0)),
    ((5, 0),),
    ((6, 0), (0, 1)),
    ((1, 1),),
    ((3, 1),),
    ((2, 1),),
    ((5, 1),),
    ((4, 1), (0, 2)),
    ((6, 1), (0, 3)),
    ((3, 2),),
    ((1, 2), (3, 3)),
    ((4, 2), (1, 3)),
    ((2, 2), (4, 3), (2, 3)),
    ((6, 2), (5, 2)),
    ((6, 3), (5, 3)),
)


class Scatter:
    ORDERS = ("yzx", "zyx", "yxz", "yzx")

    def __init__(self, w, links, fulls, got, send, recv):
        self.w, self.links = w, links
        self.sums = [full.at[:, 0] for full in fulls]
        self.c_in = [full.at[:, 1] for full in fulls]
        self.got = got
        self.send, self.recv = send, recv
        self.copies, self.make = {}, {}

    @classmethod
    def shapes(cls, a, shard, nx, nz, ny):
        sizes = {"x": nx, "z": nz, "y": ny}
        found, rest = [], "xzy"
        for stage in cls.ORDERS[a]:
            rest = rest.replace(stage, "")
            lead = (nz - 1,) if stage == "z" else ()
            found.append(lead + tuple(sizes[n] for n in rest) + shard)
        return found

    def pick(self, a, index, at):
        order = self.ORDERS[a]
        own = {"x": self.w.x, "z": self.w.z, "y": self.w.y}
        return tuple(
            at if n == order[index] else (own[n] if n in order[:index] else slice(None))
            for n in "xzy"
        )

    def begin(self, a, make):
        w = self.w
        self.make[a] = make
        shape = self.sums[a].shape[1:]
        for x_of in range(w.nx):
            self.sums[a][x_of] = make(x_of * 2 + w.co).reshape(shape).astype(BF)
        self.copies[a, "c"] = self.links.start([
            remote(self.sums[a], self.c_in[a], self.send.at[a, 0], self.recv.at[a, 0],
                   w.partner("c"))
        ])

    def start(self, a, index):
        w, stage = self.w, self.ORDERS[a][index]
        into = self.got[index][a]
        if stage == "z":
            moves = [
                (w.z_at(k), into.at[k - 1], 2 + k, w.dev(z=w.z_at(k))) for k in range(1, w.nz)
            ]
        else:
            moves = [(w.xo if stage == "x" else w.yo, into, "xy".index(stage) + 1,
                      w.partner(stage))]
        self.copies[a, index] = self.links.start([
            remote(self.sums[a].at[self.pick(a, index, at)], to, self.send.at[a, slot],
                   self.recv.at[a, slot], peer)
            for at, to, slot, peer in moves
        ])

    def total(self, a, index):
        w, stage = self.w, self.ORDERS[a][index]
        arrive(self.copies[a, index])
        here = self.pick(a, index, {"x": w.x, "z": w.z, "y": w.y}[stage])
        into = self.got[index][a]
        value = self.sums[a][here].astype(F32)
        if stage == "z":
            for k in range(w.nz - 1):
                value = value + into[k].astype(F32)
        else:
            value = value + into[...].astype(F32)
        return here, value

    def step(self, a, index):
        w = self.w
        if index == 0:
            arrive(self.copies[a, "c"])
            self.links.close(self.copies[a, "c"])
            shape = self.sums[a].shape[1:]
            for x_of in range(w.nx):
                value = self.make[a](x_of * 2 + w.c).reshape(shape)
                self.sums[a][x_of] = (value + self.c_in[a][x_of].astype(F32)).astype(BF)
        else:
            here, value = self.total(a, index - 1)
            self.sums[a][here] = value.astype(BF)
        self.start(a, index)

    def last(self, a):
        return self.total(a, 2)[1]


def norm_stats(values):
    center = values - jnp.mean(values, axis=-1, keepdims=True)
    spread = jnp.mean(center * center, axis=-1, keepdims=True)
    scale = lax.rsqrt(spread + norm_eps)
    return center * scale, scale


def norm_back(grad, unit, scale, gain):
    inner = grad * gain
    mean_one = jnp.mean(inner, axis=-1, keepdims=True)
    mean_two = jnp.mean(inner * unit, axis=-1, keepdims=True)
    back = scale * (inner - mean_one - unit * mean_two)
    return back, jnp.sum(grad * unit, axis=0, keepdims=True), jnp.sum(grad, axis=0, keepdims=True)


def swap_halves(values):
    lane = lax.broadcasted_iota(jnp.int32, values.shape, 1)
    return jnp.where(
        lax.rem(lane, HEAD_DIM) < HEAD_DIM // 2,
        pltpu.roll(values, WIDE - HEAD_DIM // 2, 1),
        pltpu.roll(values, HEAD_DIM // 2, 1),
    )


def in_head(lane, h):
    return (lane >= h * HEAD_DIM) & (lane < (h + 1) * HEAD_DIM)


def with_feats(base, lane, h, vector):
    one = vector.astype(BF).astype(F32)
    two = (vector - one).astype(BF).astype(F32)
    first = (1 - h) * HEAD_DIM + 8
    for n, term in enumerate((one, two, vector - one - two)):
        base = jnp.where(lane == first + n, term, base)
    return base


def document_edges(docs):
    feat = lax.rem(lax.broadcasted_iota(jnp.int32, (1, WIDE), 1), HEAD_DIM)
    lo = jnp.zeros((1, WIDE), jnp.int32)
    hi = jnp.zeros((1, WIDE), jnp.int32)
    below = jnp.zeros((1, 1), jnp.int32)
    for d in range(DOCS):
        upto = jnp.sum(jnp.where(docs <= d, 1, 0), axis=1, keepdims=True)
        lo = jnp.where(feat == d, below, lo)
        hi = jnp.where(feat == d, upto, hi)
        below = upto
    return lo, hi


def layer_buffers(nx, nz, ny, rows, ff, shapes):
    count, block = 2 * nx, rows + PAD
    batches = nz * ny
    vmem = lambda shape, kind=BF: pltpu.VMEM(shape, kind)
    wide = 3 * WIDE
    shard = shapes[0][0]
    scatter = [Scatter.shapes(a, s, nx, nz, ny) for a, s in enumerate(shapes)]
    named = dict(
        fulls=[vmem((nx, 2, nz, ny) + s) for s in shapes],
        part=vmem((count, 3, shard, WIDE)),
        wq=vmem((count, nz, ny, 3, shard, WIDE)),
        small_seq=vmem((count, 16, D)),
        small_all=vmem((nz + ny, 16, D)),
        small=vmem((16, D), F32),
        wide_row=vmem((8, 2 * D), F32),
        tok_all=vmem((count, rows, D)),
        normed=vmem((count, rows, D)),
        ext=vmem((3, HEADS, count * block, WIDE)),
        o_ref=vmem((count, block, WIDE), F32),
        o_low=vmem((count, block, WIDE)),
        att=vmem((count, rows, WIDE)),
        h_one=vmem((rows, D), F32),
        dh_two=vmem((D // WIDE * block, WIDE), F32),
        buf=[vmem((count * block, WIDE), F32) for _ in range(3)],
        normed_two=vmem((rows, D)),
        act=vmem((rows, ff)),
        d_hidden=vmem((rows, ff)),
        d_branch=vmem((rows, D)),
        d_attn=vmem((rows, D)),
        grouped=vmem((rows // 3, 3 * D)),
        edge=vmem((4, 16, D)),
        do_send=vmem((count, rows, WIDE)),
        dq_turned=vmem((WIDE, count * block), F32),
        do_ext=vmem((HEADS, count * block, WIDE)),
        stacked=vmem((rows, wide)),
        g_qkv=vmem((D, wide), F32),
        x_in=vmem((rows, D)),
        gq_out=vmem((batches, count, shard, wide)),
        gq_in=vmem((batches, count, shard, wide)),
        gq_seq=vmem((count, shard, wide)),
        gq_got=vmem((count, shard, wide)),
        small_grad=vmem((16, D), F32),
        sg_seq=vmem((count, 16, D), F32),
        sg_all=vmem((batches, 16, D), F32),
        late_seq=vmem((count, 8, WIDE), F32),
        late_all=vmem((batches, 8, WIDE), F32),
        norm_seq=vmem((count, 8, WIDE), F32),
        norm_all=vmem((batches, 8, WIDE), F32),
        got_one=[vmem(found[0]) for found in scatter],
        got_two=[vmem(found[1]) for found in scatter],
        got_three=[vmem(found[2]) for found in scatter],
    )
    sems = dict(
        gather=(PIECES, nz + 2), scatter=(ARRAYS, nz + 2), tok=(7,), part=(count - 1,),
        wq=(nz + 1,), small_seq=(count - 1,), small_all=(nz + 1,), edge=(2,),
        o=(count, 2), do=(count - 1,), dn=(2,), x=(1,), gq=(batches - 1,), gq_seq=(count - 1,),
        sg_seq=(count - 1,), sg_all=(batches - 1,), late_seq=(count - 1,),
        late_all=(batches - 1,), norm_seq=(count - 1,),
        norm_all=(batches - 1,),
    )
    for name, shape in sems.items():
        named["sem_" + name] = [pltpu.SemaphoreType.DMA(shape) for _ in range(2)]
    named["ready"] = pltpu.SemaphoreType.REGULAR
    named["free"] = pltpu.SemaphoreType.REGULAR
    return named


SWEEP_STEPS = (
    ((DOWN, 1),),
    ((POOL, 1), (PROJ, 1)),
    ((UP, 1), (DOWN, 2)),
    (),
)


class Bag:
    def __init__(self, template, refs):
        refs = list(refs)
        for name, value in template.items():
            if isinstance(value, list):
                setattr(self, name, [refs.pop(0) for _ in value])
            else:
                setattr(self, name, refs.pop(0))


def layer_kernel(nx, nz, ny, template, tokens, doc_ids, out_grad, qkv_w, proj_w, up_w, down_w,
                 pool_w, small_in, turn, offset, short_out, input_grad, total_qkv, total_proj,
                 total_up, total_down, total_pool, total_small, norm_out, *scratch):
    w = Where(nx, nz, ny)
    b = Bag(template, scratch)
    links = Links()
    rows = tokens.shape[0]
    block = rows + PAD
    count, batches = w.count, w.batches
    pools = rows // 3
    sub = rows // 3
    tiles = D // WIDE
    own = (w.x, w.c, w.z, w.y)

    barrier = pltpu.get_barrier_semaphore()
    peers = w.seq_peers() + w.batch_peers()
    for peer in peers:
        pl.semaphore_signal(barrier, inc=1, device_id=peer, device_id_type=MESH)
    own_small = small_in.shape[1]
    small_first = (w.seq * batches + w.batch) * own_small
    small_row, small_lane = lax.div(small_first, D), lax.rem(small_first, D)
    b.wide_row[...] = jnp.zeros(b.wide_row.shape, F32)
    b.wide_row[0:1, 0:own_small] = small_in[...]
    moved = pltpu.roll(b.wide_row[...], small_lane, 1)
    b.small[...] = jnp.zeros(b.small.shape, F32)
    b.small[pl.ds(small_row, 1)] = moved[0:1, 0:D]
    b.small[pl.ds(small_row + 1, 1)] = moved[0:1, D:]
    b.small_seq[w.seq] = b.small[...].astype(BF)
    for d in range(count):
        b.part[d] = qkv_w[:, :, d * WIDE : (d + 1) * WIDE].astype(BF)
    b.edge[0] = out_grad[0:16]
    shards = (proj_w, up_w, down_w, pool_w)
    for shard, full in zip(shards, b.fulls):
        full[own] = shard[...].astype(BF)
    gather = Gather(w, links, b.fulls, gather_pieces([s.shape for s in shards]), *b.sem_gather)
    pl.semaphore_wait(barrier, len(peers))

    send, recv = b.sem_tok
    mine = b.tok_all.at[w.seq]

    def piece(ref, n):
        return ref.at[pl.ds(n * sub, sub)]

    small_a = links.start([
        remote(b.small_seq.at[w.seq], b.small_seq.at[w.seq], b.sem_small_seq[0].at[k],
               b.sem_small_seq[1].at[k], peer)
        for k, peer in enumerate(w.seq_peers())
    ])
    part_a = links.start([
        remote(b.part.at[w.seq_at(k + 1)], b.wq.at[w.seq, w.z, w.y], b.sem_part[0].at[k],
               b.sem_part[1].at[k], peer)
        for k, peer in enumerate(w.seq_peers())
    ])
    tok_x = links.start([
        remote(piece(tokens, n), piece(mine, n), send.at[n], recv.at[n], w.partner("x"))
        for n in range(3)
    ])
    for n in range(GATHER_EARLY):
        gather.start(n, 0)
    tok_c = links.start([remote(tokens, mine, send.at[3], recv.at[3], w.partner("c"))])
    links.start([
        remote(b.edge.at[0], b.edge.at[1], b.sem_edge[0].at[0], b.sem_edge[1].at[0],
               (w.seq_at(count - 1), w.batch))
    ])
    grad_edge = links.open[-1:]
    b.wq[w.seq, w.z, w.y] = b.part[w.seq]
    lo, hi = document_edges(doc_ids[...])
    arrive(small_a)
    total = b.small_seq[0].astype(F32)
    for n in range(1, count):
        total = total + b.small_seq[n].astype(F32)
    b.small_all[w.z] = total.astype(BF)
    z_peers = [w.dev(z=w.z_at(k)) for k in range(1, nz)]
    small_b = links.start([
        remote(b.small_all.at[w.z], b.small_all.at[w.z], b.sem_small_all[0].at[k],
               b.sem_small_all[1].at[k], peer)
        for k, peer in enumerate(z_peers)
    ])
    arrive(part_a)
    part_b = links.start([
        remote(b.wq.at[:, w.z, w.y], b.wq.at[:, w.z, w.y], b.sem_wq[0].at[k],
               b.sem_wq[1].at[k], peer)
        for k, peer in enumerate(z_peers)
    ])
    for n in range(GATHER_EARLY, PIECES):
        gather.start(n, 0)
    b.tok_all[w.seq] = tokens[...]

    lane_row = lax.broadcasted_iota(jnp.int32, (1, WIDE), 1)
    feat_row = lax.rem(lane_row, HEAD_DIM)
    pad_lane = lax.broadcasted_iota(jnp.int32, (PAD, WIDE), 1)
    for h in range(HEADS):
        for n in range(count):
            pad = pl.ds(n * block + rows, PAD)
            b.ext[0, h, pad] = jnp.zeros((PAD, WIDE), BF)
            masks = ~in_head(pad_lane, h) & (lax.rem(pad_lane, HEAD_DIM) < DOCS)
            b.ext[1, h, pad] = jnp.where(masks, masked_score, 0.0).astype(BF)
            b.ext[2, h, pad] = jnp.zeros((PAD, WIDE), BF)
            b.do_ext[h, pad] = jnp.zeros((PAD, WIDE), BF)

    arrive(small_b)
    total = b.small_all[0].astype(F32)
    for n in range(1, nz):
        total = total + b.small_all[n].astype(F32)
    b.small_all[nz + w.y] = total.astype(BF)
    small_c = links.start([
        remote(b.small_all.at[nz + w.y], b.small_all.at[nz + w.y], b.sem_small_all[0].at[nz],
               b.sem_small_all[1].at[nz], w.partner("y"))
    ])
    arrive(part_b)
    part_c = links.start([
        remote(b.wq.at[:, :, w.y], b.wq.at[:, :, w.y], b.sem_wq[0].at[nz], b.sem_wq[1].at[nz],
               w.partner("y"))
    ])
    arrive(small_c)
    b.small[...] = b.small_all[nz].astype(F32) + b.small_all[nz + 1].astype(F32)
    small = b.small
    arrive(part_c)

    def qkv_weight(n):
        return b.wq[:, :, :, n].reshape(D, WIDE)

    def turning(of_block, r0):
        cos_in, sin_in = turn[0, pl.ds(r0, sub)], turn[1, pl.ds(r0, sub)]
        cos_of, sin_of = offset[0, pl.ds(of_block, 1)], offset[1, pl.ds(of_block, 1)]
        return cos_in * cos_of - sin_in * sin_of, sin_in * cos_of + cos_in * sin_of

    def project(of_block):
        weight = jnp.concatenate([qkv_weight(n) for n in range(3)], axis=1)

        def body(n, _):
            r0 = pl.multiple_of(n * sub, 16)
            unit, _ = norm_stats(b.tok_all[of_block, pl.ds(r0, sub)].astype(F32))
            normed = (unit * small[0:1] + small[1:2]).astype(BF)
            b.normed[of_block, pl.ds(r0, sub)] = normed
            qkv = dot(normed, weight)
            cosine, sine = turning(of_block, r0)
            parts = [qkv[:, m * WIDE : (m + 1) * WIDE] for m in range(3)]
            for m in range(2):
                parts[m] = parts[m] * cosine + swap_halves(parts[m]) * sine
            parts[0] = parts[0] * (LOG2E * HEAD_DIM ** -0.5)
            place = lax.broadcasted_iota(jnp.int32, (sub, WIDE), 0) + (of_block * rows + r0)
            lane = lax.broadcasted_iota(jnp.int32, (sub, WIDE), 1)
            same = (place >= lo) & (place < hi)
            ones = jnp.where((feat_row >= 8) & (feat_row < 11), 1.0, 0.0)
            q_feat = jnp.where(same, 1.0, 0.0)
            k_feat = jnp.where(feat_row < DOCS, jnp.where(same, 0.0, masked_score), ones)
            at = pl.ds(pl.multiple_of(of_block * block + r0, 16), sub)
            for h in range(HEADS):
                for m, feats in enumerate((q_feat, k_feat, 1.0)):
                    b.ext[m, h, at] = jnp.where(in_head(lane, h), parts[m], feats).astype(BF)
            return 0

        lax.fori_loop(0, 3, body, 0)

    pending = list(GATHER_STEPS)

    def advance():
        for n, index in pending.pop(0):
            gather.step(n, index)

    project(w.seq)
    advance()
    arrive(tok_c)
    project(w.x * 2 + w.co)
    advance()
    theirs = b.tok_all.at[w.xo * 2 + w.c]
    passed = []
    for n in range(3):
        arrive(tok_x[n : n + 1])
        passed += links.start([
            remote(piece(theirs, n), piece(theirs, n), send.at[4 + n], recv.at[4 + n],
                   w.partner("c"))
        ])
    project(w.xo * 2 + w.c)
    advance()
    arrive(passed)
    project(w.xo * 2 + w.co)
    advance()

    half_rows = (block // 2, rows - block // 2)

    def attend(of_block, half):
        size = block // 2
        r0 = of_block * block + half * size
        n = min(count * block, -(-(r0 + size) // 256) * 256)
        m0 = (r0 // 128) * 128
        lane = lax.broadcasted_iota(jnp.int32, (size, WIDE), 1)
        at_row = lax.broadcasted_iota(jnp.int32, (size, n - m0), 0) + r0
        at_col = lax.broadcasted_iota(jnp.int32, (size, n - m0), 1) + m0
        queries = [b.ext[0, h, pl.ds(r0, size)] for h in range(HEADS)]
        scores = [dot(queries[h], b.ext[1, h, :n], NT) for h in range(HEADS)]
        outs = []
        for h in range(HEADS):
            s = scores[h]
            tail = jnp.where(at_col <= at_row, s[:, m0:], masked_score)
            s = jnp.concatenate([s[:, :m0], tail], axis=1) if m0 else tail
            top = jnp.max(s, axis=1, keepdims=True)
            p = jnp.exp2(s - top).astype(BF)
            sums = dot(p, b.ext[2, h, :n])
            outs.append(sums / pltpu.roll(sums, HEAD_DIM, 1))
            log_total = top + jnp.log2(sums)
            q_new = with_feats(queries[h].astype(F32), lane, h, -log_total)
            b.ext[0, h, pl.ds(r0, size)] = q_new.astype(BF)
        both = jnp.where(lane < HEAD_DIM, outs[0], outs[1])
        b.o_ref[of_block, pl.ds(half * size, size)] = both
        b.o_low[of_block, pl.ds(half * size, size)] = both.astype(BF)

    def o_copy(of_block, half):
        at = pl.ds(half * (block // 2), half_rows[half])
        return remote(b.o_low.at[of_block, at], b.att.at[w.seq, at], b.sem_o[0].at[of_block, half],
                      b.sem_o[1].at[w.seq, half], (of_block, w.batch))

    for of_block in range(count):
        for half in range(2):
            attend(of_block, half)

            @pl.when(w.seq != of_block)
            def _(of_block=of_block, half=half):
                o_copy(of_block, half).start()

            advance()

        @pl.when(w.seq == of_block)
        def _(of_block=of_block):
            b.att[of_block] = b.o_low[of_block, 0:rows]

    advance()


    first, last = w.seq == 0, w.seq == count - 1

    def lay(ref, start, value):
        for n in range(tiles):
            ref[pl.ds(n * block + start, value.shape[0])] = value[:, n * WIDE : (n + 1) * WIDE]

    def whole(ref, start):
        return jnp.concatenate(
            [ref[pl.ds(n * block + start, rows)] for n in range(tiles)], axis=1
        )

    def add(ref, value):
        for n in range(tiles):
            ref[pl.ds(n * block, rows)] += value[:, n * WIDE : (n + 1) * WIDE]

    sum_one, sum_two, h_two = b.buf
    sum_one[...] = jnp.zeros(sum_one.shape, F32)
    sum_two[...] = jnp.zeros(sum_two.shape, F32)

    for k in range(1, count):
        of = w.seq_at(k)
        for half in range(2):
            at = pl.ds(half * (block // 2), half_rows[half])
            remote(b.att.at[of, at], b.att.at[of, at], b.sem_o[0].at[of, half],
                   b.sem_o[1].at[of, half], (of, w.batch)).wait_recv()
    attended = jnp.concatenate([b.att[n] for n in range(count)], axis=1)
    b.h_one[...] = tokens[...].astype(F32) + dot(attended, b.fulls[PROJ][...].reshape(D, D))
    unit, _ = norm_stats(b.h_one[...])
    b.normed_two[...] = (unit * small[2:3] + small[3:4]).astype(BF)
    advance()
    part = b.act.shape[1] // count

    def parts_of(n):
        cols = pl.ds(pl.multiple_of(n * part, part), part)
        up = b.fulls[UP][:, :, :, :, :, cols].reshape(D, part)
        down = b.fulls[DOWN][lax.div(n, 2), lax.rem(n, 2)].reshape(part, D)
        return cols, up, down

    def feed(n, _):
        cols, up, down = parts_of(n)
        hidden = dot(b.normed_two[...], up) + small[pl.ds(6 + n, 1)]
        square = hidden * hidden
        bend = jnp.tanh(GELU_C * hidden * (1.0 + 0.044715 * square))
        half = 0.5 * (1.0 + bend)
        act_low = (hidden * half).astype(BF)
        b.act[:, cols] = act_low
        slope = half + 0.5 * hidden * (1.0 - bend * bend) * (
            GELU_C * (1.0 + 3 * 0.044715 * square)
        )
        b.d_hidden[:, cols] = slope.astype(BF)
        add(sum_one, dot(act_low, down))
        return 0

    lax.fori_loop(0, count, feed, 0)
    h_low = (b.h_one[...] + whole(sum_one, 0) + small[4:5]).astype(BF)
    lay(h_two, 8, h_low.astype(F32))
    b.edge[2] = h_low[rows - 16 :]
    row_edge = links.start([
        remote(b.edge.at[2], b.edge.at[3], b.sem_edge[0].at[1], b.sem_edge[1].at[1],
               (w.seq_at(1), w.batch))
    ])
    advance()

    pool = b.fulls[POOL][...].reshape(3 * D, D)
    g_low = out_grad[...]
    spread = dot(g_low, pool, NT)
    for k in range(3):
        for n in range(tiles):
            at = k * D + n * WIDE
            b.dh_two[pl.ds(n * block + 6 + k, pools, stride=3)] = spread[:, at : at + WIDE]
    arrive(grad_edge)
    beyond = jnp.where(last, 0.0, dot(b.edge[1], pool, NT))
    lay(b.dh_two, 8 + rows - 2, beyond[0:1, 0:D])
    lay(b.dh_two, 8 + rows - 1, beyond[0:1, D : 2 * D])
    b.d_branch[...] = whole(b.dh_two, 8).astype(BF)
    small_grad = b.small_grad
    small_grad[...] = jnp.zeros(small_grad.shape, F32)
    small_grad[4:5] = jnp.sum(b.d_branch[...].astype(F32), axis=0, keepdims=True)
    small_grad[5:6] = jnp.sum(g_low.astype(F32), axis=0, keepdims=True)
    links.finish()
    for of_block in range(count):
        for half in range(2):

            @pl.when(w.seq != of_block)
            def _(of_block=of_block, half=half):
                o_copy(of_block, half).wait_send()

    for peer in w.seq_peers():
        pl.semaphore_signal(b.free, inc=1, device_id=peer, device_id_type=MESH)

    def feed_back(n, _):
        cols, up, down = parts_of(n)
        slope = b.d_hidden[:, cols].astype(F32)
        d_low = (dot(b.d_branch[...], down, NT) * slope).astype(BF)
        b.d_hidden[:, cols] = d_low
        small_grad[pl.ds(6 + n, 1)] = jnp.sum(d_low.astype(F32), axis=0, keepdims=True)
        add(sum_two, dot(d_low, up, NT))
        return 0

    lax.fori_loop(0, count, feed_back, 0)
    unit, scale = norm_stats(b.h_one[...])
    back, small_grad[2:3], small_grad[3:4] = norm_back(whole(sum_two, 0), unit, scale, small[2:3])
    grad_one = whole(b.dh_two, 8) + back
    b.h_one[...] = grad_one
    b.d_attn[...] = grad_one.astype(BF)
    spread_back = dot(b.d_attn[...], b.fulls[PROJ][...].reshape(D, D), NT).astype(BF)
    for n in range(count):
        b.do_send[n] = spread_back[:, n * WIDE : (n + 1) * WIDE]
    do_all = b.o_low
    pl.semaphore_wait(b.free, count - 1)
    given = links.start([
        remote(b.do_send.at[w.seq_at(k + 1)], do_all.at[w.seq, 0:rows], b.sem_do[0].at[k],
               b.sem_do[1].at[k], peer)
        for k, peer in enumerate(w.seq_peers())
    ])
    do_all[w.seq, 0:rows] = b.do_send[w.seq]
    b.sg_seq[w.seq] = small_grad[...]
    sg = links.start([
        remote(b.sg_seq.at[w.seq], b.sg_seq.at[w.seq], b.sem_sg_seq[0].at[k],
               b.sem_sg_seq[1].at[k], peer)
        for k, peer in enumerate(w.seq_peers())
    ])

    def tell_core():
        pl.semaphore_signal(b.ready, inc=1, device_id=w.partner("c"), device_id_type=MESH)
        pl.semaphore_wait(b.ready, 1)

    tell_core()
    scatter = Scatter(w, links, b.fulls, (b.got_one, b.got_two, b.got_three), *b.sem_scatter)

    def columns(ref):
        width = ref.shape[1] // count
        return lambda n: ref[:, pl.ds(pl.multiple_of(n * width, WIDE), width)]

    of_act, of_grouped, of_normed = columns(b.act), columns(b.grouped), columns(b.normed_two)
    scatter.begin(DOWN, lambda n: dot(of_act(n), b.d_branch[...], TN))
    scatter.begin(UP, lambda n: dot(of_normed(n), b.d_hidden[...], TN))
    scatter.step(DOWN, 0)
    arrive(row_edge)
    before = jnp.where(first, 0.0, b.edge[3].astype(F32))
    lay(h_two, 0, before[8:16])
    for k in range(3):
        for n in range(tiles):
            at = k * D + n * WIDE
            rows_of = h_two[pl.ds(n * block + 6 + k, pools, stride=3)]
            b.grouped[:, at : at + WIDE] = rows_of.astype(BF)
    short_out[...] = (dot(b.grouped[...], pool) + small[5:6]).astype(BF)
    tell_core()
    scatter.begin(POOL, lambda n: dot(of_grouped(n), g_low, TN))
    scatter.begin(PROJ, lambda n: dot(b.att[n], b.d_attn[...], TN))
    scatter.step(UP, 0)
    scatter.step(POOL, 0)
    scatter.step(PROJ, 0)

    def prepare(of_block):
        def body(n, _):
            r0 = pl.multiple_of(n * sub, 16)
            lane = lax.broadcasted_iota(jnp.int32, (sub, WIDE), 1)
            grad = do_all[of_block, pl.ds(r0, sub)].astype(F32)
            terms = grad * b.o_ref[of_block, pl.ds(r0, sub)]
            at = pl.ds(pl.multiple_of(of_block * block + r0, 16), sub)
            for h in range(HEADS):
                mine = in_head(lane, h)
                delta = jnp.sum(jnp.where(mine, terms, 0.0), axis=1, keepdims=True)
                base = jnp.where(mine, grad, 0.0)
                b.do_ext[h, at] = with_feats(base, lane, h, -delta).astype(BF)
            return 0

        lax.fori_loop(0, 3, body, 0)

    arrive(given)
    for n in range(count):
        prepare(n)
    dq, dk, dv = b.buf
    for ref in b.buf:
        ref[...] = jnp.zeros(ref.shape, F32)
    b.g_qkv[...] = jnp.zeros(b.g_qkv.shape, F32)
    b.dq_turned[...] = jnp.zeros(b.dq_turned.shape, F32)

    def pair(q_first, k_first, size, on_diagonal):
        at_q = pl.ds(pl.multiple_of(q_first, WIDE), size)
        at_k = pl.ds(pl.multiple_of(k_first, WIDE), size)
        probs = [dot(b.ext[1, h, at_k], b.ext[0, h, at_q], NT) for h in range(HEADS)]
        slopes = [dot(b.ext[2, h, at_k], b.do_ext[h, at_q], NT) for h in range(HEADS)]
        found = []
        for h in range(HEADS):
            p = jnp.exp2(probs[h])
            if on_diagonal:
                keys = lax.broadcasted_iota(jnp.int32, (size, size), 0)
                queries = lax.broadcasted_iota(jnp.int32, (size, size), 1)
                p = jnp.where(keys <= queries, p, 0.0)
            ds = (p * slopes[h]).astype(BF)
            found.append((dot(b.ext[1, h, at_k], ds, TN), dot(ds, b.ext[0, h, at_q]),
                          dot(p.astype(BF), b.do_ext[h, at_q])))
        lane = lax.broadcasted_iota(jnp.int32, (size, WIDE), 1)
        for ref, zero, one in zip((dk, dv), *[f[1:] for f in found]):
            ref[at_k] += jnp.where(lane < HEAD_DIM, zero, one)
        row = lax.broadcasted_iota(jnp.int32, (WIDE, size), 0)
        b.dq_turned[:, at_q] += jnp.where(row < HEAD_DIM, found[0][0], found[1][0])

    backs = (HEAD_DIM ** -0.5, 1.0 / LOG2E, 1.0)

    def dn_copy(turn_of):
        n = turn_of // 2
        return remote(b.tok_all.at[n], b.tok_all.at[2 + n], b.sem_dn[0].at[n], b.sem_dn[1].at[n],
                      w.partner("c"))

    def complete(turn_of, of_block):
        span = pl.ds(pl.multiple_of(of_block * block, WIDE), block)
        dq[span] = b.dq_turned[:, span].T

        def body(n, _):
            r0 = pl.multiple_of(n * sub, 16)
            cosine, sine = turning(of_block, r0)
            at = pl.ds(pl.multiple_of(of_block * block + r0, 16), sub)
            for m, ref in enumerate(b.buf):
                value = ref[at] * backs[m]
                if m < 2:
                    value = value * cosine - swap_halves(value) * sine
                b.stacked[pl.ds(r0, sub), m * WIDE : (m + 1) * WIDE] = value.astype(BF)
            return 0

        lax.fori_loop(0, 3, body, 0)
        weight = jnp.concatenate([qkv_weight(n) for n in range(3)], axis=1)
        b.g_qkv[...] += dot(b.normed[of_block], b.stacked[...], TN)
        back = dot(b.stacked[...], weight, NT)
        keeps = lax.rem(of_block, 2) == w.c

        @pl.when(keeps)
        def _():
            lay(b.dh_two, 0, back)

        @pl.when(jnp.logical_not(keeps))
        def _():
            b.tok_all[turn_of // 2] = back.astype(BF)
            dn_copy(turn_of).start()

    def summed(turn_of):
        dn_copy(turn_of).wait_recv()
        return whole(b.dh_two, 0) + b.tok_all[2 + turn_of // 2].astype(F32)

    down_first = w.x == 0
    x_copy = []
    for turn_of in range(count):
        outer = jnp.where(down_first, count - 1 - turn_of, turn_of)
        pair(outer * block, outer * block, block, True)

        def inner(n, _, outer=outer, turn_of=turn_of):
            other = jnp.where(down_first, n, turn_of + 1 + n)
            pair(jnp.where(down_first, outer, other) * block,
                 jnp.where(down_first, other, outer) * block, block, False)
            return 0

        if turn_of < count - 1:
            lax.fori_loop(0, count - 1 - turn_of, inner, 0)
        complete(turn_of, outer)
        if turn_of == count // 2 - 1:
            b.d_attn[...] = summed(turn_of).astype(BF)
            x_copy = links.start([
                remote(b.d_attn, b.x_in, b.sem_x[0].at[0], b.sem_x[1].at[0], w.partner("x"))
            ])
        for a, index in SWEEP_STEPS[turn_of]:
            scatter.step(a, index)
        if turn_of == 2:
            arrive(sg)
            total = b.sg_seq[0]
            for n in range(1, count):
                total = total + b.sg_seq[n]
            b.sg_all[w.batch] = total
            sg = links.start([
                remote(b.sg_all.at[w.batch], b.sg_all.at[w.batch], b.sem_sg_all[0].at[k],
                       b.sem_sg_all[1].at[k], peer)
                for k, peer in enumerate(w.batch_peers())
            ])

    def gather_squares(squares, total):
        flat = jnp.sum((total * total).reshape(-1, 8, total.shape[-1]), axis=0)
        for n in range(flat.shape[1] // WIDE):
            squares = squares + flat[:, n * WIDE : (n + 1) * WIDE]
        return squares

    for n in range(batches):
        z_of, y_of = n // ny, n % ny
        rows_of = b.g_qkv[...].reshape(count, nz, ny, -1, 3 * WIDE)[:, z_of, y_of]
        b.gq_out[n] = rows_of.astype(BF)
    gq = links.start([
        remote(b.gq_out.at[w.batch_at(k + 1)], b.gq_in.at[w.batch], b.sem_gq[0].at[k],
               b.sem_gq[1].at[k], peer)
        for k, peer in enumerate(w.batch_peers())
    ])
    b.gq_in[w.batch] = b.gq_out[w.batch]

    grad_normed = summed(count - 1)
    arrive(x_copy)
    grad_normed = grad_normed + b.x_in[...].astype(F32)
    unit, scale = norm_stats(tokens[...].astype(F32))
    back, small_grad[0:1], small_grad[1:2] = norm_back(grad_normed, unit, scale, small[0:1])
    input_grad[...] = b.h_one[...] + back
    late = jnp.concatenate(
        [small_grad[r : r + 1, n * WIDE : (n + 1) * WIDE] for r in range(2) for n in range(tiles)],
        axis=0,
    )
    b.late_seq[w.seq] = late
    late_sum = links.start([
        remote(b.late_seq.at[w.seq], b.late_seq.at[w.seq], b.sem_late_seq[0].at[k],
               b.sem_late_seq[1].at[k], peer)
        for k, peer in enumerate(w.seq_peers())
    ])
    for a in (POOL, UP, PROJ):
        scatter.step(a, 2)
    arrive(gq)
    total = b.gq_in[0].astype(F32)
    for n in range(1, batches):
        total = total + b.gq_in[n].astype(F32)
    b.gq_seq[...] = total.astype(BF)
    squares = gather_squares(jnp.zeros((8, WIDE), F32), total)
    gq = links.start([
        remote(b.gq_seq.at[w.seq_at(k + 1)], b.gq_got.at[w.seq], b.sem_gq_seq[0].at[k],
               b.sem_gq_seq[1].at[k], peer)
        for k, peer in enumerate(w.seq_peers())
    ])
    b.gq_got[w.seq] = b.gq_seq[w.seq]
    arrive(late_sum)
    total = b.late_seq[0]
    for n in range(1, count):
        total = total + b.late_seq[n]
    b.late_all[w.batch] = total
    late_sum = links.start([
        remote(b.late_all.at[w.batch], b.late_all.at[w.batch], b.sem_late_all[0].at[k],
               b.sem_late_all[1].at[k], peer)
        for k, peer in enumerate(w.batch_peers())
    ])
    totals = (total_proj, total_up, total_down, total_pool)
    for a in (DOWN, UP, POOL, PROJ):
        total = scatter.last(a)
        totals[a][...] = total
        squares = gather_squares(squares, total)
    b.norm_seq[w.seq] = squares
    norm = links.start([
        remote(b.norm_seq.at[w.seq], b.norm_seq.at[w.seq], b.sem_norm_seq[0].at[k],
               b.sem_norm_seq[1].at[k], peer)
        for k, peer in enumerate(w.seq_peers())
    ])
    arrive(gq)
    for n in range(3):
        total = jnp.concatenate(
            [b.gq_got[m, :, n * WIDE : (n + 1) * WIDE].astype(F32) for m in range(count)], axis=1
        )
        total_qkv[n] = total
    arrive(sg)
    total = b.sg_all[0]
    for n in range(1, batches):
        total = total + b.sg_all[n]
    arrive(late_sum)
    late = b.late_all[0]
    for n in range(1, batches):
        late = late + b.late_all[n]
    small_grad[...] = total
    for r in range(2):
        small_grad[r : r + 1] = jnp.concatenate(
            [late[r * tiles + n : r * tiles + n + 1] for n in range(tiles)], axis=1
        )
    b.wide_row[0:1, 0:D] = small_grad[pl.ds(small_row, 1)]
    b.wide_row[0:1, D:] = small_grad[pl.ds(small_row + 1, 1)]
    moved = pltpu.roll(b.wide_row[...], 2 * D - small_lane, 1)
    total_small[...] = moved[0:1, 0:own_small]
    small_squares = gather_squares(jnp.zeros((8, WIDE), F32), small_grad[...])
    arrive(norm)
    squares = b.norm_seq[0]
    for n in range(1, count):
        squares = squares + b.norm_seq[n]
    b.norm_all[w.batch] = squares
    norm = links.start([
        remote(b.norm_all.at[w.batch], b.norm_all.at[w.batch], b.sem_norm_all[0].at[k],
               b.sem_norm_all[1].at[k], peer)
        for k, peer in enumerate(w.batch_peers())
    ])
    arrive(norm)
    squares = b.norm_all[0]
    for n in range(1, batches):
        squares = squares + b.norm_all[n]
    squares = squares + small_squares
    square = jnp.sum(jnp.sum(squares, axis=1, keepdims=True), axis=0, keepdims=True)
    norm_out[...] = jnp.broadcast_to(jnp.sqrt(square), norm_out.shape)
    for turn_of in (1, 3):
        dn_copy(turn_of).wait_send()
    links.finish()


def step_kernel(norm_in, grad_in, short_in, *refs):
    states = refs[: 4 * 6]
    outs = refs[4 * 6 :]
    grad_out, short_out, norm_out = outs[:3]
    grad_out[...] = grad_in[...]
    short_out[...] = short_in[...]
    grad_norm = norm_in[0:1, 0:1]
    norm_out[...] = grad_norm
    clip = clip_norm / jnp.maximum(grad_norm, clip_norm)
    for a in range(6):
        total, weight, one, two = states[4 * a : 4 * a + 4]
        limit = clip.reshape((1,) * len(total.shape))
        rate, decay = (rate_vector, 0.0) if a == 5 else (rate_matrix, decay_weight)
        results = adam_update(total[...], one[...], two[...], weight[...], limit, rate, decay)
        for ref, value in zip(outs[3 + 3 * a : 6 + 3 * a], results):
            ref[...] = value


def rotary_tables(rows, count):
    half = HEAD_DIM // 2
    frequency = np.exp(-math.log(10000.0) * np.arange(half) / half)
    lanes = np.tile(frequency, WIDE // half)
    sign = np.tile(np.repeat([-1.0, 1.0], half), WIDE // HEAD_DIM)
    inside = np.arange(rows)[:, None] * lanes
    starts = (np.arange(8) * (np.arange(8) < count) * rows)[:, None] * lanes
    pack = lambda angle: np.stack([np.cos(angle), np.sin(angle) * sign]).astype(np.float32)
    return pack(inside), pack(starts)


def fast_local(mesh):
    nx, nz, ny = grid_of(mesh)
    count = 2 * nx
    in_vmem = pl.BlockSpec(memory_space=pltpu.VMEM)

    def call(kernel, outs, scratch, args, **params):
        return pl.pallas_call(
            kernel,
            out_shape=[jax.ShapeDtypeStruct(s, t) for s, t in outs],
            in_specs=[in_vmem] * len(args),
            out_specs=[in_vmem] * len(outs),
            scratch_shapes=scratch,
            compiler_params=pltpu.CompilerParams(vmem_limit_bytes=VMEM_LIMIT, **params),
        )(*args)

    def body(tokens, doc_ids, out_grad,
             qkv_weight, qkv_first, qkv_second,
             proj_weight, proj_first, proj_second,
             up_weight, up_first, up_second,
             down_weight, down_first, down_second,
             pool_weight, pool_first, pool_second,
             small_weight, small_first, small_second):
        rows = tokens.shape[1]
        pools = out_grad.shape[1]
        ff = up_weight.shape[1]
        own = small_weight.shape[0]
        turn, offset = rotary_tables(rows, count)
        weights = (qkv_weight, proj_weight, up_weight, down_weight, pool_weight)
        shapes = [v.shape for v in weights]
        template = layer_buffers(nx, nz, ny, rows, ff, shapes[1:])
        scratch = jax.tree.leaves(list(template.values()))
        outs = [((pools, D), BF), ((rows, D), F32)] + [(s, F32) for s in shapes]
        outs += [((1, own), F32), ((8, WIDE), F32)]
        short, grad_in, *totals, norm = call(
            lambda *r: layer_kernel(nx, nz, ny, template, *r), outs, scratch,
            (tokens[0], doc_ids, out_grad[0], *weights, small_weight.reshape(1, own), turn, offset),
            collective_id=0, has_side_effects=True)
        weights = (*weights, small_weight)
        firsts = (qkv_first, proj_first, up_first, down_first, pool_first, small_first)
        seconds = (qkv_second, proj_second, up_second, down_second, pool_second, small_second)
        groups = [list(group) for group in zip(totals, weights, firsts, seconds)]
        groups[5] = [v.reshape(1, own) for v in groups[5]]
        outs = [((rows, D), F32), ((pools, D), BF), ((1, 1), F32)]
        outs += [(v[0].shape, F32) for v in groups for _ in range(3)]
        grad_out, short_out, norm_out, *states = call(
            step_kernel, outs, [],
            (norm, grad_in, short, *[v for group in groups for v in group]))
        states[15:] = [v.reshape(own) for v in states[15:]]
        return (short_out[None], grad_out[None], norm_out.reshape(()), *states)

    return body


def solution(mesh):
    in_specs = (
        P("batch", "seq", None),
        P("batch", None),
        P("batch", "seq", None),
        P(None, ("seq", "batch"), None),
        P(None, ("seq", "batch"), None),
        P(None, ("seq", "batch"), None),
        P(("seq", "batch"), None),
        P(("seq", "batch"), None),
        P(("seq", "batch"), None),
        P(("seq", "batch"), None),
        P(("seq", "batch"), None),
        P(("seq", "batch"), None),
        P(("seq", "batch"), None),
        P(("seq", "batch"), None),
        P(("seq", "batch"), None),
        P(("seq", "batch"), None),
        P(("seq", "batch"), None),
        P(("seq", "batch"), None),
        P(("seq", "batch")),
        P(("seq", "batch")),
        P(("seq", "batch")),
    )
    out_specs = (
        P("batch", "seq", None),
        P("batch", "seq", None),
        P(),
        P(None, ("seq", "batch"), None),
        P(None, ("seq", "batch"), None),
        P(None, ("seq", "batch"), None),
        P(("seq", "batch"), None),
        P(("seq", "batch"), None),
        P(("seq", "batch"), None),
        P(("seq", "batch"), None),
        P(("seq", "batch"), None),
        P(("seq", "batch"), None),
        P(("seq", "batch"), None),
        P(("seq", "batch"), None),
        P(("seq", "batch"), None),
        P(("seq", "batch"), None),
        P(("seq", "batch"), None),
        P(("seq", "batch"), None),
        P(("seq", "batch")),
        P(("seq", "batch")),
        P(("seq", "batch")),
    )
    body = fast_local(mesh) if fits(mesh) else local
    return jax.shard_map(body, mesh=mesh, in_specs=in_specs, out_specs=out_specs, check_vma=False)
```
